32 devices in a mesh: patch: 8 (over z, y), dp: 4 (over x, core).
Axes of the slice: x: 2, y: 2, z: 4, core: 2. Of those that a mesh axis runs over, the one named last changes fastest.
Arguments:
- grid: bfloat16 [8, 16384, 264], P('dp', 'patch'), may hold values from -6 to 6
- targets: float32 [8, 16384, 84], P('dp', 'patch'), may hold values from -6 to 6
- area: float32 [16384], P('patch'), may hold values from 0.1 to 1
- sigma_weight: float32 [8], P('dp'), may hold values from 0.5 to 2
- level_weight: float32 [84], replicated, may hold values from 0.2 to 2
- valid: int32 [8, 16384], P('dp', 'patch'), may hold values from 0 to 1
- enc_index: int32 [4096, 4], P('patch'), may hold values from 0 to 2047
- dec_index: int32 [16384, 3], P('patch'), may hold values from 0 to 511
- neighbours: int32 [4096, 16], P('patch'), may hold values from 0 to 575, as said below
- params: float32 [3325440], P(('patch', 'dp'))
- first_moment: float32 [3325440], P(('patch', 'dp'))
- second_moment: float32 [3325440], P(('patch', 'dp')), as said below
- average: float32 [3325440], P(('patch', 'dp'))
Outputs:
- loss_pair: float32 [2], replicated
- norms: float32 [2, 7], replicated
- new_params: float32 [3325440], P(('patch', 'dp'))
- new_first: float32 [3325440], P(('patch', 'dp'))
- new_second: float32 [3325440], P(('patch', 'dp'))
- new_average: float32 [3325440], P(('patch', 'dp'))
The draws below stay inside these ranges and needn't reach their ends.
Inputs may be any that keep to these rules, and one draw needn't show every extreme that they name: `neighbours`: entries below 32 name the lower adjacent patch's last 32 rows, entries of 544 or more the upper one's first 32 rows, the others the patch's own rows; every rim row of both sides is read by some node of every patch; the patches close into a loop. `second_moment`: second moments are positive.
All inputs are finite; a program needn't handle non-finite values.
Results may differ from the reference program's by a relative error of at most 0.0025.
The reference program's roundings to bfloat16 on the way count: a program that leaves them out, or rounds other values in their place, can miss the bound.
Values may be sent and summed in bfloat16 or wider, within the bound.
No kernel may reach another device: no remote copies, remote signals or barrier semaphores. Data moves between devices by JAX's collectives and lax.ppermute only.
A program may use at most 320 MiB of HBM per device.

```python
import math
import jax
import jax.numpy as jnp
from jax import lax

D = 512
HEADS = 4
HEAD_DIM = 128
FF = 2048
C_OUT = 84
C_IN = 264
NB = 16
K_ENC = 4
K_DEC = 3
STEP = 10
NODES_DEV = 512
HALO = 32
PIX_DEV = 2048
NODES = 4096
PIXELS = 16384
SAMPLES = 8
NPARAM = 3325440


def layout_sizes():
    return [(C_IN * D, C_IN), (3 * D * D, D), (D * D, D // 16), (D * FF, D), (FF * D, FF), (D * C_OUT, D), (3 * D, 0)]


def per_entry(matrix_value, fan_power, gain_value, padding_value):
    pieces = []
    used = 0
    for length, fan_in in layout_sizes():
        if fan_in > 0:
            value = matrix_value * fan_in ** fan_power
        else:
            value = gain_value
        pieces.append(jnp.full((length,), value, jnp.float32))
        used += length
    pieces.append(jnp.full((NPARAM - used,), padding_value, jnp.float32))
    return jnp.concatenate(pieces)


def grad_size():
    return 2.0 / math.sqrt(SAMPLES * PIXELS)


def weight_law(key):
    unit = jax.random.normal(key, (NPARAM,), jnp.float32)
    return unit * per_entry(1.0, -0.5, 0.1, 0.02) + per_entry(0.0, 0.0, 1.0, 0.0)


def draw_params(key, part):
    key = jax.random.fold_in(key, 1)
    return weight_law(key)


def draw_average(key, part):
    key = jax.random.fold_in(key, 4)
    return weight_law(key)


def draw_first_moment(key, part):
    key = jax.random.fold_in(key, 2)
    unit = jax.random.normal(key, (NPARAM,), jnp.float32)
    size = grad_size()
    return unit * 0.111 * per_entry(size, 0.0, 4.0 * size, size)


def draw_second_moment(key, part):
    key = jax.random.fold_in(key, 3)
    factor = jnp.exp(jax.random.uniform(key, (NPARAM,), jnp.float32, 0.0, math.log(4.0)))
    size = grad_size()
    scales = per_entry(size, 0.0, 4.0 * size, size)
    return factor * 0.001001 * scales * scales


def draw_valid(key, part):
    key = jax.random.fold_in(key, 5)
    rolled = jax.random.randint(key, (SAMPLES, PIXELS), 0, 100)
    pixel_pos = jax.lax.broadcasted_iota(jnp.int32, (SAMPLES, PIXELS), 1)
    sample_pos = jax.lax.broadcasted_iota(jnp.int32, (SAMPLES, PIXELS), 0)
    limit = 25 + 50 * pixel_pos // PIXELS + 20 * sample_pos // SAMPLES
    return (rolled < limit).astype(jnp.int32)


def draw_neighbours(key, part):
    key = jax.random.fold_in(key, 6)
    pick_key, own_key, rim_key = jax.random.split(key, 3)
    pick = jax.random.randint(pick_key, (NODES, NB), 0, 10)
    own = jax.random.randint(own_key, (NODES, NB), HALO, HALO + NODES_DEV)
    rim_raw = jax.random.randint(rim_key, (NODES, NB), 0, 2 * HALO)
    rim = jnp.where(rim_raw < HALO, rim_raw, rim_raw + NODES_DEV)
    table = jnp.where(pick == 0, rim, own)
    local_row = jax.lax.broadcasted_iota(jnp.int32, (NODES, NB), 0) % NODES_DEV
    column = jax.lax.broadcasted_iota(jnp.int32, (NODES, NB), 1)
    forced = jnp.where(local_row < HALO, local_row, local_row + NODES_DEV)
    return jnp.where((column == NB - 1) & (local_row < 2 * HALO), forced, table)


def touch_ends(array, key, low, high):
    spot = [jax.random.randint(jax.random.fold_in(key, axis), (), 0, length) for axis, length in enumerate(array.shape)]
    longest = array.shape.index(max(array.shape))
    next_to = spot[:longest] + [(spot[longest] + 1) % array.shape[longest]] + spot[longest + 1:]
    return array.at[tuple(spot)].set(low).at[tuple(next_to)].set(high)


def shard_levels(key, extent, cuts, least, top_value):
    gain, own = 1.0, jax.random.fold_in(key, 6)
    for dim, shards_of in cuts:
        steps = jnp.exp(jax.random.uniform(jax.random.fold_in(own, dim), (shards_of,), jnp.float32, least / len(cuts), top_value / len(cuts)))
        gain = gain * jnp.repeat(steps, extent[dim] // shards_of).reshape([-1 if axis == dim else 1 for axis in range(len(extent))])
    return gain


def normal_values(key, shape, width, most, cuts=(), kind=jnp.bfloat16):
    drawn = jax.random.normal(key, shape, jnp.float32) * width
    if len(cuts) > 0:
        drawn = shard_levels(key, shape, cuts, -0.22, 0.18) * drawn
    return jnp.clip(drawn, min=-most, max=most).astype(kind)


def setup_inputs(seed: int = 0) -> dict:
    arg_keys = jax.random.split(jax.random.key(seed), 14)
    return {
        "grid": normal_values(arg_keys[0], (SAMPLES, PIXELS, C_IN), 1.0, 6.0, ((0, 4), (1, 8))),
        "targets": normal_values(arg_keys[1], (SAMPLES, PIXELS, C_OUT), 1.0, 6.0, ((0, 4), (1, 8)), jnp.float32),
        "area": jnp.clip(jnp.exp(math.log(1.0) - 2.3025851 * jax.random.uniform(arg_keys[2], (PIXELS,), jnp.float32) ** shard_levels(arg_keys[2], (PIXELS,), ((0, 8),), -0.2, 0.2)), 0.1, 1.0),
        "sigma_weight": jnp.clip(jnp.exp(math.log(2.0) - 1.3862944 * jax.random.uniform(arg_keys[3], (SAMPLES,), jnp.float32) ** shard_levels(arg_keys[3], (SAMPLES,), ((0, 4),), -0.2, 0.2)), 0.5, 2.0),
        "level_weight": jnp.clip(jnp.exp(jax.random.uniform(arg_keys[4], (C_OUT,), jnp.float32, math.log(0.2), math.log(2.0))), 0.2, 2.0),
        "valid": draw_valid(jax.random.fold_in(arg_keys[13], 71), 0),
        "enc_index": touch_ends(jax.random.randint(arg_keys[6], (NODES, K_ENC), 0, PIX_DEV), jax.random.fold_in(arg_keys[6], 1), 0, PIX_DEV - 1).astype(jnp.int32),
        "dec_index": touch_ends(jax.random.randint(arg_keys[7], (PIXELS, K_DEC), 0, NODES_DEV), jax.random.fold_in(arg_keys[7], 1), 0, NODES_DEV - 1).astype(jnp.int32),
        "neighbours": draw_neighbours(jax.random.fold_in(arg_keys[13], 71), 0),
        "params": draw_params(jax.random.fold_in(arg_keys[13], 71), 0),
        "first_moment": draw_first_moment(jax.random.fold_in(arg_keys[13], 71), 0),
        "second_moment": draw_second_moment(jax.random.fold_in(arg_keys[13], 71), 0),
        "average": draw_average(jax.random.fold_in(arg_keys[13], 71), 0),
    }


@jax.custom_vjp
def low(v):
    return lax.optimization_barrier(v.astype(jnp.bfloat16)).astype(jnp.float32)

@jax.custom_vjp
def low_back(v):
    return v

def low_keep(v):
    return (low(v), None)

def low_pass(kept, grad):
    return (grad,)

def back_keep(v):
    return (v, None)

def back_low(kept, grad):
    return (low(grad),)
low.defvjp(low_keep, low_pass)
low_back.defvjp(back_keep, back_low)
EPS_NORM = 1e-05
BETA_ONE = 0.9
BETA_TWO = 0.999
LAMB_EPS = 1e-06
DECAY = 0.01
RATE = 0.2
EMA_KEEP = 0.8
HIGH = lax.Precision.HIGHEST

def matrix_shapes():
    return [(C_IN, D), (D, 3 * D), (D, D), (D, FF), (FF, D), (D, C_OUT), (3, D)]

def segment_bounds():
    bounds = []
    offset = 0
    for row_count, col_count in matrix_shapes():
        bounds.append((offset, offset + row_count * col_count))
        offset += row_count * col_count
    return bounds

def unpack(flat):
    return [flat[lower:upper].reshape(shape) for (lower, upper), shape in zip(segment_bounds(), matrix_shapes())]

def matmul(left, right):
    return jnp.dot(left, right, precision=HIGH, preferred_element_type=jnp.float32)

def layer_norm(values, gain_row):
    centred = values - lax.optimization_barrier(jnp.mean(values, -1, keepdims=True))
    return centred * lax.rsqrt(lax.optimization_barrier(jnp.mean(centred * centred, -1, keepdims=True)) + EPS_NORM) * gain_row

def attend(query, pairs, index_global):
    block = min(512, NODES_DEV)
    count_blocks = NODES // block
    query_blocks = query.reshape(count_blocks, block, HEADS, HEAD_DIM)
    index_blocks = index_global.reshape(count_blocks, block, NB)

    def one_block(inputs):
        query_block, index_block = inputs
        gathered = pairs[index_block]
        keys = gathered[..., :D].reshape(block, NB, HEADS, HEAD_DIM)
        values = gathered[..., D:].reshape(block, NB, HEADS, HEAD_DIM)
        scores = jnp.einsum('bhd,bjhd->bhj', query_block, keys, precision=HIGH) * HEAD_DIM ** (-0.5)
        probs = low(jax.nn.softmax(scores, axis=-1))
        return jnp.einsum('bhj,bjhd->bhd', probs, values, precision=HIGH).reshape(block, D)
    return lax.map(jax.checkpoint(one_block), (query_blocks, index_blocks)).reshape(NODES, D)

def sample_loss(flat_low, pixels_in, target, weighting, level_weight, enc_global, dec_global, nbr_global):
    w_enc, w_qkv, w_out, w_up, w_down, w_dec, gains = unpack(flat_low)
    pre_act = low_back(matmul(pixels_in, w_enc))
    start_h = lax.optimization_barrier(jnp.mean(jax.nn.silu(pre_act)[enc_global], axis=1))
    in_one = low(layer_norm(start_h, gains[0]))
    qkv = low_back(low(matmul(in_one, w_qkv)))
    attended = low(attend(qkv[:, :D], qkv[:, D:], nbr_global))
    mid_h = start_h + low_back(matmul(attended, w_out))
    in_two = low(layer_norm(mid_h, gains[1]))
    upper = low_back(matmul(in_two, w_up))
    end_h = mid_h + low_back(matmul(low(jax.nn.silu(upper)), w_down))
    in_three = low(layer_norm(end_h, gains[2]))
    node_pred = low_back(matmul(in_three, w_dec))
    pixel_pred = lax.optimization_barrier(jnp.mean(node_pred[dec_global], axis=1))
    misfit = pixel_pred - target
    return jnp.sum(weighting[:, None] * level_weight[None, :] * misfit * misfit)

def reference(grid, targets, area, sigma_weight, level_weight, valid, enc_index, dec_index, neighbours, params, first_moment, second_moment, average):
    node_rows = jnp.arange(NODES, dtype=jnp.int32)
    patch_of = node_rows // NODES_DEV
    nbr_global = (patch_of[:, None] * NODES_DEV + neighbours - HALO) % NODES
    enc_global = patch_of[:, None] * PIX_DEV + enc_index
    pixel_patch = jnp.arange(PIXELS, dtype=jnp.int32) // PIX_DEV
    dec_global = pixel_patch[:, None] * NODES_DEV + dec_index
    weighting = valid.astype(jnp.float32) * area[None, :] * sigma_weight[:, None]
    count = jnp.sum(valid.astype(jnp.float32))
    grid_f = grid.astype(jnp.float32)

    def objective(flat):
        flat_low = low(flat)

        def one_sample(total, inputs):
            pixels_in, target, weigh = inputs
            term = jax.checkpoint(sample_loss)(flat_low, pixels_in, target, weigh, level_weight, enc_global, dec_global, nbr_global)
            return (total + term, None)
        total, unused = lax.scan(one_sample, jnp.zeros((), jnp.float32), (grid_f, targets, weighting))
        return total
    loss_sum, pullback = jax.vjp(objective, params)
    grads = pullback(jnp.ones((), jnp.float32) / count)[0]
    positions = jnp.arange(params.shape[0], dtype=jnp.int32)
    member = jnp.stack([((positions >= lower) & (positions < upper)).astype(jnp.float32) for lower, upper in segment_bounds()])
    new_first = BETA_ONE * first_moment + (1.0 - BETA_ONE) * grads
    new_second = BETA_TWO * second_moment + (1.0 - BETA_TWO) * grads * grads
    update = new_first / (1.0 - BETA_ONE ** STEP) / (jnp.sqrt(new_second / (1.0 - BETA_TWO ** STEP)) + LAMB_EPS) + DECAY * params
    squares = jnp.stack([lax.optimization_barrier(jnp.sum(member * (params * params)[None, :], axis=1)), lax.optimization_barrier(jnp.sum(member * (update * update)[None, :], axis=1))])
    norms = jnp.sqrt(squares)
    ratio = norms[0] / norms[1]
    step_ratio = lax.optimization_barrier(jnp.sum(member * ratio[:, None], axis=0))
    new_params = params - RATE * step_ratio * update
    new_average = EMA_KEEP * average + (1.0 - EMA_KEEP) * new_params
    return (jnp.stack([loss_sum, count]), norms, new_params, new_first, new_second, new_average)
```

```python
import functools
import math

import jax
import jax.numpy as jnp
from jax import lax
from jax.experimental import pallas as pl
from jax.experimental.pallas import tpu as pltpu
from jax.sharding import PartitionSpec as P

D = 512
HEADS = 4
HEAD_DIM = 128
FF = 2048
C_OUT = 84
C_IN = 264
STEP = 10
EPS_NORM = 1e-05
BETA_ONE = 0.9
BETA_TWO = 0.999
LAMB_EPS = 1e-06
DECAY = 0.01
RATE = 0.2
EMA_KEEP = 0.8
BF = jnp.bfloat16
F32 = jnp.float32
SCALE = HEAD_DIM ** (-0.5)
LOG2E = 1.4426950408889634
ABSENT = -1e30
CP = 96
AXES = ("patch", "dp")

LEAD = 8
ROW_ENC = LEAD
ROW_QKV = ROW_ENC + C_IN
ROW_OUT = ROW_QKV + 3 * D
ROW_UP = ROW_OUT + D
ROW_DOWN = ROW_UP + 4 * D
ROW_DEC = ROW_DOWN + FF
ROW_GAIN = ROW_DEC + C_OUT
ROW_END = ROW_GAIN + 3
ROWS_ALL = -(-ROW_END // 16) * 16


def matrix_shapes():
    return [(C_IN, D), (D, 3 * D), (D, D), (D, FF), (FF, D), (D, C_OUT), (3, D)]


def segment_bounds():
    bounds = []
    offset = 0
    for row_count, col_count in matrix_shapes():
        bounds.append((offset, offset + row_count * col_count))
        offset += row_count * col_count
    return bounds


NPARAM_USED = segment_bounds()[-1][1]


def dot(a, b):
    return lax.dot_general(a, b, (((1,), (0,)), ((), ())), preferred_element_type=F32)


def dot_nt(a, b):
    return lax.dot_general(a, b, (((1,), (1,)), ((), ())), preferred_element_type=F32)


def dot_tn(a, b):
    return lax.dot_general(a, b, (((0,), (0,)), ((), ())), preferred_element_type=F32)


def split(x):
    high = x.astype(BF)
    return high, (x - high.astype(F32)).astype(BF)


def sigmoid(x):
    return 1.0 / (1.0 + jnp.exp(-x))


def slope(x):
    s = sigmoid(x)
    return s * (1.0 + x * (1.0 - s))


def norm(x):
    c = x - jnp.mean(x, -1, keepdims=True)
    r = lax.rsqrt(jnp.mean(c * c, -1, keepdims=True) + EPS_NORM)
    return c * r, r


def norm_back(grad, gain, hat, r):
    g = grad * gain
    return r * (
        g
        - jnp.mean(g, -1, keepdims=True)
        - hat * jnp.mean(g * hat, -1, keepdims=True)
    )


def put_flat(ref, value, first, period):
    for lane in range(D // 128):
        ref[pl.ds(first + lane, value.shape[0], stride=period), :] = value[
            :, lane * 128 : lane * 128 + 128
        ]


def kernel_call(body, out_shape, scratch=(), flops=0, nbytes=0):
    return pl.pallas_call(
        body,
        out_shape=out_shape,
        scratch_shapes=list(scratch),
        compiler_params=pltpu.CompilerParams(vmem_limit_bytes=58 << 20),
        cost_estimate=pl.CostEstimate(flops=flops, bytes_accessed=nbytes, transcendentals=0),
    )


def shape(dims, dtype=F32):
    return jax.ShapeDtypeStruct(tuple(dims), dtype)


def prep_body(enc, enc_t, dec_t, nbr_t, targets, enc_m, enc_mt, dec_mt, log_c, targets_t):
    nodes, pixels = enc_m.shape
    ext = log_c.shape[0]

    def count_rows(index_t, base, rows, cols):
        ids = lax.broadcasted_iota(jnp.int32, (rows, cols), 0) + base
        total = jnp.zeros((rows, cols), F32)
        for k in range(index_t.shape[0]):
            total = total + jnp.where(index_t[k : k + 1, :] == ids, 1.0, 0.0)
        return total

    @pl.loop(0, nodes // 32)
    def _(i):
        rows = pl.ds(pl.multiple_of(i * 32, 32), 32)
        index = enc[rows, :]
        ids = lax.broadcasted_iota(jnp.int32, (32, pixels), 1)
        total = jnp.zeros((32, pixels), F32)
        for k in range(index.shape[1]):
            total = total + jnp.where(index[:, k : k + 1] == ids, 1.0, 0.0)
        enc_m[rows, :] = total.astype(BF)
        dec_mt[rows, :] = count_rows(dec_t, i * 32, 32, pixels).astype(BF)

    @pl.loop(0, pixels // 64)
    def _(i):
        rows = pl.ds(pl.multiple_of(i * 64, 64), 64)
        enc_mt[rows, :] = count_rows(enc_t, i * 64, 64, nodes).astype(BF)

    @pl.loop(0, ext // 64)
    def _(i):
        rows = pl.ds(pl.multiple_of(i * 64, 64), 64)
        total = count_rows(nbr_t, i * 64, 64, nodes)
        log_c[rows, :] = jnp.where(total > 0.0, jnp.log2(jnp.maximum(total, 1.0)), ABSENT)

    targets_t[...] = jnp.zeros(targets_t.shape, F32)
    for s in range(targets.shape[0]):

        @pl.loop(0, pixels // 256)
        def _(i):
            part = pl.ds(pl.multiple_of(i * 256, 256), 256)
            targets_t[s, 0:C_OUT, part] = targets[s, part, :].T


def prep(enc_index, dec_index, neighbours, targets):
    nodes, pixels = neighbours.shape[0], dec_index.shape[0]
    ext = nodes + 2 * (nodes // 16)
    return kernel_call(
        prep_body,
        [
            shape((nodes, pixels), BF),
            shape((pixels, nodes), BF),
            shape((nodes, pixels), BF),
            shape((ext, nodes)),
            shape((targets.shape[0], CP, pixels)),
        ],
        nbytes=12 << 20,
        flops=1 << 30,
    )(enc_index, enc_index.T, dec_index.T, neighbours.T, targets)


def tile_sources(starts, counts):
    sources = []
    for tile in range(ROWS_ALL // 16):
        row = tile * 16
        sources.append(
            [(d, row - s) for d, (s, c) in enumerate(zip(starts, counts)) if s <= row < s + c]
        )
    return sources


def assemble(read, window_rows, sources, first_row, rows, put):
    tile, last = first_row // 16, (first_row + rows) // 16
    while tile < last:
        source = sources[tile]
        if len(source) == 1:
            count = 1
            while (
                tile + count < last
                and len(sources[tile + count]) == 1
                and sources[tile + count][0][0] == source[0][0]
                and count < 8
            ):
                count += 1
            d, off = source[0]
            value = read(d, off, 16 * count)
        else:
            count = 1
            value = None
            for d, off in source:
                part = read(d, off, 16).astype(F32)
                if off + 16 == window_rows:
                    part = jnp.where(
                        lax.broadcasted_iota(jnp.int32, part.shape, 0) < 15, part, 0.0
                    )
                value = part if value is None else value + part
            value = value.astype(BF)
        put(tile * 16 - first_row, value)
        tile += count


def unpack_body(plan, count, sources, *refs):
    me, pieces, refs = refs[0], refs[1 : count + 1], refs[count + 1 :]
    w_enc, w_qkv, w_out, w_up, w_down, tail, total, windows, stage, sems = refs
    copies = []
    for k, (piece, index, slot, first, rows) in enumerate(plan):
        source = pieces[piece] if index is None else pieces[piece].at[index]
        copy = pltpu.make_async_copy(
            source, windows.at[slot, pl.ds(first, rows), :], sems.at[k]
        )
        copy.start()
        copies.append(copy)
    for copy in copies:
        copy.wait()
    here = me[0]
    window_rows = windows.shape[1]

    def direct(ref):
        def put(off, value):
            ref[off : off + value.shape[0], :] = value

        return put

    def staged(off, value):
        wide = value.astype(F32)
        for lane in range(D // 128):
            stage[lane, off : off + value.shape[0], :] = wide[:, lane * 128 : lane * 128 + 128]

    def read(d, off, rows):
        return windows[jnp.bitwise_xor(here, d), off : off + rows, :]

    assemble(read, window_rows, sources, 0, ROW_QKV, staged)
    for lane in range(D // 128):
        w_enc[:, lane * 128 : lane * 128 + 128] = stage[lane, LEAD:ROW_QKV, :].astype(BF)
    assemble(read, window_rows, sources, ROW_QKV, 3 * D, staged)
    for lane in range(D // 128):
        for c in range(3):
            w_qkv[:, c * D + lane * 128 : c * D + lane * 128 + 128] = stage[
                lane, pl.ds(c, D, stride=3), :
            ].astype(BF)
    assemble(read, window_rows, sources, ROW_UP, 4 * D, staged)
    for lane in range(D // 128):
        for c in range(4):
            w_up[:, c * D + lane * 128 : c * D + lane * 128 + 128] = stage[
                lane, pl.ds(c, D, stride=4), :
            ].astype(BF)
    assemble(read, window_rows, sources, ROW_OUT, D, direct(w_out))
    assemble(read, window_rows, sources, ROW_DOWN, FF, direct(w_down))
    assemble(read, window_rows, sources, ROW_DEC, ROWS_ALL - ROW_DEC, direct(tail))
    rows = windows.shape[1]
    counts = jnp.sum(windows[:, rows - 16 :, 0:128].astype(F32), axis=0)[15:16, :]
    lanes = lax.broadcasted_iota(jnp.int32, (1, 128), 1)
    parts = jnp.where(lanes == 0, 128.0, jnp.where(lanes == 1, 1.0, 0.0)) * counts
    total[...] = jnp.sum(parts, axis=1, keepdims=True) + jnp.zeros((8, 128), F32)


def unpack(me, pieces, plan, devices, rows, starts):
    sources = tile_sources(starts, [rows] * devices)
    return pl.pallas_call(
        functools.partial(unpack_body, plan, len(pieces), sources),
        out_shape=[
            shape((C_IN, D), BF),
            shape((D, 3 * D), BF),
            shape((D, D), BF),
            shape((D, FF), BF),
            shape((FF, D), BF),
            shape((ROWS_ALL - ROW_DEC, D), BF),
            shape((8, 128)),
        ],
        in_specs=[pl.BlockSpec(memory_space=pltpu.SMEM)]
        + [pl.BlockSpec(memory_space=pl.ANY)] * len(pieces),
        scratch_shapes=[
            pltpu.VMEM((devices, rows, D), BF),
            pltpu.VMEM((D // 128, 4 * D, 128), F32),
            pltpu.SemaphoreType.DMA((len(plan),)),
        ],
        compiler_params=pltpu.CompilerParams(vmem_limit_bytes=58 << 20),
        cost_estimate=pl.CostEstimate(flops=0, bytes_accessed=14 << 20, transcendentals=0),
    )(me, *pieces)


def permute(x, mask):
    count = lax.axis_size(AXES)
    return lax.ppermute(x, AXES, [(d, d ^ mask) for d in range(count)])


def gather_windows(window, mesh_axes, meanwhile):
    rows = window.shape[0]
    if mesh_axes != (8, 4):
        devices = lax.axis_size(AXES)
        everything = lax.all_gather(window, AXES, axis=0, tiled=False)
        me = lax.axis_index(AXES)
        order = jnp.bitwise_xor(jnp.arange(devices), me)
        return [everything[order]], [(0, d, d, 0, rows) for d in range(devices)], meanwhile
    half = rows // 2
    pieces, plan = [], []

    def add(piece, slots, first=0):
        for value, flip in ((piece, 0), (permute(piece, 1), 1)):
            for i, slot in enumerate(slots):
                index = None if piece.ndim == 2 else i
                plan.append((len(pieces), index, slot ^ flip, first, piece.shape[-2]))
            pieces.append(value)

    def in_plane(value, slots):
        by_x, by_y = permute(value, 2), permute(value, 4)
        add(value, slots)
        add(by_x, [s ^ 2 for s in slots])
        add(by_y, [s ^ 4 for s in slots])
        add(permute(by_y[..., :half, :], 2), [s ^ 6 for s in slots])
        add(permute(by_x[..., half:, :], 4), [s ^ 6 for s in slots], half)

    others = jnp.stack([permute(window, m) for m in (8, 16, 24)])
    in_plane(window, [0])
    others, meanwhile = lax.optimization_barrier((others, meanwhile))
    in_plane(others, [8, 16, 24])
    return pieces, plan, meanwhile


def sum_windows(keep, send, mesh_axes):
    rows = keep.shape[1]
    if mesh_axes != (8, 4):
        devices = lax.axis_size(AXES)
        me = lax.axis_index(AXES)
        both = jnp.stack([keep, send], axis=1).reshape(devices, rows, 128)
        order = jnp.bitwise_xor(jnp.arange(devices), me)
        return lax.psum_scatter(both[order], AXES, scatter_dimension=0, tiled=False)
    half = rows // 2
    total = (keep + permute(send, 1)).reshape(4, 2, 2, rows, 128)
    part_a, part_b = total[:, :, :, :half], total[:, :, :, half:]
    got_a = permute(part_a[:, :, 1].astype(BF), 2)
    got_b = permute(part_b[:, 1].astype(BF), 4)
    part_a = part_a[:, :, 0] + got_a.astype(F32)
    part_b = part_b[:, 0] + got_b.astype(F32)
    got_a = permute(part_a[:, 1].astype(BF), 4)
    got_b = permute(part_b[:, 1].astype(BF), 2)
    part_a = part_a[:, 0] + got_a.astype(F32)
    part_b = part_b[:, 0] + got_b.astype(F32)
    total = jnp.concatenate([part_a, part_b], axis=1)
    result = total[0]
    for k in (1, 2, 3):
        result = result + permute(total[k].astype(BF), 8 * k).astype(F32)
    return result


def sum_everywhere(x, mesh_axes):
    if mesh_axes != (8, 4):
        return lax.psum(x, AXES)
    for k in range(5):
        x = x + permute(x, 1 << k)
    return x


def encode_body(grid, w_enc, enc_m, w_qkv, gains, h0, qkv, high, low):
    samples, pixels = grid.shape[0], grid.shape[1]
    nodes = h0.shape[1]
    for s in range(samples):

        @pl.loop(0, pixels // 256)
        def _(i):
            rows = pl.ds(pl.multiple_of(i * 256, 256), 256)
            pre = dot(grid[s, rows, :], w_enc[...])
            value = pre * sigmoid(pre)
            high[rows, :], low[rows, :] = split(value)

        @pl.loop(0, nodes // 256)
        def _(i):
            rows = pl.ds(pl.multiple_of(i * 256, 256), 256)
            counts = enc_m[rows, :]
            start = (dot(counts, high[...]) + dot(counts, low[...])) * 0.25
            h0[s, rows, :] = start
            hat, _ = norm(start)
            n1 = (hat * gains[0:1, :]).astype(BF)
            qkv[s, rows, :] = dot(n1, w_qkv[...]).astype(BF)


def encode(grid, w_enc, enc_m, w_qkv, gains):
    samples, pixels = grid.shape[:2]
    nodes = enc_m.shape[0]
    return kernel_call(
        encode_body,
        [shape((samples, nodes, D)), shape((samples, nodes, 3 * D), BF)],
        [pltpu.VMEM((pixels, D), BF), pltpu.VMEM((pixels, D), BF)],
        nbytes=12 << 20,
        flops=8 << 30,
    )(grid, w_enc, enc_m, w_qkv, gains)


def gather_pairs(qkv, before, after, pairs, s):
    halo, nodes = before.shape[1], qkv.shape[1]
    pairs[0:halo, :] = before[s]
    pairs[halo : halo + nodes, :] = qkv[s, :, D:]
    pairs[halo + nodes :, :] = after[s]


def attention_weights(keys, query, log_c):
    x = dot_nt(keys, query) * (SCALE * LOG2E) + log_c[...]
    e = jnp.exp2(x - jnp.max(x, 0, keepdims=True))
    return e * (1.0 / jnp.sum(e, 0, keepdims=True))


def attend_body(qkv, before, after, log_c, out, pairs):
    for s in range(qkv.shape[0]):
        gather_pairs(qkv, before, after, pairs, s)
        for h in range(HEADS):
            lanes = slice(h * HEAD_DIM, (h + 1) * HEAD_DIM)
            keys = pairs[:, lanes]
            values = pairs[:, D + h * HEAD_DIM : D + (h + 1) * HEAD_DIM]
            probs = attention_weights(keys, qkv[s, :, lanes], log_c)
            out_t = dot_tn(values, probs.astype(BF))
            out[s, :, lanes] = out_t.T.astype(BF)


def attend(qkv, before, after, log_c):
    samples, nodes = qkv.shape[:2]
    return kernel_call(
        attend_body,
        shape((samples, nodes, D), BF),
        [pltpu.VMEM((log_c.shape[0], 2 * D), BF)],
        nbytes=8 << 20,
        flops=2 << 30,
    )(qkv, before, after, log_c)


def window_blocks(begins, ends, starts, first, rows):
    blocks = []
    for d, (lower, upper, start) in enumerate(zip(begins, ends, starts)):
        low = max(lower, first)
        high = min(upper, first + rows)
        if low < high:
            blocks.append((d, low - start, low - first, high - low))
    return blocks


def window_blocks_of(devices, shard, starts, arrays):
    begins = [(LEAD * D + d * shard) // 1024 * 8 for d in range(devices)]
    ends = [-(-(LEAD * D + (d + 1) * shard) // 1024) * 8 for d in range(devices)]
    plans, k = {}, 0
    for name, first, size in arrays:
        plans[name] = []
        for block in window_blocks(begins, ends, [4 * x for x in starts], 4 * first, size):
            plans[name].append((k,) + block)
            k += 1
    return plans, k


def window_copies(here, blocks, source, keep, send, sems, action):
    for k, d, to, at, rows in blocks:
        slot = jnp.bitwise_xor(here, d)
        for target, side in ((keep, 0), (send, 1)):

            @pl.when(jnp.bitwise_and(slot, 1) == side)
            def _():
                copy = pltpu.make_async_copy(
                    source.at[pl.ds(at, rows), :],
                    target.at[lax.shift_right_logical(slot, 1), pl.ds(to, rows), :],
                    sems.at[k],
                )
                getattr(copy, action)()


def mlp_body(
    plans,
    me, h0, attended, w_out, w_up, w_down, w_dec, gains, dec_mt, targets_t, weight, levels, scale,
    dh1, d_dec, d_gains, loss, keep, send,
    h1, n2, upper, act, h2, n3, pred, d_pred, dm, du, d_y, total_out, d_out, d_up, d_down, sems,
):
    samples, nodes, _ = h0.shape
    here = me[0]
    pixels = dec_mt.shape[1]
    tile = 256
    tiles = nodes // tile
    for s in range(samples):

        @pl.loop(0, tiles)
        def _(i):
            rows = pl.ds(pl.multiple_of(i * tile, tile), tile)
            flat = pl.ds(pl.multiple_of(s * nodes + i * tile, tile), tile)
            mid = h0[s, rows, :] + dot(attended[s, rows, :], w_out[...])
            h1[flat, :] = mid
            hat, _ = norm(mid)
            in_two = (hat * gains[1:2, :]).astype(BF)
            n2[flat, :] = in_two
            end = mid
            for c in range(4):
                cols = slice(c * D, (c + 1) * D)
                u = dot(in_two, w_up[:, cols])
                upper[flat, cols] = u
                a = (u * sigmoid(u)).astype(BF)
                act[flat, cols] = a
                end = end + dot(a, w_down[cols, :])
            h2[flat, :] = end
            hat, _ = norm(end)
            in_three = (hat * gains[2:3, :]).astype(BF)
            n3[flat, :] = in_three
            y_t = dot(in_three, w_dec[...]).T
            high, low = split(y_t[0:CP, :])
            pred[s * CP : (s + 1) * CP, rows] = high
            pred[(samples + s) * CP : (samples + s + 1) * CP, rows] = low

    d_pred[...] = jnp.zeros(d_pred.shape, F32)
    loss[...] = jnp.zeros(loss.shape, F32)

    @pl.loop(0, pixels // 256)
    def _(i):
        part = pl.ds(pl.multiple_of(i * 256, 256), 256)
        counts = dec_mt[:, part]
        y_all = dot(pred[...], counts)
        highs, lows = [], []
        for s in range(samples):
            y = y_all[s * CP : (s + 1) * CP] + y_all[(samples + s) * CP : (samples + s + 1) * CP]
            misfit = y * (1.0 / 3.0) - targets_t[s, :, part]
            g = weight[s : s + 1, part] * levels[...] * misfit
            loss[...] += jnp.sum(g * misfit, axis=0, keepdims=True)
            high, low = split(g * scale[0:1, 0:1])
            highs.append(high)
            lows.append(low)
        d_pred[...] += dot_nt(jnp.concatenate(highs + lows, axis=0), counts)

    total_out[...] = jnp.zeros(total_out.shape, F32)
    d_dec[...] = jnp.zeros(d_dec.shape, F32)
    d_gains[...] = jnp.zeros(d_gains.shape, F32)
    for s in range(samples):
        total = d_pred[s * CP : (s + 1) * CP] + d_pred[(samples + s) * CP : (samples + s + 1) * CP]
        padded = jnp.concatenate([total, jnp.zeros((128 - CP, nodes), F32)], axis=0)
        d_y[...] = padded.T.astype(BF)

        @pl.loop(0, tiles)
        def _(i):
            rows = pl.ds(pl.multiple_of(i * tile, tile), tile)
            flat = pl.ds(pl.multiple_of(s * nodes + i * tile, tile), tile)
            d_part = d_y[rows, :]
            d_dec[...] += dot_tn(n3[flat, :], d_part)
            grad = dot_nt(d_part, w_dec[...])
            hat, r = norm(h2[flat, :])
            d_gains[2:3, :] += jnp.sum(grad * hat, axis=0, keepdims=True)
            d_end = norm_back(grad, gains[2:3, :], hat, r)
            d_low = d_end.astype(BF)
            dm[flat, :] = d_low
            d_in = jnp.zeros((tile, D), F32)
            for c in range(4):
                cols = slice(c * D, (c + 1) * D)
                d_act = dot_nt(d_low, w_down[cols, :])
                d_u = (d_act * slope(upper[flat, cols])).astype(BF)
                du[flat, cols] = d_u
                d_in = d_in + dot_nt(d_u, w_up[:, cols])
            hat, r = norm(h1[flat, :])
            d_gains[1:2, :] += jnp.sum(d_in * hat, axis=0, keepdims=True)
            d_mid = d_end + norm_back(d_in, gains[1:2, :], hat, r)
            dh1[s, rows, :] = d_mid
            total_out[...] += dot_tn(attended[s, rows, :], d_mid.astype(BF))

    def copies(name, source, action):
        window_copies(here, plans[name], source, keep, send, sems, action)

    for c in range(4):
        cols = slice(c * D, (c + 1) * D)
        put_flat(d_down, dot_tn(act[:, cols], dm[...]), 4 * c * D, 4)
    copies("down", d_down, "start")
    put_flat(d_out, total_out[...], 0, 4)
    copies("out", d_out, "start")
    for c in range(4):
        cols = slice(c * D, (c + 1) * D)
        put_flat(d_up, dot_tn(n2[...], du[:, cols]), 4 * c, 16)
    copies("up", d_up, "start")
    copies("down", d_down, "wait")
    copies("out", d_out, "wait")
    copies("up", d_up, "wait")


def mlp(me, h0, attended, w_out, w_up, w_down, w_dec, gains, dec_mt, targets_t, weight, levels, scale,
        devices, shard, starts, win):
    samples, nodes, _ = h0.shape
    rows = samples * nodes
    plans, count = window_blocks_of(
        devices, shard, starts,
        (("out", ROW_OUT, 4 * D), ("up", ROW_UP, 16 * D), ("down", ROW_DOWN, 4 * FF)),
    )
    vmem = pl.BlockSpec(memory_space=pltpu.VMEM)
    hbm = pl.BlockSpec(memory_space=pl.ANY)
    return pl.pallas_call(
        functools.partial(mlp_body, plans),
        out_shape=[
            shape((samples, nodes, D)),
            shape((D, 128)),
            shape((8, D)),
            shape((1, 256)),
            shape((devices // 2, 4 * win, 128)),
            shape((devices // 2, 4 * win, 128)),
        ],
        in_specs=[pl.BlockSpec(memory_space=pltpu.SMEM)] + [vmem] * 12,
        out_specs=[vmem] * 4 + [hbm] * 2,
        scratch_shapes=[
            pltpu.VMEM((rows, D), F32),
            pltpu.VMEM((rows, D), BF),
            pltpu.VMEM((rows, FF), F32),
            pltpu.VMEM((rows, FF), BF),
            pltpu.VMEM((rows, D), F32),
            pltpu.VMEM((rows, D), BF),
            pltpu.VMEM((2 * samples * CP, nodes), BF),
            pltpu.VMEM((2 * samples * CP, nodes), F32),
            pltpu.VMEM((rows, D), BF),
            pltpu.VMEM((rows, FF), BF),
            pltpu.VMEM((nodes, 128), BF),
            pltpu.VMEM((D, D), F32),
            pltpu.VMEM((4 * D, 128), F32),
            pltpu.VMEM((16 * D, 128), F32),
            pltpu.VMEM((4 * FF, 128), F32),
            pltpu.SemaphoreType.DMA((count,)),
        ],
        compiler_params=pltpu.CompilerParams(vmem_limit_bytes=60 << 20),
        cost_estimate=pl.CostEstimate(flops=16 << 30, bytes_accessed=24 << 20, transcendentals=0),
    )(me, h0, attended, w_out, w_up, w_down, w_dec, gains, dec_mt, targets_t, weight, levels, scale)


def attend_back_body(
    qkv, before, after, log_c, dh1, w_out,
    d_query, d_own, d_before, d_after,
    pairs, do_both,
):
    samples, nodes, _ = dh1.shape
    halo = before.shape[1]
    for s in range(samples):
        gather_pairs(qkv, before, after, pairs, s)
        for i in range(nodes // 256):
            rows = slice(i * 256, (i + 1) * 256)
            da = dh1[s, rows, :].astype(BF)
            high, low = split(dot_nt(da, w_out[...]))
            for h in range(HEADS):
                lanes = slice(h * HEAD_DIM, (h + 1) * HEAD_DIM)
                do_both[rows, 2 * h * HEAD_DIM : (2 * h + 1) * HEAD_DIM] = high[:, lanes]
                do_both[rows, (2 * h + 1) * HEAD_DIM : (2 * h + 2) * HEAD_DIM] = low[:, lanes]
        for h in range(HEADS):
            lanes = slice(h * HEAD_DIM, (h + 1) * HEAD_DIM)
            vlanes = slice(D + h * HEAD_DIM, D + (h + 1) * HEAD_DIM)
            query = qkv[s, :, lanes]
            keys = pairs[:, lanes]
            values = pairs[:, vlanes]
            do = do_both[:, 2 * h * HEAD_DIM : (2 * h + 2) * HEAD_DIM]
            probs = attention_weights(keys, query, log_c)
            d_probs = dot_nt(jnp.concatenate([values, values], axis=1), do)
            centre = jnp.sum(probs * d_probs, 0, keepdims=True)
            high, low = split(probs * (d_probs - centre))
            dv2 = dot(probs.astype(BF), do)
            dv = dv2[:, :HEAD_DIM] + dv2[:, HEAD_DIM:]
            dk = (dot(high, query) + dot(low, query)) * SCALE
            dq_t = (dot_tn(keys, high) + dot_tn(keys, low)) * SCALE
            d_query[s, :, lanes] = dq_t.T.astype(BF)
            d_own[s, :, lanes] = dk[halo : halo + nodes]
            d_own[s, :, vlanes] = dv[halo : halo + nodes]
            d_before[s, :, lanes] = dk[:halo].astype(BF)
            d_before[s, :, vlanes] = dv[:halo].astype(BF)
            d_after[s, :, lanes] = dk[halo + nodes :].astype(BF)
            d_after[s, :, vlanes] = dv[halo + nodes :].astype(BF)


def attend_back(qkv, before, after, log_c, dh1, w_out):
    samples, nodes, _ = dh1.shape
    halo = before.shape[1]
    return kernel_call(
        attend_back_body,
        [
            shape((samples, nodes, D), BF),
            shape((samples, nodes, 2 * D)),
            shape((samples, halo, 2 * D), BF),
            shape((samples, halo, 2 * D), BF),
        ],
        [pltpu.VMEM((log_c.shape[0], 2 * D), BF), pltpu.VMEM((nodes, 2 * D), BF)],
        nbytes=20 << 20,
        flops=8 << 30,
    )(qkv, before, after, log_c, dh1, w_out)


def encode_back_body(
    plans,
    me, grid, w_enc, w_qkv, gains, enc_mt, h0, dh1, d_query, d_own, from_lower, from_upper,
    d_small, keep_in, send_in,
    keep, send,
    dqkv, n1, both, total_enc, d_gain, d_enc, d_qkv, small, sems,
):
    samples, nodes, _ = h0.shape
    here = me[0]

    def copies(name, source, action):
        window_copies(here, plans[name], source, keep, send, sems, action)

    small[...] = d_small[...]
    pixels = grid.shape[1]
    halo = from_lower.shape[1]
    d_gain[...] = jnp.zeros(d_gain.shape, F32)
    total_enc[...] = jnp.zeros(total_enc.shape, F32)
    for s in range(samples):
        base = s * nodes
        dqkv[base : base + nodes, 0:D] = d_query[s]
        dqkv[base : base + nodes, D:] = d_own[s].astype(BF)
        low_rim = d_own[s, 0:halo, :] + from_lower[s].astype(F32)
        dqkv[base : base + halo, D:] = low_rim.astype(BF)
        high_rim = d_own[s, nodes - halo :, :] + from_upper[s].astype(F32)
        dqkv[base + nodes - halo : base + nodes, D:] = high_rim.astype(BF)
        for i in range(nodes // 256):
            rows = slice(i * 256, (i + 1) * 256)
            flat = slice(base + i * 256, base + (i + 1) * 256)
            hat, r = norm(h0[s, rows, :])
            n1[flat, :] = (hat * gains[0:1, :]).astype(BF)
            grad = dot_nt(dqkv[flat, :], w_qkv[...])
            d_gain[0:1, :] += jnp.sum(grad * hat, axis=0, keepdims=True)
            d_start = dh1[s, rows, :] + norm_back(grad, gains[0:1, :], hat, r)
            high, low = split(d_start * 0.25)
            both[rows, 0:D] = high
            both[rows, D:] = low

        @pl.loop(0, pixels // 256)
        def _(i):
            rows = pl.ds(pl.multiple_of(i * 256, 256), 256)
            x = grid[s, rows, :]
            pre = dot(x, w_enc[...])
            spread2 = dot(enc_mt[rows, :], both[...])
            spread = spread2[:, 0:D] + spread2[:, D:]
            d_pre = (spread * slope(pre)).astype(BF)
            total_enc[...] += dot_tn(x, d_pre)

    for c in range(3):
        put_flat(d_qkv, dot_tn(n1[...], dqkv[:, c * D : (c + 1) * D]), 4 * c, 12)
    copies("qkv", d_qkv, "start")
    put_flat(d_enc, total_enc[...], 0, 4)
    for lane in range(D // 128):
        row = 4 * C_OUT + lane
        small[row : row + 1, :] = d_gain[0:1, lane * 128 : lane * 128 + 128]
    for action in ("start", "wait"):
        copies("enc", d_enc, action)
        copies("small", small, action)
        if action == "wait":
            copies("qkv", d_qkv, action)


def encode_back(me, grid, w_enc, w_qkv, gains, enc_mt, h0, dh1, d_query, d_own, from_lower, from_upper,
                d_small, keep, send, devices, shard, starts):
    samples, nodes, _ = h0.shape
    rows = samples * nodes
    plans, count = window_blocks_of(
        devices, shard, starts,
        (("enc", ROW_ENC, 4 * C_IN), ("qkv", ROW_QKV, 12 * D), ("small", ROW_DEC, d_small.shape[0])),
    )
    vmem = pl.BlockSpec(memory_space=pltpu.VMEM)
    hbm = pl.BlockSpec(memory_space=pl.ANY)
    return pl.pallas_call(
        functools.partial(encode_back_body, plans),
        out_shape=[shape(keep.shape), shape(send.shape)],
        in_specs=[pl.BlockSpec(memory_space=pltpu.SMEM)] + [vmem] * 12 + [hbm] * 2,
        out_specs=[hbm, hbm],
        input_output_aliases={13: 0, 14: 1},
        scratch_shapes=[
            pltpu.VMEM((rows, 3 * D), BF),
            pltpu.VMEM((rows, D), BF),
            pltpu.VMEM((nodes, 2 * D), BF),
            pltpu.VMEM((C_IN, D), F32),
            pltpu.VMEM((8, D), F32),
            pltpu.VMEM((4 * C_IN, 128), F32),
            pltpu.VMEM((12 * D, 128), F32),
            pltpu.VMEM(d_small.shape, F32),
            pltpu.SemaphoreType.DMA((count,)),
        ],
        compiler_params=pltpu.CompilerParams(vmem_limit_bytes=58 << 20),
        cost_estimate=pl.CostEstimate(flops=12 << 30, bytes_accessed=24 << 20, transcendentals=0),
    )(me, grid, w_enc, w_qkv, gains, enc_mt, h0, dh1, d_query, d_own, from_lower, from_upper,
      d_small, keep, send)


def ring(axis, distance):
    count = lax.axis_size(axis)
    return [(i, (i + distance) % count) for i in range(count)]


def window_plan(shard, count):
    starts = [(LEAD * D + d * shard) // (16 * D) * 16 for d in range(count)]
    ends = [-(-(LEAD * D + (d + 1) * shard) // D) for d in range(count)]
    rows = max(-(-(e - s + 1) // 16) * 16 for s, e in zip(starts, ends))
    return starts, rows


def per_device(
    grid, targets, area, sigma_weight, level_weight, valid, enc_index, dec_index, neighbours,
    params, first_moment, second_moment, average,
):
    shard = params.shape[0]
    devices = lax.axis_size(AXES)
    me = lax.axis_index(AXES)
    nodes = neighbours.shape[0]
    halo = nodes // 16
    starts, win = window_plan(shard, devices)
    begin = LEAD * D + me * shard
    shift = begin - begin // (16 * D) * (16 * D)

    mesh_axes = (lax.axis_size("patch"), lax.axis_size("dp"))
    place = me.astype(jnp.int32).reshape(1)

    count = jnp.sum(valid)
    digits = jnp.stack([count // 128, count % 128]).astype(BF)
    payload = lax.dynamic_update_slice(jnp.zeros((win * D,), BF), params.astype(BF), (shift,))
    payload = lax.dynamic_update_slice(payload, digits, ((win - 1) * D,))
    weight = valid.astype(F32) * area[None, :] * sigma_weight[:, None]
    levels = jnp.pad(level_weight, (0, CP - C_OUT)).reshape(CP, 1)
    meanwhile = prep(enc_index, dec_index, neighbours, targets), weight, levels, grid
    pieces, plan, meanwhile = gather_windows(payload.reshape(win, D), mesh_axes, meanwhile)
    (enc_m, enc_mt, dec_mt, log_c, targets_t), weight, levels, grid = meanwhile

    w_enc, w_qkv, w_out, w_up, w_down, tail, counted = unpack(
        place, pieces, plan, devices, win, starts
    )
    count_total = counted[0, 0]
    w_dec = jnp.pad(tail[:C_OUT].reshape(D, C_OUT), ((0, 0), (0, 128 - C_OUT)))
    gains = jnp.pad(tail[C_OUT : C_OUT + 3].astype(F32), ((0, 5), (0, 0)))

    h0, qkv = encode(grid, w_enc, enc_m, w_qkv, gains)
    before = lax.ppermute(qkv[:, nodes - halo :, D:], "patch", ring("patch", 1))
    after = lax.ppermute(qkv[:, :halo, D:], "patch", ring("patch", -1))
    attended = attend(qkv, before, after, log_c)
    scale = 2.0 / counted * (1.0 / 3.0)
    dh1, d_dec, d_gains, loss_rows, keep, send = mlp(
        place, h0, attended, w_out, w_up, w_down, w_dec, gains, dec_mt, targets_t, weight, levels,
        scale, devices, shard, starts, win,
    )
    d_query, d_own, d_before, d_after = attend_back(qkv, before, after, log_c, dh1, w_out)
    from_upper = lax.ppermute(d_before, "patch", ring("patch", -1))
    from_lower = lax.ppermute(d_after, "patch", ring("patch", 1))
    d_small = jnp.concatenate(
        [
            d_dec[:, :C_OUT].reshape(4 * C_OUT, 128),
            jnp.zeros((4, 128), F32),
            d_gains[1:3].reshape(8, 128),
            jnp.zeros((4 * (ROWS_ALL - ROW_END), 128), F32),
        ]
    )
    keep, send = encode_back(
        place, grid, w_enc, w_qkv, gains, enc_mt, h0, dh1, d_query, d_own, from_lower, from_upper,
        d_small, keep, send, devices, shard, starts,
    )
    grad_window = sum_windows(keep, send, mesh_axes)
    grad = lax.dynamic_slice(grad_window.reshape(-1), (shift,), (shard,))

    positions = me * shard + lax.iota(jnp.int32, shard)
    member = jnp.stack(
        [
            ((positions >= lower) & (positions < upper)).astype(F32)
            for lower, upper in segment_bounds()
        ]
    )
    new_first = BETA_ONE * first_moment + (1.0 - BETA_ONE) * grad
    new_second = BETA_TWO * second_moment + (1.0 - BETA_TWO) * grad * grad
    update = (
        new_first
        / (1.0 - BETA_ONE**STEP)
        / (jnp.sqrt(new_second / (1.0 - BETA_TWO**STEP)) + LAMB_EPS)
        + DECAY * params
    )
    squares = jnp.concatenate(
        [
            jnp.sum(member * (params * params)[None, :], axis=1),
            jnp.sum(member * (update * update)[None, :], axis=1),
            jnp.sum(loss_rows).reshape(1),
        ]
    )
    totals = sum_everywhere(squares, mesh_axes)
    norms = jnp.sqrt(totals[:14]).reshape(2, 7)
    ratio = norms[0] / norms[1]
    step_ratio = jnp.sum(member * ratio[:, None], axis=0)
    new_params = params - RATE * step_ratio * update
    new_average = EMA_KEEP * average + (1.0 - EMA_KEEP) * new_params
    return (
        jnp.stack([totals[14], count_total]),
        norms,
        new_params,
        new_first,
        new_second,
        new_average,
    )


def solution(mesh):
    flat = P(AXES)
    in_specs = (
        P("dp", "patch", None),
        P("dp", "patch", None),
        P("patch"),
        P("dp"),
        P(),
        P("dp", "patch"),
        P("patch", None),
        P("patch", None),
        P("patch", None),
        flat,
        flat,
        flat,
        flat,
    )
    out_specs = (P(), P(), flat, flat, flat, flat)
    return jax.shard_map(
        per_device, mesh=mesh, in_specs=in_specs, out_specs=out_specs, check_vma=False
    )
```

```python
import functools
import math

import jax
import jax.numpy as jnp
from jax import lax
from jax.experimental import pallas as pl
from jax.experimental.pallas import tpu as pltpu
from jax.sharding import PartitionSpec as P

D = 512
HEADS = 4
HEAD_DIM = 128
FF = 2048
C_OUT = 84
C_IN = 264
STEP = 10
EPS_NORM = 1e-05
BETA_ONE = 0.9
BETA_TWO = 0.999
LAMB_EPS = 1e-06
DECAY = 0.01
RATE = 0.2
EMA_KEEP = 0.8
BF = jnp.bfloat16
F32 = jnp.float32
SCALE = HEAD_DIM ** (-0.5)
LOG2E = 1.4426950408889634
ABSENT = -1e30
CP = 96
AXES = ("patch", "dp")

LEAD = 8
ROW_ENC = LEAD
ROW_QKV = ROW_ENC + C_IN
ROW_OUT = ROW_QKV + 3 * D
ROW_UP = ROW_OUT + D
ROW_DOWN = ROW_UP + 4 * D
ROW_DEC = ROW_DOWN + FF
ROW_GAIN = ROW_DEC + C_OUT
ROW_END = ROW_GAIN + 3
ROWS_ALL = -(-ROW_END // 16) * 16


def matrix_shapes():
    return [(C_IN, D), (D, 3 * D), (D, D), (D, FF), (FF, D), (D, C_OUT), (3, D)]


def segment_bounds():
    bounds = []
    offset = 0
    for row_count, col_count in matrix_shapes():
        bounds.append((offset, offset + row_count * col_count))
        offset += row_count * col_count
    return bounds


NPARAM_USED = segment_bounds()[-1][1]


def dot(a, b):
    return lax.dot_general(a, b, (((1,), (0,)), ((), ())), preferred_element_type=F32)


def dot_nt(a, b):
    return lax.dot_general(a, b, (((1,), (1,)), ((), ())), preferred_element_type=F32)


def dot_tn(a, b):
    return lax.dot_general(a, b, (((0,), (0,)), ((), ())), preferred_element_type=F32)


def split(x):
    high = x.astype(BF)
    return high, (x - high.astype(F32)).astype(BF)


def sigmoid(x):
    return 0.5 * jnp.tanh(0.5 * x) + 0.5


def slope(x, s):
    return s * (1.0 + x * (1.0 - s))


def norm(x):
    c = x - jnp.mean(x, -1, keepdims=True)
    r = lax.rsqrt(jnp.mean(c * c, -1, keepdims=True) + EPS_NORM)
    return c * r, r


def norm_back(grad, gain, hat, r):
    g = grad * gain
    return r * (
        g
        - jnp.mean(g, -1, keepdims=True)
        - hat * jnp.mean(g * hat, -1, keepdims=True)
    )


def put_flat(ref, value, first, period):
    for lane in range(D // 128):
        ref[pl.ds(first + lane, value.shape[0], stride=period), :] = value[
            :, lane * 128 : lane * 128 + 128
        ]


def kernel_call(body, out_shape, scratch=(), flops=0, nbytes=0):
    return pl.pallas_call(
        body,
        out_shape=out_shape,
        scratch_shapes=list(scratch),
        compiler_params=pltpu.CompilerParams(vmem_limit_bytes=58 << 20),
        cost_estimate=pl.CostEstimate(flops=flops, bytes_accessed=nbytes, transcendentals=0),
    )


def shape(dims, dtype=F32):
    return jax.ShapeDtypeStruct(tuple(dims), dtype)


def count_rows(index_t, base, rows, cols):
    ids = lax.broadcasted_iota(jnp.int32, (rows, cols), 0) + base
    total = jnp.zeros((rows, cols), F32)
    for k in range(index_t.shape[0]):
        total = total + jnp.where(index_t[k : k + 1, :] == ids, 1.0, 0.0)
    return total


def count_encoder_body(enc, enc_t, enc_m, enc_mt):
    nodes, pixels = enc_m.shape

    @pl.loop(0, nodes // 32)
    def _(i):
        rows = pl.ds(pl.multiple_of(i * 32, 32), 32)
        index = enc[rows, :]
        ids = lax.broadcasted_iota(jnp.int32, (32, pixels), 1)
        total = jnp.zeros((32, pixels), F32)
        for k in range(index.shape[1]):
            total = total + jnp.where(index[:, k : k + 1] == ids, 1.0, 0.0)
        enc_m[rows, :] = total.astype(BF)

    @pl.loop(0, pixels // 64)
    def _(i):
        rows = pl.ds(pl.multiple_of(i * 64, 64), 64)
        enc_mt[rows, :] = count_rows(enc_t, i * 64, 64, nodes).astype(BF)


def count_rest_body(dec_t, nbr_t, targets, dec_mt, log_c, targets_t):
    nodes, pixels = dec_mt.shape

    @pl.loop(0, nodes // 32)
    def _(i):
        rows = pl.ds(pl.multiple_of(i * 32, 32), 32)
        dec_mt[rows, :] = count_rows(dec_t, i * 32, 32, pixels).astype(BF)

    @pl.loop(0, log_c.shape[0] // 64)
    def _(i):
        rows = pl.ds(pl.multiple_of(i * 64, 64), 64)
        total = count_rows(nbr_t, i * 64, 64, nodes)
        log_c[rows, :] = jnp.where(total > 0.0, jnp.log2(jnp.maximum(total, 1.0)), ABSENT)

    targets_t[...] = jnp.zeros(targets_t.shape, F32)
    for s in range(targets.shape[0]):

        @pl.loop(0, pixels // 256)
        def _(i):
            part = pl.ds(pl.multiple_of(i * 256, 256), 256)
            targets_t[s, 0:C_OUT, part] = targets[s, part, :].T


def count_encoder(enc_index, pixels):
    nodes = enc_index.shape[0]
    return kernel_call(
        count_encoder_body,
        [shape((nodes, pixels), BF), shape((pixels, nodes), BF)],
        nbytes=5 << 20,
        flops=1 << 29,
    )(enc_index, enc_index.T)


def count_rest(dec_index, neighbours, targets):
    nodes, pixels = neighbours.shape[0], dec_index.shape[0]
    ext = nodes + 2 * (nodes // 16)
    return kernel_call(
        count_rest_body,
        [shape((nodes, pixels), BF), shape((ext, nodes)), shape((targets.shape[0], CP, pixels))],
        nbytes=8 << 20,
        flops=1 << 29,
    )(dec_index.T, neighbours.T, targets)


def tile_sources(starts, rows):
    return [
        [(d, tile * 16 - s) for d, s in enumerate(starts) if s <= tile * 16 < s + rows]
        for tile in range(ROWS_ALL // 16)
    ]


def assemble(read, window_rows, sources, first_row, rows, put):
    tile, last = first_row // 16, (first_row + rows) // 16
    while tile < last:
        source = sources[tile]
        if len(source) == 1:
            count = 1
            while (
                tile + count < last
                and len(sources[tile + count]) == 1
                and sources[tile + count][0][0] == source[0][0]
                and count < 8
            ):
                count += 1
            d, off = source[0]
            value = read(d, off, 16 * count)
        else:
            count = 1
            value = None
            for d, off in source:
                part = read(d, off, 16).astype(F32)
                if off + 16 == window_rows:
                    part = jnp.where(
                        lax.broadcasted_iota(jnp.int32, part.shape, 0) < 15, part, 0.0
                    )
                value = part if value is None else value + part
            value = value.astype(BF)
        put(tile * 16 - first_row, value)
        tile += count


def wide(stage, ref, period):
    for lane in range(D // 128):
        for c in range(period):
            lanes = slice(c * D + lane * 128, c * D + lane * 128 + 128)
            ref[:, lanes] = stage[lane, pl.ds(c, ref.shape[0], stride=period), :].astype(BF)


def unpack_body(plan, parts, sources, place_of, count, *refs):
    me, pieces, refs = refs[0], refs[1 : count + 1], refs[count + 1 :]
    outs, (windows, stage, sems) = refs[: len(parts)], refs[len(parts) :]
    copies = []

    for k, (piece, at, slot, first, rows) in enumerate(plan):
        copy = pltpu.make_async_copy(
            pieces[piece].at[pl.ds(at, rows), :],
            windows.at[slot, pl.ds(first, rows), :],
            sems.at[k],
        )
        copy.start()
        copies.append(copy)
    for copy in copies:
        copy.wait()
    here = me[0]
    window_rows = windows.shape[1]

    def read(d, off, rows):
        return windows[place_of(here, d), off : off + rows, :]

    for part, ref in zip(parts, outs):
        if part == "count":
            total = jnp.sum(windows[:, window_rows - 16 :, 0:128].astype(F32), axis=0)[15:16, :]
            lanes = lax.broadcasted_iota(jnp.int32, (1, 128), 1)
            digits = jnp.where(lanes == 0, 128.0, jnp.where(lanes == 1, 1.0, 0.0)) * total
            ref[...] = jnp.sum(digits, axis=1, keepdims=True) + jnp.zeros((8, 128), F32)
            continue
        first, rows, period, _ = PARTS[part]

        def direct(off, value):
            ref[off : off + value.shape[0], :] = value

        def staged(off, value):
            wide_value = value.astype(F32)
            for lane in range(D // 128):
                stage[lane, off : off + value.shape[0], :] = wide_value[
                    :, lane * 128 : lane * 128 + 128
                ]

        if part == "gain":
            assemble(read, window_rows, sources, first, rows, staged)
            row = ROW_GAIN - first
            for lane in range(D // 128):
                ref[:, lane * 128 : lane * 128 + 128] = stage[lane, row : row + 1, :] + jnp.zeros(
                    (8, 128), F32
                )
        elif period == 1:
            assemble(read, window_rows, sources, first, rows, direct)
        else:
            assemble(read, window_rows, sources, first, rows, staged)
            if part == "enc":
                for lane in range(D // 128):
                    lanes = slice(lane * 128, lane * 128 + 128)
                    ref[:, lanes] = stage[lane, LEAD:ROW_QKV, :].astype(BF)
            else:
                wide(stage, ref, period)


PARTS = {
    "enc": (0, ROW_QKV, 0, (C_IN, D)),
    "qkv": (ROW_QKV, 3 * D, 3, (D, 3 * D)),
    "gain": (ROW_GAIN // 16 * 16, 16, 0, (8, D)),
    "out": (ROW_OUT, D, 1, (D, D)),
    "up": (ROW_UP, 4 * D, 4, (D, FF)),
    "down": (ROW_DOWN, FF, 1, (FF, D)),
    "tail": (ROW_DEC, ROWS_ALL - ROW_DEC, 1, (ROWS_ALL - ROW_DEC, D)),
}


def unpack(me, pieces, plan, parts, place_of, slots, rows, starts):
    sources = tile_sources(starts, rows)
    outs = [
        shape((8, 128)) if p == "count" else shape(PARTS[p][3], F32 if p == "gain" else BF)
        for p in parts
    ]
    return pl.pallas_call(
        functools.partial(unpack_body, plan, parts, sources, place_of, len(pieces)),
        out_shape=outs,
        in_specs=[pl.BlockSpec(memory_space=pltpu.SMEM)]
        + [pl.BlockSpec(memory_space=pl.ANY)] * len(pieces),
        scratch_shapes=[
            pltpu.VMEM((slots, rows, D), BF),
            pltpu.VMEM((D // 128, 4 * D, 128), F32),
            pltpu.SemaphoreType.DMA((len(plan),)),
        ],
        compiler_params=pltpu.CompilerParams(vmem_limit_bytes=58 << 20),
        cost_estimate=pl.CostEstimate(
            flops=0, bytes_accessed=slots * rows * D * 4, transcendentals=0
        ),
    )(me, *pieces)


def permute(x, mask):
    count = lax.axis_size(AXES)
    return lax.ppermute(x, AXES, [(d, d ^ mask) for d in range(count)])


def place_by_xor(here, d):
    return jnp.bitwise_xor(here, d)


def gather_windows(window, first_work, second_work):
    rows = window.shape[0]
    half = rows // 2
    pieces, plan = [], []

    def add(piece, near, parts):
        for part, flip in ((piece, 0), (permute(piece, 1), 1)):
            for at, slot, to, size in parts:
                plan.append((len(pieces), at, slot ^ near ^ flip, to, size))
            pieces.append(part)

    planes = (8, 16, 24)
    others = [permute(window, m) for m in planes]
    by_x, by_y = permute(window, 2), permute(window, 4)
    first_done = first_work()
    others, by_x, by_y, first_done = lax.optimization_barrier(
        (jnp.concatenate(others), by_x, by_y, first_done)
    )
    others_x, others_y = permute(others, 2), permute(others, 4)
    second_done = second_work()
    others_x, others_y, second_done = lax.optimization_barrier((others_x, others_y, second_done))

    def halves(near_part, far_part, first):
        far = [far_part[i * rows + first : i * rows + first + half] for i in range(3)]
        return jnp.concatenate([near_part[first : first + half]] + far)

    across_a = permute(halves(by_y, others_y, 0), 2)
    across_b = permute(halves(by_x, others_x, half), 4)
    whole = [(0, 0, 0, rows)]
    stacked = [(i * rows, slot, 0, rows) for i, slot in enumerate(planes)]
    add(window, 0, whole)
    add(by_x, 2, whole)
    add(by_y, 4, whole)
    add(others, 0, stacked)
    add(others_x, 2, stacked)
    add(others_y, 4, stacked)
    add(across_a, 6, [(i * half, slot, 0, half) for i, slot in enumerate((0,) + planes)])
    add(across_b, 6, [(i * half, slot, half, half) for i, slot in enumerate((0,) + planes)])
    return pieces, plan, first_done, second_done


def encode_body(grid, w_enc, enc_m, w_qkv, gains, h0, qkv, high, low):
    samples, pixels = grid.shape[0], grid.shape[2]
    nodes = h0.shape[1]
    for s in range(samples):

        @pl.loop(0, pixels // 512, unroll=True)
        def _(i):
            rows = pl.ds(pl.multiple_of(i * 512, 512), 512)
            pre = dot_tn(grid[s, :, rows], w_enc[...])
            value = pre * sigmoid(pre)
            high[rows, :], low[rows, :] = split(value)

        @pl.loop(0, nodes // 512, unroll=True)
        def _(i):
            rows = pl.ds(pl.multiple_of(i * 512, 512), 512)
            counts = enc_m[rows, :]
            start = (dot(counts, high[...]) + dot(counts, low[...])) * 0.25
            h0[s, rows, :] = start
            hat, _ = norm(start)
            n1 = (hat * gains[0:1, :]).astype(BF)
            qkv[s, rows, :] = dot(n1, w_qkv[...]).astype(BF)


def encode(grid, w_enc, enc_m, w_qkv, gains):
    samples, pixels = grid.shape[0], grid.shape[2]
    nodes = enc_m.shape[0]
    return kernel_call(
        encode_body,
        [shape((samples, nodes, D)), shape((samples, nodes, 3 * D), BF)],
        [pltpu.VMEM((pixels, D), BF), pltpu.VMEM((pixels, D), BF)],
        nbytes=12 << 20,
        flops=8 << 30,
    )(grid, w_enc, enc_m, w_qkv, gains)


def gather_pairs(qkv, before, after, pairs, s):
    halo, nodes = before.shape[1], qkv.shape[1]
    pairs[0:halo, :] = before[s]
    pairs[halo : halo + nodes, :] = qkv[s, :, D:]
    pairs[halo + nodes :, :] = after[s]


def attention_weights(keys, query, log_c):
    x = dot_nt(keys, query) * (SCALE * LOG2E) + log_c[...]
    e = jnp.exp2(x - jnp.max(x, 0, keepdims=True))
    return e * (1.0 / jnp.sum(e, 0, keepdims=True))


def attend_body(qkv, before, after, log_c, out, pairs):
    for s in range(qkv.shape[0]):
        gather_pairs(qkv, before, after, pairs, s)
        for h in range(HEADS):
            lanes = slice(h * HEAD_DIM, (h + 1) * HEAD_DIM)
            keys = pairs[:, lanes]
            values = pairs[:, D + h * HEAD_DIM : D + (h + 1) * HEAD_DIM]
            probs = attention_weights(keys, qkv[s, :, lanes], log_c)
            out_t = dot_tn(values, probs.astype(BF))
            out[s, :, lanes] = out_t.T.astype(BF)


def attend(qkv, before, after, log_c):
    samples, nodes = qkv.shape[:2]
    return kernel_call(
        attend_body,
        shape((samples, nodes, D), BF),
        [pltpu.VMEM((log_c.shape[0], 2 * D), BF)],
        nbytes=8 << 20,
        flops=2 << 30,
    )(qkv, before, after, log_c)


class Layout:
    def __init__(self, shard, devices, fast):
        self.devices = devices
        self.starts, self.win = window_plan(shard, devices)
        self.rows = 4 * self.win
        self.begins = [(LEAD * D + d * shard) // 1024 * 8 for d in range(devices)]
        self.ends = [-(-(LEAD * D + (d + 1) * shard) // 1024) * 8 for d in range(devices)]
        self.small = 4 * (ROWS_ALL - ROW_DEC)
        first = (("out", ROW_OUT, 4 * D), ("up", ROW_UP, 16 * D), ("down", ROW_DOWN, 4 * FF))
        second = (("enc", ROW_ENC, 4 * C_IN), ("qkv", ROW_QKV, 12 * D), ("small", ROW_DEC, self.small))
        self.fast = fast
        if fast:
            self.apart = 4 * (ROW_OUT - self.starts[8])
            self.sizes = (12 * self.rows, 4 * self.rows + self.apart + self.small)
        else:
            self.sizes = (sum(x[2] for x in first), sum(x[2] for x in second))
        self.plans = self.make(first, 1), self.make(second, 0)

    def make(self, arrays, plane):
        plans, k, at = {}, 0, 0
        for name, row, size in arrays:
            plans[name] = []
            if not self.fast:
                plans[name].append((k, None, at, 0, size))
                k, at = k + 1, at + size
                continue
            if name == "small":
                plans[name].append((k, "both", 4 * self.rows + self.apart, 0, size))
                k += 2
                continue
            for d, (lower, upper, start) in enumerate(zip(self.begins, self.ends, self.starts)):
                low, high = max(lower, 4 * row), min(upper, 4 * (row + size // 4))
                if low >= high:
                    continue
                if d == 8 and plane == 0:
                    to = 4 * self.rows + low - 4 * start
                    plans[name].append((k, "both", to, low - 4 * row, high - low))
                    k += 2
                else:
                    place = (d // 8 - plane) * 4 * self.rows + low - 4 * start
                    plans[name].append((k, d % 8, place, low - 4 * row, high - low))
                    k += 1
        return plans, k


def window_copies(here, rows_of_slot, blocks, source, keep, send, sems, action):
    for k, near, to, at, rows in blocks:

        def copy(target, first, sem):
            getattr(
                pltpu.make_async_copy(
                    source.at[pl.ds(at, rows), :], target.at[pl.ds(first, rows), :], sems.at[sem]
                ),
                action,
            )()

        if near is None:
            copy(keep, to, k)
        elif near == "both":
            copy(keep, to, k)
            copy(send, to, k + 1)
        else:
            slot = jnp.bitwise_and(jnp.bitwise_xor(here, near), 7)
            first = pl.multiple_of(lax.shift_right_logical(slot, 1) * rows_of_slot + to, 8)
            for target, side in ((keep, 0), (send, 1)):

                @pl.when(jnp.bitwise_and(slot, 1) == side)
                def _():
                    copy(target, first, k)


def sum_flat(first, second, layout):
    flat = jnp.concatenate(
        [
            jnp.zeros((4 * LEAD, 128), F32),
            second[: 4 * (ROW_OUT - LEAD)],
            first,
            second[4 * (ROW_OUT - LEAD) :],
            jnp.zeros((max(0, 4 * (layout.starts[-1] + layout.win - ROWS_ALL)), 128), F32),
        ]
    )
    windows = jnp.concatenate([flat[4 * s : 4 * s + layout.rows] for s in layout.starts])
    return lax.psum_scatter(windows, AXES, scatter_dimension=0, tiled=True)


def low(x):
    return x.astype(BF)


def packed(blocks, extra):
    return low(jnp.concatenate([blocks.reshape(-1, 128), extra]))


def add_packed(flat, blocks, extra):
    flat = flat.astype(F32)
    count = flat.shape[0] - extra.shape[0]
    return blocks + flat[:count].reshape(blocks.shape), extra + flat[count:]


def across_planes(x, allowed, k):
    pairs = [(d, d ^ (8 * k)) for d in range(32) if allowed((d ^ (8 * k)) // 8, d % 8)]
    return lax.ppermute(x, AXES, pairs)


def sum_rest(early, early_got, second, layout, me):
    rows = layout.rows
    half = rows // 2
    near, mine = me % 8, me // 8

    late = second[0] + permute(second[1], 1)
    early_a = early[:, :, 0, :half] + early_got[0].astype(F32)
    early_b = early[:, 0, :, half:] + early_got[1].astype(F32)
    early_a = early_a[:, 0] + permute(low(early_a[:, 1]), 4).astype(F32)
    early_b = early_b[:, 0] + permute(low(early_b[:, 1]), 2).astype(F32)
    planes = jnp.concatenate([early_a, early_b], axis=1)

    def plane(k):
        return lax.dynamic_index_in_dim(
            planes, jnp.maximum(jnp.bitwise_xor(mine, k) - 1, 0), 0, False
        )

    upper = plane(0)
    for k in (1, 2, 3):
        upper = upper + across_planes(low(plane(k)), lambda p, q: p > 0, k).astype(F32)

    apart = late[4 * rows :]
    late = late[: 4 * rows].reshape(2, 2, rows, 128)
    cut = apart.shape[0] // 2
    late_a, apart_a = add_packed(
        permute(packed(late[:, 1, :half], apart[:cut]), 2), late[:, 0, :half], apart[:cut]
    )
    late_b, apart_b = add_packed(
        permute(packed(late[1, :, half:], apart[cut:]), 4), late[0, :, half:], apart[cut:]
    )
    late_a, apart_a = add_packed(permute(packed(late_a[1], apart_a), 4), late_a[0], apart_a)
    late_b, apart_b = add_packed(permute(packed(late_b[1], apart_b), 2), late_b[0], apart_b)
    apart = jnp.concatenate([apart_a, apart_b])
    lead, small = layout.apart, 4 * (ROW_DEC - layout.starts[31])
    one = jnp.concatenate([apart[:lead], jnp.zeros((rows - lead, 128), F32)])
    three = jnp.concatenate([jnp.zeros((small, 128), F32), apart[lead : lead + rows - small]])
    parts = jnp.stack([jnp.concatenate([late_a, late_b]), one, one, three])

    def part(k):
        return lax.dynamic_index_in_dim(parts, jnp.bitwise_xor(mine, k), 0, False)

    lower = part(0)
    for k in (1, 2, 3):
        got = across_planes(
            low(part(k)), lambda p, q: p == 0 or (p, q) == (1, 0) or (p, q) == (3, 7), k
        )
        lower = lower + got.astype(F32)
    row = lax.broadcasted_iota(jnp.int32, (rows, 1), 0)
    take = (mine == 0) | ((me == 8) & (row < lead)) | ((me == 31) & (row >= small))
    return jnp.where(take, lower, upper)


def sum_everywhere(x, fast):
    if not fast:
        return lax.psum(x, AXES)
    for k in range(5):
        x = x + permute(x, 1 << k)
    return x


def mlp_body(
    layout,
    me, h0, attended, w_out, w_dec, gains, weight, levels, scale, w_up_hbm, w_down_hbm, dec_mt_hbm, targets_hbm,
    dh1, d_dec, d_gains, loss, keep, send,
    h1, n2, upper, act, h2, n3, pred, d_pred, dm, du, d_y, total_out, d_out, d_up, d_down, w_up, w_down, dec_mt, targets_t, sems, in_sems,
):
    samples, nodes, _ = h0.shape
    here = me[0]
    loads = [
        pltpu.make_async_copy(source, target, in_sems.at[k])
        for k, (source, target) in enumerate(
            ((w_up_hbm, w_up), (w_down_hbm, w_down), (dec_mt_hbm, dec_mt), (targets_hbm, targets_t))
        )
    ]
    for load in loads:
        load.start()
    pixels = dec_mt.shape[1]
    tile = 512
    tiles = nodes // tile
    for s in range(samples):

        @pl.loop(0, tiles, unroll=True)
        def _(i):
            rows = pl.ds(pl.multiple_of(i * tile, tile), tile)
            flat = pl.ds(pl.multiple_of(s * nodes + i * tile, tile), tile)
            mid = h0[s, rows, :] + dot(attended[s, rows, :], w_out[...])
            h1[flat, :] = mid
            hat, _ = norm(mid)
            in_two = (hat * gains[1:2, :]).astype(BF)
            n2[flat, :] = in_two
            if s == 0:
                loads[0].wait()
                loads[1].wait()
            end = mid
            for c in range(4):
                cols = slice(c * D, (c + 1) * D)
                u = dot(in_two, w_up[:, cols])
                sig = sigmoid(u)
                upper[flat, cols] = slope(u, sig)
                a = (u * sig).astype(BF)
                act[flat, cols] = a
                end = end + dot(a, w_down[cols, :])
            h2[flat, :] = end
            hat, _ = norm(end)
            in_three = (hat * gains[2:3, :]).astype(BF)
            n3[flat, :] = in_three
            y_t = dot(in_three, w_dec[...]).T
            high, low = split(y_t[0:CP, :])
            pred[s * CP : (s + 1) * CP, rows] = high
            pred[(samples + s) * CP : (samples + s + 1) * CP, rows] = low

    loads[2].wait()
    loads[3].wait()
    d_pred[...] = jnp.zeros(d_pred.shape, F32)
    loss[...] = jnp.zeros(loss.shape, F32)

    @pl.loop(0, pixels // 512)
    def _(i):
        part = pl.ds(pl.multiple_of(i * 512, 512), 512)
        counts = dec_mt[:, part]
        y_all = dot(pred[...], counts)
        highs, lows = [], []
        for s in range(samples):
            y = y_all[s * CP : (s + 1) * CP] + y_all[(samples + s) * CP : (samples + s + 1) * CP]
            misfit = y * (1.0 / 3.0) - targets_t[s, :, part]
            g = weight[s : s + 1, part] * levels[...] * misfit
            loss[...] += jnp.sum(g * misfit, axis=0, keepdims=True)
            high, low = split(g * scale[0:1, 0:1])
            highs.append(high)
            lows.append(low)
        d_pred[...] += dot_nt(jnp.concatenate(highs + lows, axis=0), counts)

    total_out[...] = jnp.zeros(total_out.shape, F32)
    d_dec[...] = jnp.zeros(d_dec.shape, F32)
    d_gains[...] = jnp.zeros(d_gains.shape, F32)
    for s in range(samples):
        total = d_pred[s * CP : (s + 1) * CP] + d_pred[(samples + s) * CP : (samples + s + 1) * CP]
        padded = jnp.concatenate([total, jnp.zeros((128 - CP, nodes), F32)], axis=0)
        d_y[...] = padded.T.astype(BF)

        @pl.loop(0, tiles, unroll=True)
        def _(i):
            rows = pl.ds(pl.multiple_of(i * tile, tile), tile)
            flat = pl.ds(pl.multiple_of(s * nodes + i * tile, tile), tile)
            d_part = d_y[rows, :]
            d_dec[...] += dot_tn(n3[flat, :], d_part)
            grad = dot_nt(d_part, w_dec[...])
            hat, r = norm(h2[flat, :])
            d_gains[2:3, :] += jnp.sum(grad * hat, axis=0, keepdims=True)
            d_end = norm_back(grad, gains[2:3, :], hat, r)
            d_low = d_end.astype(BF)
            dm[flat, :] = d_low
            d_in = jnp.zeros((tile, D), F32)
            for c in range(4):
                cols = slice(c * D, (c + 1) * D)
                d_act = dot_nt(d_low, w_down[cols, :])
                d_u = (d_act * upper[flat, cols]).astype(BF)
                du[flat, cols] = d_u
                d_in = d_in + dot_nt(d_u, w_up[:, cols])
            hat, r = norm(h1[flat, :])
            d_gains[1:2, :] += jnp.sum(d_in * hat, axis=0, keepdims=True)
            d_mid = d_end + norm_back(d_in, gains[1:2, :], hat, r)
            dh1[s, rows, :] = d_mid
            total_out[...] += dot_tn(attended[s, rows, :], d_mid.astype(BF))

    def copies(name, source, action):
        window_copies(
            here, layout.rows, layout.plans[0][0][name], source, keep, send, sems, action
        )

    for c in range(4):
        cols = slice(c * D, (c + 1) * D)
        put_flat(d_down, dot_tn(act[:, cols], dm[...]), 4 * c * D, 4)
    copies("down", d_down, "start")
    put_flat(d_out, total_out[...], 0, 4)
    copies("out", d_out, "start")
    for c in range(4):
        cols = slice(c * D, (c + 1) * D)
        put_flat(d_up, dot_tn(n2[...], du[:, cols]), 4 * c, 16)
    copies("up", d_up, "start")
    copies("down", d_down, "wait")
    copies("out", d_out, "wait")
    copies("up", d_up, "wait")


def mlp(me, h0, attended, w_out, w_up, w_down, w_dec, gains, dec_mt, targets_t, weight, levels, scale, layout):
    samples, nodes, _ = h0.shape
    rows = samples * nodes
    count = layout.plans[0][1]
    sent = layout.sizes[0] if layout.fast else 8
    vmem = pl.BlockSpec(memory_space=pltpu.VMEM)
    hbm = pl.BlockSpec(memory_space=pl.ANY)
    return pl.pallas_call(
        functools.partial(mlp_body, layout),
        out_shape=[
            shape((samples, nodes, D)),
            shape((D, 128)),
            shape((8, D)),
            shape((1, 512)),
            shape((layout.sizes[0], 128)),
            shape((sent, 128)),
        ],
        in_specs=[pl.BlockSpec(memory_space=pltpu.SMEM)] + [vmem] * 8 + [hbm] * 4,
        out_specs=[vmem] * 4 + [hbm] * 2,
        scratch_shapes=[
            pltpu.VMEM((rows, D), F32),
            pltpu.VMEM((rows, D), BF),
            pltpu.VMEM((rows, FF), F32),
            pltpu.VMEM((rows, FF), BF),
            pltpu.VMEM((rows, D), F32),
            pltpu.VMEM((rows, D), BF),
            pltpu.VMEM((2 * samples * CP, nodes), BF),
            pltpu.VMEM((2 * samples * CP, nodes), F32),
            pltpu.VMEM((rows, D), BF),
            pltpu.VMEM((rows, FF), BF),
            pltpu.VMEM((nodes, 128), BF),
            pltpu.VMEM((D, D), F32),
            pltpu.VMEM((4 * D, 128), F32),
            pltpu.VMEM((16 * D, 128), F32),
            pltpu.VMEM((4 * FF, 128), F32),
            pltpu.VMEM(w_up.shape, BF),
            pltpu.VMEM(w_down.shape, BF),
            pltpu.VMEM(dec_mt.shape, BF),
            pltpu.VMEM(targets_t.shape, F32),
            pltpu.SemaphoreType.DMA((count,)),
            pltpu.SemaphoreType.DMA((4,)),
        ],
        compiler_params=pltpu.CompilerParams(vmem_limit_bytes=60 << 20),
        cost_estimate=pl.CostEstimate(flops=16 << 30, bytes_accessed=24 << 20, transcendentals=0),
    )(me, h0, attended, w_out, w_dec, gains, weight, levels, scale, w_up, w_down, dec_mt, targets_t)


def attend_back_body(
    qkv, before, after, log_c, dh1, w_out,
    d_qkv, d_rims, d_before, d_after,
    pairs, do_both,
):
    samples, nodes, _ = dh1.shape
    halo = before.shape[1]
    for s in range(samples):
        gather_pairs(qkv, before, after, pairs, s)
        for i in range(nodes // 256):
            rows = slice(i * 256, (i + 1) * 256)
            da = dh1[s, rows, :].astype(BF)
            high, low = split(dot_nt(da, w_out[...]))
            for h in range(HEADS):
                lanes = slice(h * HEAD_DIM, (h + 1) * HEAD_DIM)
                do_both[rows, 2 * h * HEAD_DIM : (2 * h + 1) * HEAD_DIM] = high[:, lanes]
                do_both[rows, (2 * h + 1) * HEAD_DIM : (2 * h + 2) * HEAD_DIM] = low[:, lanes]
        for h in range(HEADS):
            lanes = slice(h * HEAD_DIM, (h + 1) * HEAD_DIM)
            vlanes = slice(D + h * HEAD_DIM, D + (h + 1) * HEAD_DIM)
            query = qkv[s, :, lanes]
            keys = pairs[:, lanes]
            values = pairs[:, vlanes]
            do = do_both[:, 2 * h * HEAD_DIM : (2 * h + 2) * HEAD_DIM]
            probs = attention_weights(keys, query, log_c)
            d_probs = dot_nt(jnp.concatenate([values, values], axis=1), do)
            centre = jnp.sum(probs * d_probs, 0, keepdims=True)
            high, low = split(probs * (d_probs - centre))
            dv2 = dot(probs.astype(BF), do)
            dv = dv2[:, :HEAD_DIM] + dv2[:, HEAD_DIM:]
            dk = (dot(high, query) + dot(low, query)) * SCALE
            dq_t = (dot_tn(keys, high) + dot_tn(keys, low)) * SCALE
            d_qkv[s, :, lanes] = dq_t.T.astype(BF)
            klanes = slice(D + h * HEAD_DIM, D + (h + 1) * HEAD_DIM)
            wide_lanes = slice(2 * D + h * HEAD_DIM, 2 * D + (h + 1) * HEAD_DIM)
            d_qkv[s, :, klanes] = dk[halo : halo + nodes].astype(BF)
            d_qkv[s, :, wide_lanes] = dv[halo : halo + nodes].astype(BF)
            for rim, first in ((0, halo), (1, nodes)):
                d_rims[s, rim, :, lanes] = dk[first : first + halo]
                d_rims[s, rim, :, vlanes] = dv[first : first + halo]
            d_before[s, :, lanes] = dk[:halo].astype(BF)
            d_before[s, :, vlanes] = dv[:halo].astype(BF)
            d_after[s, :, lanes] = dk[halo + nodes :].astype(BF)
            d_after[s, :, vlanes] = dv[halo + nodes :].astype(BF)


def attend_back(qkv, before, after, log_c, dh1, w_out):
    samples, nodes, _ = dh1.shape
    halo = before.shape[1]
    return kernel_call(
        attend_back_body,
        [
            shape((samples, nodes, 3 * D), BF),
            shape((samples, 2, halo, 2 * D)),
            shape((samples, halo, 2 * D), BF),
            shape((samples, halo, 2 * D), BF),
        ],
        [pltpu.VMEM((log_c.shape[0], 2 * D), BF), pltpu.VMEM((nodes, 2 * D), BF)],
        nbytes=20 << 20,
        flops=8 << 30,
    )(qkv, before, after, log_c, dh1, w_out)


def encode_back_body(
    layout,
    me, grid, w_enc, w_qkv, gains, enc_mt, h0, dh1, d_in, d_rims, from_lower, from_upper,
    d_small,
    keep, send,
    dqkv, n1, both, total_enc, d_gain, d_enc, d_qkv, small, sems,
):
    samples, nodes, _ = h0.shape
    here = me[0]

    def copies(name, source, action):
        window_copies(
            here, layout.rows, layout.plans[1][0][name], source, keep, send, sems, action
        )

    small[...] = d_small[...]
    pixels = grid.shape[2]
    halo = from_lower.shape[1]
    d_gain[...] = jnp.zeros(d_gain.shape, F32)
    total_enc[...] = jnp.zeros(total_enc.shape, F32)
    for s in range(samples):
        base = s * nodes
        dqkv[base : base + nodes, :] = d_in[s]
        low_rim = d_rims[s, 0] + from_lower[s].astype(F32)
        dqkv[base : base + halo, D:] = low_rim.astype(BF)
        high_rim = d_rims[s, 1] + from_upper[s].astype(F32)
        dqkv[base + nodes - halo : base + nodes, D:] = high_rim.astype(BF)
        for i in range(nodes // 256):
            rows = slice(i * 256, (i + 1) * 256)
            flat = slice(base + i * 256, base + (i + 1) * 256)
            hat, r = norm(h0[s, rows, :])
            n1[flat, :] = (hat * gains[0:1, :]).astype(BF)
            grad = dot_nt(dqkv[flat, :], w_qkv[...])
            d_gain[0:1, :] += jnp.sum(grad * hat, axis=0, keepdims=True)
            d_start = dh1[s, rows, :] + norm_back(grad, gains[0:1, :], hat, r)
            high, low = split(d_start * 0.25)
            both[rows, 0:D] = high
            both[rows, D:] = low

        @pl.loop(0, pixels // 512, unroll=True)
        def _(i):
            rows = pl.ds(pl.multiple_of(i * 512, 512), 512)
            x_t = grid[s, :, rows]
            pre = dot_tn(x_t, w_enc[...])
            spread2 = dot(enc_mt[rows, :], both[...])
            spread = spread2[:, 0:D] + spread2[:, D:]
            d_pre = (spread * slope(pre, sigmoid(pre))).astype(BF)
            total_enc[...] += dot(x_t, d_pre)

    for c in range(3):
        put_flat(d_qkv, dot_tn(n1[...], dqkv[:, c * D : (c + 1) * D]), 4 * c, 12)
    copies("qkv", d_qkv, "start")
    put_flat(d_enc, total_enc[...], 0, 4)
    for lane in range(D // 128):
        row = 4 * C_OUT + lane
        small[row : row + 1, :] = d_gain[0:1, lane * 128 : lane * 128 + 128]
    for action in ("start", "wait"):
        copies("enc", d_enc, action)
        copies("small", small, action)
        if action == "wait":
            copies("qkv", d_qkv, action)


def encode_back(me, grid, w_enc, w_qkv, gains, enc_mt, h0, dh1, d_in, d_rims, from_lower, from_upper,
                d_small, layout):
    samples, nodes, _ = h0.shape
    rows = samples * nodes
    vmem = pl.BlockSpec(memory_space=pltpu.VMEM)
    hbm = pl.BlockSpec(memory_space=pl.ANY)
    return pl.pallas_call(
        functools.partial(encode_back_body, layout),
        out_shape=[shape((layout.sizes[1], 128)), shape((layout.sizes[1] if layout.fast else 8, 128))],
        in_specs=[pl.BlockSpec(memory_space=pltpu.SMEM)] + [vmem] * 12,
        out_specs=[hbm, hbm],
        scratch_shapes=[
            pltpu.VMEM((rows, 3 * D), BF),
            pltpu.VMEM((rows, D), BF),
            pltpu.VMEM((nodes, 2 * D), BF),
            pltpu.VMEM((C_IN, D), F32),
            pltpu.VMEM((8, D), F32),
            pltpu.VMEM((4 * C_IN, 128), F32),
            pltpu.VMEM((12 * D, 128), F32),
            pltpu.VMEM(d_small.shape, F32),
            pltpu.SemaphoreType.DMA((layout.plans[1][1],)),
        ],
        compiler_params=pltpu.CompilerParams(vmem_limit_bytes=58 << 20),
        cost_estimate=pl.CostEstimate(flops=12 << 30, bytes_accessed=24 << 20, transcendentals=0),
    )(me, grid, w_enc, w_qkv, gains, enc_mt, h0, dh1, d_in, d_rims, from_lower, from_upper, d_small)


def ring(axis, distance):
    count = lax.axis_size(axis)
    return [(i, (i + distance) % count) for i in range(count)]


def window_plan(shard, count):
    starts = [(LEAD * D + d * shard) // (16 * D) * 16 for d in range(count)]
    ends = [-(-(LEAD * D + (d + 1) * shard) // D) for d in range(count)]
    rows = max(-(-(e - s + 1) // 16) * 16 for s, e in zip(starts, ends))
    return starts, rows


def per_device(
    grid, targets, area, sigma_weight, level_weight, valid, enc_index, dec_index, neighbours,
    params, first_moment, second_moment, average,
):
    shard = params.shape[0]
    devices = lax.axis_size(AXES)
    me = lax.axis_index(AXES)
    nodes = neighbours.shape[0]
    halo = nodes // 16
    fast = (lax.axis_size("patch"), lax.axis_size("dp")) == (8, 4)
    layout = Layout(shard, devices, fast)
    starts, win = layout.starts, layout.win
    begin = LEAD * D + me * shard
    shift = begin - begin // (16 * D) * (16 * D)
    place = me.astype(jnp.int32).reshape(1)

    count = jnp.sum(valid)
    digits = jnp.stack([count // 128, count % 128]).astype(BF)
    payload = lax.dynamic_update_slice(jnp.zeros((win * D,), BF), params.astype(BF), (shift,))
    payload = lax.dynamic_update_slice(payload, digits, ((win - 1) * D,)).reshape(win, D)
    weight = valid.astype(F32) * area[None, :] * sigma_weight[:, None]
    levels = jnp.pad(level_weight, (0, CP - C_OUT)).reshape(CP, 1)
    pixels = dec_index.shape[0]
    first_work = lambda: count_encoder(enc_index, pixels)
    positions = me * shard + lax.iota(jnp.int32, shard)
    bounds = segment_bounds() + [(-1, -1)]
    lower = jnp.array([x for x, _ in bounds], jnp.int32)[:, None]
    upper = jnp.array([x for _, x in bounds], jnp.int32)[:, None]
    member = ((positions >= lower) & (positions < upper)).astype(F32)
    second_work = lambda: (count_rest(dec_index, neighbours, targets), weight, levels, member)
    if fast:
        pieces, plan, first_done, second_done = gather_windows(payload, first_work, second_work)
        place_of = place_by_xor
    else:
        everything = lax.all_gather(payload, AXES, axis=0, tiled=False)
        pieces = [everything.reshape(devices * win, D)]
        plan = [(0, d * win, d, 0, win) for d in range(devices)]
        place_of = lambda here, d: d
        first_done, second_done = first_work(), second_work()
    enc_m, enc_mt = first_done
    (dec_mt, log_c, targets_t), weight, levels, member = second_done
    grid = jnp.swapaxes(grid, 1, 2)

    w_enc, w_qkv, head = unpack(
        place, pieces, plan, ("enc", "qkv", "gain"), place_of, devices, win, starts
    )
    h0, qkv = encode(grid, w_enc, enc_m, w_qkv, head)
    before = lax.ppermute(qkv[:, nodes - halo :, D:], "patch", ring("patch", 1))
    after = lax.ppermute(qkv[:, :halo, D:], "patch", ring("patch", -1))
    w_out, w_up, w_down, tail, counted = unpack(
        place, pieces, plan, ("out", "up", "down", "tail", "count"), place_of, devices, win, starts
    )
    w_dec = jnp.pad(tail[:C_OUT].reshape(D, C_OUT), ((0, 0), (0, 128 - C_OUT)))
    gains = jnp.pad(tail[C_OUT : C_OUT + 3].astype(F32), ((0, 5), (0, 0)))
    count_total = counted[0, 0]
    attended = attend(qkv, before, after, log_c)
    scale = 2.0 / counted * (1.0 / 3.0)
    dh1, d_dec, d_gains, loss_rows, keep, send = mlp(
        place, h0, attended, w_out, w_up, w_down, w_dec, gains, dec_mt, targets_t, weight, levels,
        scale, layout,
    )
    if fast:
        summed = keep + permute(send, 1)
    d_qkv, d_rims, d_before, d_after = attend_back(qkv, before, after, log_c, dh1, w_out)
    from_upper = lax.ppermute(d_before, "patch", ring("patch", -1))
    from_lower = lax.ppermute(d_after, "patch", ring("patch", 1))
    d_small = jnp.concatenate(
        [
            d_dec[:, :C_OUT].reshape(4 * C_OUT, 128),
            jnp.zeros((4, 128), F32),
            d_gains[1:3].reshape(8, 128),
            jnp.zeros((4 * (ROWS_ALL - ROW_END), 128), F32),
        ]
    )
    if fast:
        summed, d_qkv, from_upper, from_lower, d_small = lax.optimization_barrier(
            (summed, d_qkv, from_upper, from_lower, d_small)
        )
        half = layout.rows // 2
        early = summed.reshape(3, 2, 2, layout.rows, 128)
        got = permute(low(early[:, :, 1, :half]), 2), permute(low(early[:, 1, :, half:]), 4)
    second = encode_back(
        place, grid, w_enc, w_qkv, gains, enc_mt, h0, dh1, d_qkv, d_rims, from_lower, from_upper,
        d_small, layout,
    )
    if fast:
        second, got = lax.optimization_barrier((second, got))
        grad_window = sum_rest(early, got, second, layout, me)
    else:
        grad_window = sum_flat(keep, second[0], layout)
    grad = lax.dynamic_slice(grad_window.reshape(-1), (shift,), (shard,))

    new_first = BETA_ONE * first_moment + (1.0 - BETA_ONE) * grad
    new_second = BETA_TWO * second_moment + (1.0 - BETA_TWO) * grad * grad
    update = (
        new_first
        / (1.0 - BETA_ONE**STEP)
        / (jnp.sqrt(new_second / (1.0 - BETA_TWO**STEP)) + LAMB_EPS)
        + DECAY * params
    )
    both = jnp.stack([params * params, update * update])
    sums = jnp.sum(member[None] * both[:, None, :], axis=2)
    loss_at = (jnp.arange(2)[:, None] == 0) & (jnp.arange(8)[None, :] == 7)
    sums = jnp.where(loss_at, jnp.sum(loss_rows), sums)
    totals = sum_everywhere(sums, fast)
    norms = jnp.sqrt(totals[:, :7])
    step_ratio = jnp.sum(member[:7] * (norms[0] / norms[1])[:, None], axis=0)
    new_params = params - RATE * step_ratio * update
    new_average = EMA_KEEP * average + (1.0 - EMA_KEEP) * new_params
    return (
        jnp.stack([totals[0, 7], count_total]),
        norms,
        new_params,
        new_first,
        new_second,
        new_average,
    )


def solution(mesh):
    flat = P(AXES)
    in_specs = (
        P("dp", "patch", None),
        P("dp", "patch", None),
        P("patch"),
        P("dp"),
        P(),
        P("dp", "patch"),
        P("patch", None),
        P("patch", None),
        P("patch", None),
        flat,
        flat,
        flat,
        flat,
    )
    out_specs = (P(), P(), flat, flat, flat, flat)
    return jax.shard_map(
        per_device, mesh=mesh, in_specs=in_specs, out_specs=out_specs, check_vma=False
    )
```

```python
import functools
import math

import jax
import jax.numpy as jnp
from jax import lax
from jax.experimental import pallas as pl
from jax.experimental.pallas import tpu as pltpu
from jax.sharding import PartitionSpec as P

D = 512
HEADS = 4
HEAD_DIM = 128
FF = 2048
C_OUT = 84
C_IN = 264
STEP = 10
EPS_NORM = 1e-05
BETA_ONE = 0.9
BETA_TWO = 0.999
LAMB_EPS = 1e-06
DECAY = 0.01
RATE = 0.2
EMA_KEEP = 0.8
BF = jnp.bfloat16
F32 = jnp.float32
SCALE = HEAD_DIM ** (-0.5)
LOG2E = 1.4426950408889634
ABSENT = -1e30
CP = 96
AXES = ("patch", "dp")

LEAD = 8
ROW_ENC = LEAD
ROW_QKV = ROW_ENC + C_IN
ROW_OUT = ROW_QKV + 3 * D
ROW_UP = ROW_OUT + D
ROW_DOWN = ROW_UP + 4 * D
ROW_DEC = ROW_DOWN + FF
ROW_GAIN = ROW_DEC + C_OUT
ROW_END = ROW_GAIN + 3
ROWS_ALL = -(-ROW_END // 16) * 16


def matrix_shapes():
    return [(C_IN, D), (D, 3 * D), (D, D), (D, FF), (FF, D), (D, C_OUT), (3, D)]


def segment_bounds():
    bounds = []
    offset = 0
    for row_count, col_count in matrix_shapes():
        bounds.append((offset, offset + row_count * col_count))
        offset += row_count * col_count
    return bounds


NPARAM_USED = segment_bounds()[-1][1]


def dot(a, b):
    return lax.dot_general(a, b, (((1,), (0,)), ((), ())), preferred_element_type=F32)


def dot_nt(a, b):
    return lax.dot_general(a, b, (((1,), (1,)), ((), ())), preferred_element_type=F32)


def dot_tn(a, b):
    return lax.dot_general(a, b, (((0,), (0,)), ((), ())), preferred_element_type=F32)


def split(x):
    high = x.astype(BF)
    return high, (x - high.astype(F32)).astype(BF)


def sigmoid(x):
    return 0.5 * jnp.tanh(0.5 * x) + 0.5


def slope(x, s):
    return s * (1.0 + x * (1.0 - s))


def norm(x):
    c = x - jnp.mean(x, -1, keepdims=True)
    r = lax.rsqrt(jnp.mean(c * c, -1, keepdims=True) + EPS_NORM)
    return c * r, r


def norm_back(grad, gain, hat, r):
    g = grad * gain
    return r * (
        g
        - jnp.mean(g, -1, keepdims=True)
        - hat * jnp.mean(g * hat, -1, keepdims=True)
    )


def put_flat(ref, value, first, period):
    for lane in range(D // 128):
        ref[pl.ds(first + lane, value.shape[0], stride=period), :] = value[
            :, lane * 128 : lane * 128 + 128
        ]


def kernel_call(body, out_shape, scratch=(), flops=0, nbytes=0):
    return pl.pallas_call(
        body,
        out_shape=out_shape,
        scratch_shapes=list(scratch),
        compiler_params=pltpu.CompilerParams(vmem_limit_bytes=58 << 20),
        cost_estimate=pl.CostEstimate(flops=flops, bytes_accessed=nbytes, transcendentals=0),
    )


def shape(dims, dtype=F32):
    return jax.ShapeDtypeStruct(tuple(dims), dtype)


def count_rows(index_t, base, rows, cols):
    ids = lax.broadcasted_iota(jnp.int32, (rows, cols), 0) + base
    total = jnp.zeros((rows, cols), F32)
    for k in range(index_t.shape[0]):
        total = total + jnp.where(index_t[k : k + 1, :] == ids, 1.0, 0.0)
    return total


def count_encoder_body(enc, enc_t, enc_m, enc_mt):
    nodes, pixels = enc_m.shape

    @pl.loop(0, nodes // 32)
    def _(i):
        rows = pl.ds(pl.multiple_of(i * 32, 32), 32)
        index = enc[rows, :]
        ids = lax.broadcasted_iota(jnp.int32, (32, pixels), 1)
        total = jnp.zeros((32, pixels), F32)
        for k in range(index.shape[1]):
            total = total + jnp.where(index[:, k : k + 1] == ids, 1.0, 0.0)
        enc_m[rows, :] = total.astype(BF)

    @pl.loop(0, pixels // 64)
    def _(i):
        rows = pl.ds(pl.multiple_of(i * 64, 64), 64)
        enc_mt[rows, :] = count_rows(enc_t, i * 64, 64, nodes).astype(BF)


def count_rest_body(dec_t, nbr_t, targets, dec_mt, log_c, targets_t):
    nodes, pixels = dec_mt.shape

    @pl.loop(0, nodes // 32)
    def _(i):
        rows = pl.ds(pl.multiple_of(i * 32, 32), 32)
        dec_mt[rows, :] = count_rows(dec_t, i * 32, 32, pixels).astype(BF)

    @pl.loop(0, log_c.shape[0] // 64)
    def _(i):
        rows = pl.ds(pl.multiple_of(i * 64, 64), 64)
        total = count_rows(nbr_t, i * 64, 64, nodes)
        log_c[rows, :] = jnp.where(total > 0.0, jnp.log2(jnp.maximum(total, 1.0)), ABSENT)

    targets_t[...] = jnp.zeros(targets_t.shape, F32)
    for s in range(targets.shape[0]):

        @pl.loop(0, pixels // 256)
        def _(i):
            part = pl.ds(pl.multiple_of(i * 256, 256), 256)
            targets_t[s, 0:C_OUT, part] = targets[s, part, :].T


def count_encoder(enc_index, pixels):
    nodes = enc_index.shape[0]
    return kernel_call(
        count_encoder_body,
        [shape((nodes, pixels), BF), shape((pixels, nodes), BF)],
        nbytes=5 << 20,
        flops=1 << 29,
    )(enc_index, enc_index.T)


def count_rest(dec_index, neighbours, targets):
    nodes, pixels = neighbours.shape[0], dec_index.shape[0]
    ext = nodes + 2 * (nodes // 16)
    return kernel_call(
        count_rest_body,
        [shape((nodes, pixels), BF), shape((ext, nodes)), shape((targets.shape[0], CP, pixels))],
        nbytes=8 << 20,
        flops=1 << 29,
    )(dec_index.T, neighbours.T, targets)


def tile_sources(starts, rows):
    return [
        [(d, tile * 16 - s) for d, s in enumerate(starts) if s <= tile * 16 < s + rows]
        for tile in range(ROWS_ALL // 16)
    ]


def assemble(read, window_rows, sources, first_row, rows, put):
    tile, last = first_row // 16, (first_row + rows) // 16
    while tile < last:
        source = sources[tile]
        if len(source) == 1:
            count = 1
            while (
                tile + count < last
                and len(sources[tile + count]) == 1
                and sources[tile + count][0][0] == source[0][0]
                and count < 8
            ):
                count += 1
            d, off = source[0]
            value = read(d, off, 16 * count)
        else:
            count = 1
            value = None
            for d, off in source:
                part = read(d, off, 16).astype(F32)
                if off + 16 == window_rows:
                    part = jnp.where(
                        lax.broadcasted_iota(jnp.int32, part.shape, 0) < 15, part, 0.0
                    )
                value = part if value is None else value + part
            value = value.astype(BF)
        put(tile * 16 - first_row, value)
        tile += count


def wide(stage, ref, period):
    for lane in range(D // 128):
        for c in range(period):
            lanes = slice(c * D + lane * 128, c * D + lane * 128 + 128)
            ref[:, lanes] = stage[lane, pl.ds(c, ref.shape[0], stride=period), :].astype(BF)


def unpack_body(plan, parts, sources, place_of, owner_of, count, *refs):
    me, pieces, refs = refs[0], refs[1 : count + 1], refs[count + 1 :]
    outs, (windows, stage, sems) = refs[: len(parts)], refs[len(parts) :]
    here = me[0]
    first = min(PARTS[p][0] for p in parts if p != "count")
    last = max(PARTS[p][0] + PARTS[p][1] for p in parts if p not in ("count", "gains"))
    used = {d for source in sources[first // 16 : last // 16] for d, _ in source}
    if "gains" in parts:
        used |= {d for d, _ in sources[ROW_GAIN // 16]}
    low_used, high_used = min(used), max(used - {max(used)})
    copies = []
    for k, (piece, at, slot, to, rows) in enumerate(plan):
        copy = pltpu.make_async_copy(
            pieces[piece].at[pl.ds(at, rows), :], windows.at[slot, pl.ds(to, rows), :], sems.at[k]
        )
        owner = owner_of(here, slot)
        needed = (owner >= low_used) & (owner <= high_used) | (owner == max(used))
        if "count" in parts:
            copy.start()
        else:
            pl.when(needed)(copy.start)
        copies.append((copy, needed))
    for copy, needed in copies:
        if "count" in parts:
            copy.wait()
        else:
            pl.when(needed)(copy.wait)
    window_rows = windows.shape[1]

    def read(d, off, rows):
        return windows[place_of(here, d), off : off + rows, :]

    for part, ref in zip(parts, outs):
        if part == "count":
            total = jnp.sum(windows[:, window_rows - 16 :, 0:128].astype(F32), axis=0)[15:16, :]
            lanes = lax.broadcasted_iota(jnp.int32, (1, 128), 1)
            digits = jnp.where(lanes == 0, 128.0, jnp.where(lanes == 1, 1.0, 0.0)) * total
            ref[...] = jnp.sum(digits, axis=1, keepdims=True) + jnp.zeros((8, 128), F32)
            continue
        first, rows, period, _ = PARTS[part]

        def direct(off, value):
            ref[off : off + value.shape[0], :] = value

        def staged(off, value):
            wide_value = value.astype(F32)
            for lane in range(D // 128):
                stage[lane, off : off + value.shape[0], :] = wide_value[
                    :, lane * 128 : lane * 128 + 128
                ]

        if part == "gains":
            assemble(read, window_rows, sources, first, rows, staged)
            row = ROW_GAIN - first
            for lane in range(D // 128):
                ref[:, lane * 128 : lane * 128 + 128] = stage[lane, row : row + 8, :]
        elif period == 1:
            assemble(read, window_rows, sources, first, rows, direct)
        else:
            assemble(read, window_rows, sources, first, rows, staged)
            if part == "enc":
                for lane in range(D // 128):
                    lanes = slice(lane * 128, lane * 128 + 128)
                    ref[:, lanes] = stage[lane, LEAD:ROW_QKV, :].astype(BF)
            elif part == "dec":
                for lane in range(D // 128):
                    lanes = slice(lane * 128, lane * 128 + 128)
                    row = ROW_DEC - first
                    ref[:, lanes] = stage[lane, row : row + C_OUT, :].astype(BF)
            else:
                wide(stage, ref, period)


PARTS = {
    "enc": (0, ROW_QKV, 0, (C_IN, D)),
    "qkv": (ROW_QKV, 3 * D, 3, (D, 3 * D)),
    "out": (ROW_OUT, D, 1, (D, D)),
    "up": (ROW_UP, 4 * D, 4, (D, FF)),
    "down": (ROW_DOWN, FF, 1, (FF, D)),
    "dec": (ROW_DEC // 16 * 16, -(-ROW_GAIN // 16) * 16 - ROW_DEC // 16 * 16, 0, (C_OUT, D)),
    "gains": (ROW_GAIN // 16 * 16, 16, 0, (8, D)),
}


def unpack(me, pieces, plan, parts, place_of, slots, rows, starts):
    sources = tile_sources(starts, rows)
    outs = [
        shape((8, 128)) if p == "count" else shape(PARTS[p][3], F32 if p == "gains" else BF)
        for p in parts
    ]
    return pl.pallas_call(
        functools.partial(unpack_body, plan, parts, sources, place_of, place_of, len(pieces)),
        out_shape=outs,
        in_specs=[pl.BlockSpec(memory_space=pltpu.SMEM)]
        + [pl.BlockSpec(memory_space=pl.ANY)] * len(pieces),
        scratch_shapes=[
            pltpu.VMEM((slots, rows, D), BF),
            pltpu.VMEM((D // 128, 4 * D, 128), F32),
            pltpu.SemaphoreType.DMA((len(plan),)),
        ],
        compiler_params=pltpu.CompilerParams(vmem_limit_bytes=58 << 20),
        cost_estimate=pl.CostEstimate(
            flops=0, bytes_accessed=slots * rows * D * 4, transcendentals=0
        ),
    )(me, *pieces)


def permute(x, mask):
    count = lax.axis_size(AXES)
    return lax.ppermute(x, AXES, [(d, d ^ mask) for d in range(count)])


def place_by_xor(here, d):
    return jnp.bitwise_xor(here, d)


def gather_windows(window, first_work, second_work, second_inputs, third_work, third_inputs):
    rows = window.shape[0]
    half = rows // 2
    pieces, plan = [], []

    def add(piece, near, parts):
        for part, flip in ((piece, 0), (permute(piece, 1), 1)):
            for at, slot, to, size in parts:
                plan.append((len(pieces), at, slot ^ near ^ flip, to, size))
            pieces.append(part)

    planes = (8, 16, 24)
    others = [permute(window, m) for m in planes]
    by_x, by_y = permute(window, 2), permute(window, 4)
    first_done = first_work()
    others, by_x, by_y, first_done, second_inputs = lax.optimization_barrier(
        (jnp.concatenate(others), by_x, by_y, first_done, second_inputs)
    )
    others_x, others_y = permute(others, 2), permute(others, 4)
    second_done = second_work(*second_inputs)
    others_x, others_y, second_done, third_inputs = lax.optimization_barrier(
        (others_x, others_y, second_done, third_inputs)
    )

    def halves(near_part, far_part, first):
        far = [far_part[i * rows + first : i * rows + first + half] for i in range(3)]
        return jnp.concatenate([near_part[first : first + half]] + far)

    across_a = permute(halves(by_y, others_y, 0), 2)
    across_b = permute(halves(by_x, others_x, half), 4)
    across_a, across_b, third_done = lax.optimization_barrier(
        (across_a, across_b, third_work(*third_inputs))
    )
    whole = [(0, 0, 0, rows)]
    stacked = [(i * rows, slot, 0, rows) for i, slot in enumerate(planes)]
    add(window, 0, whole)
    add(by_x, 2, whole)
    add(by_y, 4, whole)
    add(others, 0, stacked)
    add(others_x, 2, stacked)
    add(others_y, 4, stacked)
    add(across_a, 6, [(i * half, slot, 0, half) for i, slot in enumerate((0,) + planes)])
    add(across_b, 6, [(i * half, slot, half, half) for i, slot in enumerate((0,) + planes)])
    return pieces, plan, first_done, second_done, third_done


def encode_body(grid, w_enc, enc_m, w_qkv, gains, h0, qkv, leading, last, high, low):
    samples, pixels = grid.shape[0], grid.shape[2]
    nodes, halo = h0.shape[1], last.shape[1]
    for s in range(samples):

        @pl.loop(0, pixels // 512, unroll=True)
        def _(i):
            rows = pl.ds(pl.multiple_of(i * 512, 512), 512)
            pre = dot_tn(grid[s, :, rows], w_enc[...])
            value = pre * sigmoid(pre)
            high[rows, :], low[rows, :] = split(value)

        @pl.loop(0, nodes // 512, unroll=True)
        def _(i):
            rows = pl.ds(pl.multiple_of(i * 512, 512), 512)
            counts = enc_m[rows, :]
            start = (dot(counts, high[...]) + dot(counts, low[...])) * 0.25
            h0[s, rows, :] = start
            hat, _ = norm(start)
            n1 = (hat * gains[0:1, :]).astype(BF)
            qkv[s, rows, :] = dot(n1, w_qkv[...]).astype(BF)

        leading[s] = qkv[s, 0:halo, D:]
        last[s] = qkv[s, nodes - halo :, D:]


def encode(grid, w_enc, enc_m, w_qkv, gains):
    samples, pixels = grid.shape[0], grid.shape[2]
    nodes = enc_m.shape[0]
    return kernel_call(
        encode_body,
        [shape((samples, nodes, D)), shape((samples, nodes, 3 * D), BF)]
        + [shape((samples, nodes // 16, 2 * D), BF)] * 2,
        [pltpu.VMEM((pixels, D), BF), pltpu.VMEM((pixels, D), BF)],
        nbytes=12 << 20,
        flops=8 << 30,
    )(grid, w_enc, enc_m, w_qkv, gains)


def gather_pairs(qkv, before, after, pairs, s):
    halo, nodes = before.shape[1], qkv.shape[1]
    pairs[0:halo, :] = before[s]
    pairs[halo : halo + nodes, :] = qkv[s, :, D:]
    pairs[halo + nodes :, :] = after[s]


def attention_weights(keys, query, log_c):
    x = dot_nt(keys, query) * (SCALE * LOG2E) + log_c[...]
    e = jnp.exp2(x - jnp.max(x, 0, keepdims=True))
    return e * (1.0 / jnp.sum(e, 0, keepdims=True))


def attend_body(qkv, before, after, log_c, out, pairs):
    for s in range(qkv.shape[0]):
        gather_pairs(qkv, before, after, pairs, s)
        for h in range(HEADS):
            lanes = slice(h * HEAD_DIM, (h + 1) * HEAD_DIM)
            keys = pairs[:, lanes]
            values = pairs[:, D + h * HEAD_DIM : D + (h + 1) * HEAD_DIM]
            probs = attention_weights(keys, qkv[s, :, lanes], log_c)
            out_t = dot_tn(values, probs.astype(BF))
            out[s, :, lanes] = out_t.T.astype(BF)


def attend(qkv, before, after, log_c):
    samples, nodes = qkv.shape[:2]
    return kernel_call(
        attend_body,
        shape((samples, nodes, D), BF),
        [pltpu.VMEM((log_c.shape[0], 2 * D), BF)],
        nbytes=8 << 20,
        flops=2 << 30,
    )(qkv, before, after, log_c)


class Layout:
    def __init__(self, shard, devices, fast):
        self.devices = devices
        self.starts, self.win = window_plan(shard, devices)
        self.begins = [(LEAD * D + d * shard) // 1024 * 8 for d in range(devices)]
        self.ends = [-(-(LEAD * D + (d + 1) * shard) // 1024) * 8 for d in range(devices)]
        self.rows = -(-max(e - b for b, e in zip(self.begins, self.ends)) // 32) * 32
        self.small = 4 * (ROWS_ALL - ROW_DEC)
        first = (("out", ROW_OUT, 4 * D), ("up", ROW_UP, 16 * D), ("down", ROW_DOWN, 4 * FF))
        second = (("enc", ROW_ENC, 4 * C_IN), ("qkv", ROW_QKV, 12 * D), ("small", ROW_DEC, self.small))
        self.fast = fast
        if fast:
            self.apart = 4 * ROW_OUT - self.begins[8]
            extra = -(-(self.apart + self.small) // 32) * 32
            self.sizes = (12 * self.rows, 4 * self.rows + extra)
        else:
            self.sizes = (sum(x[2] for x in first), sum(x[2] for x in second))
        self.plans = self.make(first, 1), self.make(second, 0)

    def make(self, arrays, plane):
        plans, k, at = {}, 0, 0
        for name, row, size in arrays:
            plans[name] = []
            if not self.fast:
                plans[name].append((k, None, at, 0, size))
                k, at = k + 1, at + size
                continue
            if name == "small":
                plans[name].append((k, "both", 4 * self.rows + self.apart, 0, size))
                k += 2
                continue
            for d, (lower, upper) in enumerate(zip(self.begins, self.ends)):
                low, high = max(lower, 4 * row), min(upper, 4 * (row + size // 4))
                if low >= high:
                    continue
                if d == 8 and plane == 0:
                    to = 4 * self.rows + low - lower
                    plans[name].append((k, "both", to, low - 4 * row, high - low))
                    k += 2
                else:
                    place = (d // 8 - plane) * 4 * self.rows + low - lower
                    plans[name].append((k, d % 8, place, low - 4 * row, high - low))
                    k += 1
        return plans, k


def window_copies(here, rows_of_slot, blocks, source, keep, send, sems, action):
    for k, near, to, at, rows in blocks:

        def copy(target, first, sem):
            getattr(
                pltpu.make_async_copy(
                    source.at[pl.ds(at, rows), :], target.at[pl.ds(first, rows), :], sems.at[sem]
                ),
                action,
            )()

        if near is None:
            copy(keep, to, k)
        elif near == "both":
            copy(keep, to, k)
            copy(send, to, k + 1)
        else:
            slot = jnp.bitwise_and(jnp.bitwise_xor(here, near), 7)
            first = pl.multiple_of(lax.shift_right_logical(slot, 1) * rows_of_slot + to, 8)
            for target, side in ((keep, 0), (send, 1)):

                @pl.when(jnp.bitwise_and(slot, 1) == side)
                def _():
                    copy(target, first, k)


def sum_flat(first, second, layout):
    flat = jnp.concatenate(
        [
            jnp.zeros((4 * LEAD, 128), F32),
            second[: 4 * (ROW_OUT - LEAD)],
            first,
            second[4 * (ROW_OUT - LEAD) :],
            jnp.zeros((max(0, layout.begins[-1] + layout.rows - 4 * ROWS_ALL), 128), F32),
        ]
    )
    windows = jnp.concatenate([flat[b : b + layout.rows] for b in layout.begins])
    return lax.psum_scatter(windows, AXES, scatter_dimension=0, tiled=True)


def low(x):
    return x.astype(BF)


def packed(blocks, extra):
    return low(jnp.concatenate([blocks.reshape(-1, 128), extra]))


def add_packed(flat, blocks, extra):
    flat = flat.astype(F32)
    count = flat.shape[0] - extra.shape[0]
    return blocks + flat[:count].reshape(blocks.shape), extra + flat[count:]


def across_planes(x, allowed, k):
    pairs = [(d, d ^ (8 * k)) for d in range(32) if allowed((d ^ (8 * k)) // 8, d % 8)]
    return lax.ppermute(x, AXES, pairs)


def add_halves(layout, keep, other, got, sends):
    half = layout.rows // 2
    keep, other = keep.reshape(24, half, 128), other.reshape(24, half, 128)
    steps = []
    for out, (picks, source, _) in enumerate(sends):
        for i, pick in enumerate(picks):
            steps.append((out, i, pick, source))

    def body(*refs):
        keep_ref, other_ref = refs[:2]
        gots, outs = refs[2 : 2 + len(got)], refs[2 + len(got) : 2 + len(got) + len(sends)]
        slots, sems = refs[-2:]
        copies = []
        for k, (out, i, pick, source) in enumerate(steps):
            pair = [
                pltpu.make_async_copy(ref.at[pick], slots.at[2 * k + j], sems.at[2 * k + j])
                for j, ref in enumerate((keep_ref, other_ref))
            ]
            for copy in pair:
                copy.start()
            copies.append(pair)
        for k, (out, i, pick, source) in enumerate(steps):
            for copy in copies[k]:
                copy.wait()
            value = slots[2 * k] + slots[2 * k + 1]
            if source is not None:
                which, at = source[0], source[1][i]
                value = value + gots[which][at].astype(F32)
            outs[out][i] = value.astype(outs[out].dtype)

    hbm = pl.BlockSpec(memory_space=pl.ANY)
    vmem = pl.BlockSpec(memory_space=pltpu.VMEM)
    return pl.pallas_call(
        body,
        out_shape=[shape((len(p), half, 128), BF if sent else F32) for p, _, sent in sends],
        in_specs=[hbm, hbm] + [vmem] * len(got),
        out_specs=[vmem] * len(sends),
        scratch_shapes=[
            pltpu.VMEM((2 * len(steps), half, 128), F32),
            pltpu.SemaphoreType.DMA((2 * len(steps),)),
        ],
        compiler_params=pltpu.CompilerParams(vmem_limit_bytes=58 << 20),
        cost_estimate=pl.CostEstimate(
            flops=0, bytes_accessed=len(steps) * half * 1536, transcendentals=0
        ),
    )(keep, other, *got)


def first_send(keep, other, layout):
    to_x = [(p * 4 + y * 2 + 1) * 2 for p in range(3) for y in range(2)]
    to_y = [(p * 4 + 2 + x) * 2 + 1 for p in range(3) for x in range(2)]
    return add_halves(layout, keep, other, (), [(to_x, None, True), (to_y, None, True)])


def second_send(keep, other, got_a, got_b, layout):
    sends = []
    for which, (lower, stride) in enumerate(((0, 2), (1, 1))):
        for far in range(2):
            picks = [(p * 4 + far * stride) * 2 + lower for p in range(3)]
            sends.append((picks, (which, [p * 2 + far for p in range(3)]), far == 1))
    return add_halves(layout, keep, other, (got_a, got_b), sends)


def sum_rest(kept, got, second, layout, me):
    rows = layout.rows
    half = rows // 2
    near, mine = me % 8, me // 8

    other = permute(second[1], 1)
    kept_a, kept_b = kept[0] + got[0].astype(F32), kept[1] + got[1].astype(F32)

    def plane(k):
        at = jnp.maximum(jnp.bitwise_xor(mine, k) - 1, 0)
        return jnp.concatenate(
            [lax.dynamic_index_in_dim(x, at, 0, False) for x in (kept_a, kept_b)]
        )

    ups = [across_planes(low(plane(k)), lambda p, q: p > 0, k) for k in (1, 2, 3)]

    late = second[0] + other
    apart = late[4 * rows :]
    late = late[: 4 * rows].reshape(2, 2, rows, 128)
    cut = apart.shape[0] // 2
    late_a, apart_a = add_packed(
        permute(packed(late[:, 1, :half], apart[:cut]), 2), late[:, 0, :half], apart[:cut]
    )
    late_b, apart_b = add_packed(
        permute(packed(late[1, :, half:], apart[cut:]), 4), late[0, :, half:], apart[cut:]
    )
    late_a, apart_a = add_packed(permute(packed(late_a[1], apart_a), 4), late_a[0], apart_a)
    late_b, apart_b = add_packed(permute(packed(late_b[1], apart_b), 2), late_b[0], apart_b)
    apart = jnp.concatenate([apart_a, apart_b])
    lead, small = layout.apart, 4 * ROW_DEC - layout.begins[31]
    size = min(layout.small, rows - small)
    one = jnp.concatenate([apart[:lead], jnp.zeros((rows - lead, 128), F32)])
    three = jnp.concatenate(
        [
            jnp.zeros((small, 128), F32),
            apart[lead : lead + size],
            jnp.zeros((rows - small - size, 128), F32),
        ]
    )
    parts = jnp.stack([jnp.concatenate([late_a, late_b]), one, one, three])

    def part(k):
        return lax.dynamic_index_in_dim(parts, jnp.bitwise_xor(mine, k), 0, False)

    lower = part(0)
    for k in (1, 2, 3):
        got = across_planes(
            low(part(k)), lambda p, q: p == 0 or (p, q) == (1, 0) or (p, q) == (3, 7), k
        )
        lower = lower + got.astype(F32)
    upper = plane(0)
    for up in ups:
        upper = upper + up.astype(F32)
    row = lax.broadcasted_iota(jnp.int32, (rows, 1), 0)
    take = (mine == 0) | ((me == 8) & (row < lead)) | ((me == 31) & (row >= small))
    return jnp.where(take, lower, upper)


def sum_everywhere(x, fast):
    if not fast:
        return lax.psum(x, AXES)
    for k in range(5):
        x = x + permute(x, 1 << k)
    return x


def mlp_body(
    layout,
    me, h0, attended, w_out, w_dec, gains, weight, levels, counted, w_up_hbm, w_down_hbm, dec_mt_hbm, targets_hbm,
    dh1, d_dec, d_gains, loss, keep, send,
    h1, n2, upper, act, h2, n3, pred, d_pred, dm, du, d_y, total_out, d_out, d_up, d_down, w_up, w_down, dec_mt, targets_t, sems, in_sems,
):
    samples, nodes, _ = h0.shape
    here = me[0]
    loads = [
        pltpu.make_async_copy(source, target, in_sems.at[k])
        for k, (source, target) in enumerate(
            ((w_up_hbm, w_up), (w_down_hbm, w_down), (dec_mt_hbm, dec_mt), (targets_hbm, targets_t))
        )
    ]
    for load in loads:
        load.start()
    pixels = dec_mt.shape[1]
    pred[...] = jnp.zeros(pred.shape, BF)
    scale = (2.0 / counted[0:1, 0:1]) * (1.0 / 3.0)
    tile = 512
    tiles = nodes // tile
    for s in range(samples):

        @pl.loop(0, tiles, unroll=True)
        def _(i):
            rows = pl.ds(pl.multiple_of(i * tile, tile), tile)
            flat = pl.ds(pl.multiple_of(s * nodes + i * tile, tile), tile)
            mid = h0[s, rows, :] + dot(attended[s, rows, :], w_out[...])
            h1[flat, :] = mid
            hat, _ = norm(mid)
            in_two = (hat * gains[1:2, :]).astype(BF)
            n2[flat, :] = in_two
            if s == 0:
                loads[0].wait()
                loads[1].wait()
            end = mid
            for c in range(4):
                cols = slice(c * D, (c + 1) * D)
                u = dot(in_two, w_up[:, cols])
                sig = sigmoid(u)
                upper[flat, cols] = slope(u, sig)
                a = (u * sig).astype(BF)
                act[flat, cols] = a
                end = end + dot(a, w_down[cols, :])
            h2[flat, :] = end
            hat, _ = norm(end)
            in_three = (hat * gains[2:3, :]).astype(BF)
            n3[flat, :] = in_three
            high, low = split(dot(in_three, w_dec[...]).T)
            pred[s * CP : s * CP + C_OUT, rows] = high
            pred[(samples + s) * CP : (samples + s) * CP + C_OUT, rows] = low

    loads[2].wait()
    loads[3].wait()
    d_pred[...] = jnp.zeros(d_pred.shape, F32)
    loss[...] = jnp.zeros(loss.shape, F32)

    @pl.loop(0, pixels // 512)
    def _(i):
        part = pl.ds(pl.multiple_of(i * 512, 512), 512)
        counts = dec_mt[:, part]
        y_all = dot(pred[...], counts)
        highs, lows = [], []
        for s in range(samples):
            y = y_all[s * CP : (s + 1) * CP] + y_all[(samples + s) * CP : (samples + s + 1) * CP]
            misfit = y * (1.0 / 3.0) - targets_t[s, :, part]
            g = weight[s : s + 1, part] * levels[...] * misfit
            loss[...] += jnp.sum(g * misfit, axis=0, keepdims=True)
            high, low = split(g * scale)
            highs.append(high)
            lows.append(low)
        d_pred[...] += dot_nt(jnp.concatenate(highs + lows, axis=0), counts)

    total_out[...] = jnp.zeros(total_out.shape, F32)
    d_dec[...] = jnp.zeros(d_dec.shape, F32)
    d_gains[...] = jnp.zeros(d_gains.shape, F32)
    for s in range(samples):
        total = d_pred[s * CP : (s + 1) * CP] + d_pred[(samples + s) * CP : (samples + s + 1) * CP]
        padded = jnp.concatenate([total, jnp.zeros((128 - CP, nodes), F32)], axis=0)
        d_y[...] = padded.T.astype(BF)

        @pl.loop(0, tiles, unroll=True)
        def _(i):
            rows = pl.ds(pl.multiple_of(i * tile, tile), tile)
            flat = pl.ds(pl.multiple_of(s * nodes + i * tile, tile), tile)
            d_part = d_y[rows, 0:C_OUT]
            d_dec[...] += dot_tn(n3[flat, :], d_part)
            grad = dot_nt(d_part, w_dec[...])
            hat, r = norm(h2[flat, :])
            d_gains[2:3, :] += jnp.sum(grad * hat, axis=0, keepdims=True)
            d_end = norm_back(grad, gains[2:3, :], hat, r)
            d_low = d_end.astype(BF)
            dm[flat, :] = d_low
            d_in = jnp.zeros((tile, D), F32)
            for c in range(4):
                cols = slice(c * D, (c + 1) * D)
                d_act = dot_nt(d_low, w_down[cols, :])
                d_u = (d_act * upper[flat, cols]).astype(BF)
                du[flat, cols] = d_u
                d_in = d_in + dot_nt(d_u, w_up[:, cols])
            hat, r = norm(h1[flat, :])
            d_gains[1:2, :] += jnp.sum(d_in * hat, axis=0, keepdims=True)
            d_mid = d_end + norm_back(d_in, gains[1:2, :], hat, r)
            dh1[s, rows, :] = d_mid
            total_out[...] += dot_tn(attended[s, rows, :], d_mid.astype(BF))

    def copies(name, source, action):
        window_copies(
            here, layout.rows, layout.plans[0][0][name], source, keep, send, sems, action
        )

    for c in range(4):
        cols = slice(c * D, (c + 1) * D)
        put_flat(d_down, dot_tn(act[:, cols], dm[...]), 4 * c * D, 4)
    copies("down", d_down, "start")
    put_flat(d_out, total_out[...], 0, 4)
    copies("out", d_out, "start")
    for c in range(4):
        cols = slice(c * D, (c + 1) * D)
        put_flat(d_up, dot_tn(n2[...], du[:, cols]), 4 * c, 16)
    copies("up", d_up, "start")
    copies("down", d_down, "wait")
    copies("out", d_out, "wait")
    copies("up", d_up, "wait")


def mlp(me, h0, attended, w_out, w_up, w_down, w_dec, gains, dec_mt, targets_t, weight, levels, counted, layout):
    samples, nodes, _ = h0.shape
    rows = samples * nodes
    count = layout.plans[0][1]
    sent = layout.sizes[0] if layout.fast else 8
    vmem = pl.BlockSpec(memory_space=pltpu.VMEM)
    hbm = pl.BlockSpec(memory_space=pl.ANY)
    return pl.pallas_call(
        functools.partial(mlp_body, layout),
        out_shape=[
            shape((samples, nodes, D)),
            shape((D, C_OUT)),
            shape((8, D)),
            shape((1, 512)),
            shape((layout.sizes[0], 128)),
            shape((sent, 128)),
        ],
        in_specs=[pl.BlockSpec(memory_space=pltpu.SMEM)] + [vmem] * 8 + [hbm] * 4,
        out_specs=[vmem] * 4 + [hbm] * 2,
        scratch_shapes=[
            pltpu.VMEM((rows, D), F32),
            pltpu.VMEM((rows, D), BF),
            pltpu.VMEM((rows, FF), F32),
            pltpu.VMEM((rows, FF), BF),
            pltpu.VMEM((rows, D), F32),
            pltpu.VMEM((rows, D), BF),
            pltpu.VMEM((2 * samples * CP, nodes), BF),
            pltpu.VMEM((2 * samples * CP, nodes), F32),
            pltpu.VMEM((rows, D), BF),
            pltpu.VMEM((rows, FF), BF),
            pltpu.VMEM((nodes, 128), BF),
            pltpu.VMEM((D, D), F32),
            pltpu.VMEM((4 * D, 128), F32),
            pltpu.VMEM((16 * D, 128), F32),
            pltpu.VMEM((4 * FF, 128), F32),
            pltpu.VMEM(w_up.shape, BF),
            pltpu.VMEM(w_down.shape, BF),
            pltpu.VMEM(dec_mt.shape, BF),
            pltpu.VMEM(targets_t.shape, F32),
            pltpu.SemaphoreType.DMA((count,)),
            pltpu.SemaphoreType.DMA((4,)),
        ],
        compiler_params=pltpu.CompilerParams(vmem_limit_bytes=60 << 20),
        cost_estimate=pl.CostEstimate(flops=16 << 30, bytes_accessed=24 << 20, transcendentals=0),
    )(me, h0, attended, w_out, w_dec, gains, weight, levels, counted, w_up, w_down, dec_mt, targets_t)


def attend_back_body(
    qkv, before, after, log_c, dh1, w_out,
    d_qkv, d_rims, d_before, d_after,
    pairs, do_both,
):
    samples, nodes, _ = dh1.shape
    halo = before.shape[1]
    for s in range(samples):
        gather_pairs(qkv, before, after, pairs, s)
        for i in range(nodes // 256):
            rows = slice(i * 256, (i + 1) * 256)
            da = dh1[s, rows, :].astype(BF)
            high, low = split(dot_nt(da, w_out[...]))
            for h in range(HEADS):
                lanes = slice(h * HEAD_DIM, (h + 1) * HEAD_DIM)
                do_both[rows, 2 * h * HEAD_DIM : (2 * h + 1) * HEAD_DIM] = high[:, lanes]
                do_both[rows, (2 * h + 1) * HEAD_DIM : (2 * h + 2) * HEAD_DIM] = low[:, lanes]
        for h in range(HEADS):
            lanes = slice(h * HEAD_DIM, (h + 1) * HEAD_DIM)
            vlanes = slice(D + h * HEAD_DIM, D + (h + 1) * HEAD_DIM)
            query = qkv[s, :, lanes]
            keys = pairs[:, lanes]
            values = pairs[:, vlanes]
            do = do_both[:, 2 * h * HEAD_DIM : (2 * h + 2) * HEAD_DIM]
            probs = attention_weights(keys, query, log_c)
            d_probs = dot_nt(jnp.concatenate([values, values], axis=1), do)
            centre = jnp.sum(probs * d_probs, 0, keepdims=True)
            high, low = split(probs * (d_probs - centre))
            dv2 = dot(probs.astype(BF), do)
            dv = dv2[:, :HEAD_DIM] + dv2[:, HEAD_DIM:]
            dk = (dot(high, query) + dot(low, query)) * SCALE
            dq_t = (dot_tn(keys, high) + dot_tn(keys, low)) * SCALE
            d_qkv[s, :, lanes] = dq_t.T.astype(BF)
            klanes = slice(D + h * HEAD_DIM, D + (h + 1) * HEAD_DIM)
            wide_lanes = slice(2 * D + h * HEAD_DIM, 2 * D + (h + 1) * HEAD_DIM)
            d_qkv[s, :, klanes] = dk[halo : halo + nodes].astype(BF)
            d_qkv[s, :, wide_lanes] = dv[halo : halo + nodes].astype(BF)
            for rim, first in ((0, halo), (1, nodes)):
                d_rims[s, rim, :, lanes] = dk[first : first + halo]
                d_rims[s, rim, :, vlanes] = dv[first : first + halo]
            d_before[s, :, lanes] = dk[:halo].astype(BF)
            d_before[s, :, vlanes] = dv[:halo].astype(BF)
            d_after[s, :, lanes] = dk[halo + nodes :].astype(BF)
            d_after[s, :, vlanes] = dv[halo + nodes :].astype(BF)


def attend_back(qkv, before, after, log_c, dh1, w_out):
    samples, nodes, _ = dh1.shape
    halo = before.shape[1]
    return kernel_call(
        attend_back_body,
        [
            shape((samples, nodes, 3 * D), BF),
            shape((samples, 2, halo, 2 * D)),
            shape((samples, halo, 2 * D), BF),
            shape((samples, halo, 2 * D), BF),
        ],
        [pltpu.VMEM((log_c.shape[0], 2 * D), BF), pltpu.VMEM((nodes, 2 * D), BF)],
        nbytes=20 << 20,
        flops=8 << 30,
    )(qkv, before, after, log_c, dh1, w_out)


def node_back_body(
    layout,
    me, w_qkv, gains, h0, dh1, d_in, d_rims, from_lower, from_upper, d_dec, d_gains,
    both, keep, send,
    dqkv, n1, d_gain, d_qkv, small, sems,
):
    samples, nodes, _ = h0.shape
    here = me[0]

    def copies(name, source, action):
        window_copies(
            here, layout.rows, layout.plans[1][0][name], source, keep, send, sems, action
        )

    halo = from_lower.shape[1]
    d_gain[...] = d_gains[...]
    for s in range(samples):
        base = s * nodes
        dqkv[base : base + nodes, :] = d_in[s]
        low_rim = d_rims[s, 0] + from_lower[s].astype(F32)
        dqkv[base : base + halo, D:] = low_rim.astype(BF)
        high_rim = d_rims[s, 1] + from_upper[s].astype(F32)
        dqkv[base + nodes - halo : base + nodes, D:] = high_rim.astype(BF)
        flat = slice(base, base + nodes)
        hat, r = norm(h0[s])
        n1[flat, :] = (hat * gains[0:1, :]).astype(BF)
        grad = dot_nt(dqkv[flat, :], w_qkv[...])
        d_gain[0:1, :] += jnp.sum(grad * hat, axis=0, keepdims=True)
        d_start = dh1[s] + norm_back(grad, gains[0:1, :], hat, r)
        high, low = split(d_start * 0.25)
        both[s, :, 0:D] = high
        both[s, :, D:] = low
    small[0 : 4 * C_OUT, :] = d_dec[...]
    small[4 * C_OUT :, :] = jnp.zeros((small.shape[0] - 4 * C_OUT, 128), F32)
    for k in range(3):
        for lane in range(D // 128):
            row = 4 * (C_OUT + k) + lane
            small[row : row + 1, :] = d_gain[k : k + 1, lane * 128 : lane * 128 + 128]
    copies("small", small, "start")
    for c in range(3):
        put_flat(d_qkv, dot_tn(n1[...], dqkv[:, c * D : (c + 1) * D]), 4 * c, 12)
    copies("qkv", d_qkv, "start")
    copies("small", small, "wait")
    copies("qkv", d_qkv, "wait")


def node_back(me, w_qkv, gains, h0, dh1, d_in, d_rims, from_lower, from_upper, d_dec, d_gains, layout):
    samples, nodes, _ = h0.shape
    rows = samples * nodes
    vmem = pl.BlockSpec(memory_space=pltpu.VMEM)
    hbm = pl.BlockSpec(memory_space=pl.ANY)
    return pl.pallas_call(
        functools.partial(node_back_body, layout),
        out_shape=[
            shape((samples, nodes, 2 * D), BF),
            shape((layout.sizes[1], 128)),
            shape((layout.sizes[1] if layout.fast else 8, 128)),
        ],
        in_specs=[pl.BlockSpec(memory_space=pltpu.SMEM)] + [vmem] * 10,
        out_specs=[vmem, hbm, hbm],
        scratch_shapes=[
            pltpu.VMEM((rows, 3 * D), BF),
            pltpu.VMEM((rows, D), BF),
            pltpu.VMEM((8, D), F32),
            pltpu.VMEM((12 * D, 128), F32),
            pltpu.VMEM((layout.small, 128), F32),
            pltpu.SemaphoreType.DMA((layout.plans[1][1],)),
        ],
        compiler_params=pltpu.CompilerParams(vmem_limit_bytes=58 << 20),
        cost_estimate=pl.CostEstimate(flops=8 << 30, bytes_accessed=16 << 20, transcendentals=0),
    )(me, w_qkv, gains, h0, dh1, d_in, d_rims, from_lower, from_upper, d_dec, d_gains)


def pixel_back_body(layout, me, grid, w_enc, enc_mt, both, keep_in, send_in, keep, send, total, d_enc, sems):
    samples, _, pixels = grid.shape
    total[...] = jnp.zeros(total.shape, F32)
    for s in range(samples):

        @pl.loop(0, pixels // 512, unroll=True)
        def _(i):
            rows = pl.ds(pl.multiple_of(i * 512, 512), 512)
            x_t = grid[s, :, rows]
            pre = dot_tn(x_t, w_enc[...])
            spread2 = dot(enc_mt[rows, :], both[s])
            spread = spread2[:, 0:D] + spread2[:, D:]
            d_pre = (spread * slope(pre, sigmoid(pre))).astype(BF)
            total[...] += dot(x_t, d_pre)

    put_flat(d_enc, total[...], 0, 4)
    for action in ("start", "wait"):
        window_copies(
            me[0], layout.rows, layout.plans[1][0]["enc"], d_enc, keep, send, sems, action
        )


def pixel_back(me, grid, w_enc, enc_mt, both, keep, send, layout):
    vmem = pl.BlockSpec(memory_space=pltpu.VMEM)
    hbm = pl.BlockSpec(memory_space=pl.ANY)
    return pl.pallas_call(
        functools.partial(pixel_back_body, layout),
        out_shape=[shape(keep.shape), shape(send.shape)],
        in_specs=[pl.BlockSpec(memory_space=pltpu.SMEM)] + [vmem] * 4 + [hbm] * 2,
        out_specs=[hbm, hbm],
        input_output_aliases={5: 0, 6: 1},
        scratch_shapes=[
            pltpu.VMEM((C_IN, D), F32),
            pltpu.VMEM((4 * C_IN, 128), F32),
            pltpu.SemaphoreType.DMA((layout.plans[1][1],)),
        ],
        compiler_params=pltpu.CompilerParams(vmem_limit_bytes=58 << 20),
        cost_estimate=pl.CostEstimate(flops=8 << 30, bytes_accessed=12 << 20, transcendentals=0),
    )(me, grid, w_enc, enc_mt, both, keep, send)


def ring(axis, distance):
    count = lax.axis_size(axis)
    return [(i, (i + distance) % count) for i in range(count)]


def window_plan(shard, count):
    starts = [(LEAD * D + d * shard) // (16 * D) * 16 for d in range(count)]
    ends = [-(-(LEAD * D + (d + 1) * shard) // D) for d in range(count)]
    rows = max(-(-(e - s + 1) // 16) * 16 for s, e in zip(starts, ends))
    return starts, rows


def per_device(
    grid, targets, area, sigma_weight, level_weight, valid, enc_index, dec_index, neighbours,
    params, first_moment, second_moment, average,
):
    shard = params.shape[0]
    devices = lax.axis_size(AXES)
    me = lax.axis_index(AXES)
    fast = (lax.axis_size("patch"), lax.axis_size("dp")) == (8, 4)
    layout = Layout(shard, devices, fast)
    starts, win = layout.starts, layout.win
    begin = LEAD * D + me * shard
    shift = begin - begin // (16 * D) * (16 * D)
    place = me.astype(jnp.int32).reshape(1)

    count = jnp.sum(valid)
    digits = jnp.stack([count // 128, count % 128]).astype(BF)
    payload = lax.dynamic_update_slice(jnp.zeros((win * D,), BF), params.astype(BF), (shift,))
    payload = lax.dynamic_update_slice(payload, digits, ((win - 1) * D,)).reshape(win, D)
    weight = valid.astype(F32) * area[None, :] * sigma_weight[:, None]
    levels = jnp.pad(level_weight, (0, CP - C_OUT)).reshape(CP, 1)
    pixels = dec_index.shape[0]
    first_work = lambda: count_encoder(enc_index, pixels)
    local_count = count.astype(F32)

    def second_work(dec_index, neighbours, targets):
        return count_rest(dec_index, neighbours, targets), weight, levels

    def third_work(params):
        positions = me * shard + lax.iota(jnp.int32, shard)
        bounds = segment_bounds() + [(-1, -1)]
        lower = jnp.array([x for x, _ in bounds], jnp.int32)[:, None]
        upper = jnp.array([x for _, x in bounds], jnp.int32)[:, None]
        member = ((positions >= lower) & (positions < upper)).astype(F32)
        return member, jnp.sum(member * (params * params)[None, :], axis=1)

    second_inputs, third_inputs = (dec_index, neighbours, targets), (params,)
    if fast:
        pieces, plan, first_done, second_done, third_done = gather_windows(
            payload, first_work, second_work, second_inputs, third_work, third_inputs
        )
        place_of = place_by_xor
    else:
        everything = lax.all_gather(payload, AXES, axis=0, tiled=False)
        pieces = [everything.reshape(devices * win, D)]
        plan = [(0, d * win, d, 0, win) for d in range(devices)]
        place_of = lambda here, d: d
        first_done, second_done = first_work(), second_work(*second_inputs)
        third_done = third_work(*third_inputs)
    member, old_sums = third_done
    enc_m, enc_mt = first_done
    (dec_mt, log_c, targets_t), weight, levels = second_done
    grid = jnp.swapaxes(grid, 1, 2)

    w_enc, w_qkv, gains = unpack(
        place, pieces, plan, ("enc", "qkv", "gains"), place_of, devices, win, starts
    )
    h0, qkv, leading, last = encode(grid, w_enc, enc_m, w_qkv, gains)
    before = lax.ppermute(last, "patch", ring("patch", 1))
    after = lax.ppermute(leading, "patch", ring("patch", -1))
    w_out, w_up, w_down, w_dec, counted = unpack(
        place, pieces, plan, ("out", "up", "down", "dec", "count"), place_of, devices, win, starts
    )
    w_dec = w_dec.reshape(D, C_OUT)
    attended = attend(qkv, before, after, log_c)
    dh1, d_dec, d_gains, loss_rows, keep, send = mlp(
        place, h0, attended, w_out, w_up, w_down, w_dec, gains, dec_mt, targets_t, weight, levels,
        counted, layout,
    )
    back = attend_back(qkv, before, after, log_c, dh1, w_out)
    if fast:
        other = permute(send, 1)
        other, back = lax.optimization_barrier((other, back))
    d_qkv, d_rims, d_before, d_after = back
    from_upper = lax.ppermute(d_before, "patch", ring("patch", -1))
    from_lower = lax.ppermute(d_after, "patch", ring("patch", 1))
    d_dec = d_dec.reshape(4 * C_OUT, 128)
    if fast:
        send_a, send_b = first_send(keep, other, layout)
        got = permute(send_a, 2), permute(send_b, 4)
        send_a, send_b, d_dec, from_upper, from_lower = lax.optimization_barrier(
            (send_a, send_b, d_dec, from_upper, from_lower)
        )
    second = node_back(
        place, w_qkv, gains, h0, dh1, d_qkv, d_rims, from_lower, from_upper, d_dec, d_gains, layout
    )
    if fast:
        second, got = lax.optimization_barrier((second, got))
        keep_a, send_a, keep_b, send_b = second_send(keep, other, *got, layout)
        got = permute(send_a, 4), permute(send_b, 2)
        second, send_a, send_b = lax.optimization_barrier((second, send_a, send_b))
    second = pixel_back(place, grid, w_enc, enc_mt, *second, layout)
    if fast:
        second, got = lax.optimization_barrier((second, got))
        grad_window = sum_rest((keep_a, keep_b), got, second, layout, me)
    else:
        grad_window = sum_flat(keep, second[0], layout)
    grad = lax.dynamic_slice(grad_window.reshape(-1), (begin - begin // 1024 * 1024,), (shard,))

    new_first = BETA_ONE * first_moment + (1.0 - BETA_ONE) * grad
    new_second = BETA_TWO * second_moment + (1.0 - BETA_TWO) * grad * grad
    update = (
        new_first
        / (1.0 - BETA_ONE**STEP)
        / (jnp.sqrt(new_second / (1.0 - BETA_TWO**STEP)) + LAMB_EPS)
        + DECAY * params
    )
    sums = jnp.stack([old_sums, jnp.sum(member * (update * update)[None, :], axis=1)])
    own = jnp.stack([jnp.sum(loss_rows), local_count])[:, None]
    sums = jnp.where(jnp.arange(8)[None, :] == 7, own, sums)
    totals = sum_everywhere(sums, fast)
    norms = jnp.sqrt(totals[:, :7])
    step_ratio = jnp.sum(member[:7] * (norms[0] / norms[1])[:, None], axis=0)
    new_params = params - RATE * step_ratio * update
    new_average = EMA_KEEP * average + (1.0 - EMA_KEEP) * new_params
    return (
        totals[:, 7],
        norms,
        new_params,
        new_first,
        new_second,
        new_average,
    )


def solution(mesh):
    flat = P(AXES)
    in_specs = (
        P("dp", "patch", None),
        P("dp", "patch", None),
        P("patch"),
        P("dp"),
        P(),
        P("dp", "patch"),
        P("patch", None),
        P("patch", None),
        P("patch", None),
        flat,
        flat,
        flat,
        flat,
    )
    out_specs = (P(), P(), flat, flat, flat, flat)
    return jax.shard_map(
        per_device, mesh=mesh, in_specs=in_specs, out_specs=out_specs, check_vma=False
    )
```

```python
import functools
import math

import jax
import jax.numpy as jnp
from jax import lax
from jax.experimental import pallas as pl
from jax.experimental.pallas import tpu as pltpu
from jax.sharding import PartitionSpec as P

D = 512
HEADS = 4
HEAD_DIM = 128
FF = 2048
C_OUT = 84
C_IN = 264
STEP = 10
EPS_NORM = 1e-05
BETA_ONE = 0.9
BETA_TWO = 0.999
LAMB_EPS = 1e-06
DECAY = 0.01
RATE = 0.2
EMA_KEEP = 0.8
BF = jnp.bfloat16
F32 = jnp.float32
SCALE = HEAD_DIM ** (-0.5)
LOG2E = 1.4426950408889634
ABSENT = -1e30
CP = 96
AXES = ("patch", "dp")

LEAD = 8
ROW_ENC = LEAD
ROW_QKV = ROW_ENC + C_IN
ROW_OUT = ROW_QKV + 3 * D
ROW_UP = ROW_OUT + D
ROW_DOWN = ROW_UP + 4 * D
ROW_DEC = ROW_DOWN + FF
ROW_GAIN = ROW_DEC + C_OUT
ROW_END = ROW_GAIN + 3
ROWS_ALL = -(-ROW_END // 16) * 16


def matrix_shapes():
    return [(C_IN, D), (D, 3 * D), (D, D), (D, FF), (FF, D), (D, C_OUT), (3, D)]


def segment_bounds():
    bounds = []
    offset = 0
    for row_count, col_count in matrix_shapes():
        bounds.append((offset, offset + row_count * col_count))
        offset += row_count * col_count
    return bounds


NPARAM_USED = segment_bounds()[-1][1]


def dot(a, b):
    return lax.dot_general(a, b, (((1,), (0,)), ((), ())), preferred_element_type=F32)


def dot_nt(a, b):
    return lax.dot_general(a, b, (((1,), (1,)), ((), ())), preferred_element_type=F32)


def dot_tn(a, b):
    return lax.dot_general(a, b, (((0,), (0,)), ((), ())), preferred_element_type=F32)


def split(x):
    high = x.astype(BF)
    return high, (x - high.astype(F32)).astype(BF)


def sigmoid(x):
    return 0.5 * jnp.tanh(0.5 * x) + 0.5


def slope(x, s):
    return s * (1.0 + x * (1.0 - s))


def norm(x):
    c = x - jnp.mean(x, -1, keepdims=True)
    r = lax.rsqrt(jnp.mean(c * c, -1, keepdims=True) + EPS_NORM)
    return c * r, r


def norm_back(grad, gain, hat, r):
    g = grad * gain
    return r * (
        g
        - jnp.mean(g, -1, keepdims=True)
        - hat * jnp.mean(g * hat, -1, keepdims=True)
    )


def put_flat(ref, value, first, period):
    for lane in range(D // 128):
        ref[pl.ds(first + lane, value.shape[0], stride=period), :] = value[
            :, lane * 128 : lane * 128 + 128
        ]


def kernel_call(body, out_shape, scratch=(), flops=0, nbytes=0):
    return pl.pallas_call(
        body,
        out_shape=out_shape,
        scratch_shapes=list(scratch),
        compiler_params=pltpu.CompilerParams(vmem_limit_bytes=58 << 20),
        cost_estimate=pl.CostEstimate(flops=flops, bytes_accessed=nbytes, transcendentals=0),
    )


def by_sample(*dims):
    return pl.BlockSpec((1,) + dims, lambda s: (s,) + (0,) * len(dims))


def same(*dims):
    return pl.BlockSpec(dims, lambda s: (0,) * len(dims))


HBM = pl.BlockSpec(memory_space=pl.ANY)
SCALAR = pl.BlockSpec(memory_space=pltpu.SMEM)


def shape(dims, dtype=F32):
    return jax.ShapeDtypeStruct(tuple(dims), dtype)


def count_rows(index_t, base, rows, cols):
    ids = lax.broadcasted_iota(jnp.int32, (rows, cols), 0) + base
    total = jnp.zeros((rows, cols), F32)
    for k in range(index_t.shape[0]):
        total = total + jnp.where(index_t[k : k + 1, :] == ids, 1.0, 0.0)
    return total


def count_encoder_body(enc, enc_t, enc_m, enc_mt):
    nodes, pixels = enc_m.shape

    @pl.loop(0, nodes // 32)
    def _(i):
        rows = pl.ds(pl.multiple_of(i * 32, 32), 32)
        index = enc[rows, :]
        ids = lax.broadcasted_iota(jnp.int32, (32, pixels), 1)
        total = jnp.zeros((32, pixels), F32)
        for k in range(index.shape[1]):
            total = total + jnp.where(index[:, k : k + 1] == ids, 1.0, 0.0)
        enc_m[rows, :] = total.astype(BF)

    @pl.loop(0, pixels // 64)
    def _(i):
        rows = pl.ds(pl.multiple_of(i * 64, 64), 64)
        enc_mt[rows, :] = count_rows(enc_t, i * 64, 64, nodes).astype(BF)


def count_rest_body(dec_t, nbr_t, targets, dec_mt, log_c, targets_t):
    nodes, pixels = dec_mt.shape

    @pl.loop(0, nodes // 32)
    def _(i):
        rows = pl.ds(pl.multiple_of(i * 32, 32), 32)
        dec_mt[rows, :] = count_rows(dec_t, i * 32, 32, pixels).astype(BF)

    @pl.loop(0, log_c.shape[0] // 64)
    def _(i):
        rows = pl.ds(pl.multiple_of(i * 64, 64), 64)
        total = count_rows(nbr_t, i * 64, 64, nodes)
        log_c[rows, :] = jnp.where(total > 0.0, jnp.log2(jnp.maximum(total, 1.0)), ABSENT)

    targets_t[...] = jnp.zeros(targets_t.shape, F32)
    for s in range(targets.shape[0]):

        @pl.loop(0, pixels // 256)
        def _(i):
            part = pl.ds(pl.multiple_of(i * 256, 256), 256)
            targets_t[s, 0:C_OUT, part] = targets[s, part, :].T


def count_encoder(enc_index, pixels):
    nodes = enc_index.shape[0]
    return kernel_call(
        count_encoder_body,
        [shape((nodes, pixels), BF), shape((pixels, nodes), BF)],
        nbytes=5 << 20,
        flops=1 << 29,
    )(enc_index, enc_index.T)


def count_rest(dec_index, neighbours, targets):
    nodes, pixels = neighbours.shape[0], dec_index.shape[0]
    ext = nodes + 2 * (nodes // 16)
    return kernel_call(
        count_rest_body,
        [shape((nodes, pixels), BF), shape((ext, nodes)), shape((targets.shape[0], CP, pixels))],
        nbytes=8 << 20,
        flops=1 << 29,
    )(dec_index.T, neighbours.T, targets)


def tile_sources(starts, rows):
    return [
        [(d, tile * 16 - s) for d, s in enumerate(starts) if s <= tile * 16 < s + rows]
        for tile in range(ROWS_ALL // 16)
    ]


def assemble(read, window_rows, sources, first_row, rows, put):
    tile, last = first_row // 16, (first_row + rows) // 16
    while tile < last:
        source = sources[tile]
        if len(source) == 1:
            count = 1
            while (
                tile + count < last
                and len(sources[tile + count]) == 1
                and sources[tile + count][0][0] == source[0][0]
                and count < 8
            ):
                count += 1
            d, off = source[0]
            value = read(d, off, 16 * count)
        else:
            count = 1
            value = None
            for d, off in source:
                part = read(d, off, 16).astype(F32)
                if off + 16 == window_rows:
                    part = jnp.where(
                        lax.broadcasted_iota(jnp.int32, part.shape, 0) < 15, part, 0.0
                    )
                value = part if value is None else value + part
            value = value.astype(BF)
        put(tile * 16 - first_row, value)
        tile += count


def wide(stage, ref, period):
    for lane in range(D // 128):
        for c in range(period):
            lanes = slice(c * D + lane * 128, c * D + lane * 128 + 128)
            ref[:, lanes] = stage[lane, pl.ds(c, ref.shape[0], stride=period), :].astype(BF)


def unpack_body(plan, parts, sources, place_of, owner_of, count, *refs):
    me, pieces, refs = refs[0], refs[1 : count + 1], refs[count + 1 :]
    outs, (windows, stage, sems) = refs[: len(parts)], refs[len(parts) :]
    here = me[0]
    used = set()
    for part in parts:
        if part == "count":
            used = set(range(windows.shape[0]))
        else:
            row, rows = PARTS[part][:2]
            used |= {d for source in sources[row // 16 : (row + rows) // 16] for d, _ in source}
    ranges = [d for d in sorted(used) if d - 1 not in used], [d for d in sorted(used) if d + 1 not in used]
    for piece, at, slot, to, rows in plan:
        copy = pltpu.make_async_copy(
            pieces[piece].at[pl.ds(at, rows), :], windows.at[slot, pl.ds(to, rows), :], sems.at[slot]
        )
        owner = owner_of(here, slot)
        needed = functools.reduce(
            jnp.logical_or, [(owner >= lo) & (owner <= hi) for lo, hi in zip(*ranges)]
        )
        if len(used) == windows.shape[0]:
            copy.start()
        else:
            pl.when(needed)(copy.start)
    window_rows = windows.shape[1]
    waited = set()

    def wait_for(d):
        if d not in waited:
            waited.add(d)
            slot = place_of(here, d)
            pltpu.make_async_copy(windows.at[slot], windows.at[slot], sems.at[slot]).wait()

    def read(d, off, rows):
        wait_for(d)
        return windows[place_of(here, d), off : off + rows, :]

    for part, ref in zip(parts, outs):
        if part == "count":
            for d in range(windows.shape[0]):
                wait_for(d)
            total = jnp.sum(windows[:, window_rows - 16 :, :].astype(F32), axis=0)[15:16, :]
            ref[...] = jnp.sum(total, axis=1, keepdims=True) + jnp.zeros((8, 128), F32)
            continue
        first, rows, period, _ = PARTS[part]

        def direct(off, value):
            ref[off : off + value.shape[0], :] = value

        def staged(off, value):
            wide_value = value.astype(F32)
            for lane in range(D // 128):
                stage[lane, off : off + value.shape[0], :] = wide_value[
                    :, lane * 128 : lane * 128 + 128
                ]

        if part == "gains":
            assemble(read, window_rows, sources, first, rows, staged)
            row = ROW_GAIN - first
            for lane in range(D // 128):
                ref[:, lane * 128 : lane * 128 + 128] = stage[lane, row : row + 8, :]
        elif period == 1:
            assemble(read, window_rows, sources, first, rows, direct)
        else:
            assemble(read, window_rows, sources, first, rows, staged)
            if part == "enc":
                for lane in range(D // 128):
                    lanes = slice(lane * 128, lane * 128 + 128)
                    ref[:, lanes] = stage[lane, LEAD:ROW_QKV, :].astype(BF)
            elif part == "dec":
                for lane in range(D // 128):
                    lanes = slice(lane * 128, lane * 128 + 128)
                    row = ROW_DEC - first
                    ref[:, lanes] = stage[lane, row : row + C_OUT, :].astype(BF)
            else:
                wide(stage, ref, period)


PARTS = {
    "enc": (0, ROW_QKV, 0, (C_IN, D)),
    "qkv": (ROW_QKV, 3 * D, 3, (D, 3 * D)),
    "out": (ROW_OUT, D, 1, (D, D)),
    "up": (ROW_UP, 4 * D, 4, (D, FF)),
    "down": (ROW_DOWN, FF, 1, (FF, D)),
    "dec": (ROW_DEC // 16 * 16, -(-ROW_GAIN // 16) * 16 - ROW_DEC // 16 * 16, 0, (C_OUT, D)),
    "gains": (ROW_GAIN // 16 * 16, 16, 0, (8, D)),
}


def unpack(me, pieces, plan, parts, place_of, slots, rows, starts):
    sources = tile_sources(starts, rows)
    outs = [
        shape((8, 128)) if p == "count" else shape(PARTS[p][3], F32 if p == "gains" else BF)
        for p in parts
    ]
    return pl.pallas_call(
        functools.partial(unpack_body, plan, parts, sources, place_of, place_of, len(pieces)),
        out_shape=outs,
        in_specs=[pl.BlockSpec(memory_space=pltpu.SMEM)]
        + [pl.BlockSpec(memory_space=pl.ANY)] * len(pieces),
        scratch_shapes=[
            pltpu.VMEM((slots, rows, D), BF),
            pltpu.VMEM((D // 128, 4 * D, 128), F32),
            pltpu.SemaphoreType.DMA((slots,)),
        ],
        compiler_params=pltpu.CompilerParams(vmem_limit_bytes=58 << 20),
        cost_estimate=pl.CostEstimate(
            flops=0, bytes_accessed=slots * rows * D * 4, transcendentals=0
        ),
    )(me, *pieces)


def permute(x, mask):
    count = lax.axis_size(AXES)
    return lax.ppermute(x, AXES, [(d, d ^ mask) for d in range(count)])


def place_by_xor(here, d):
    return jnp.bitwise_xor(here, d)


def gather_windows(window, first_work, second_work, second_inputs, third_work, third_inputs):
    rows = window.shape[0]
    half = rows // 2
    pieces, plan = [], []

    def add(piece, near, parts):
        for part, flip in ((piece, 0), (permute(piece, 1), 1)):
            for at, slot, to, size in parts:
                plan.append((len(pieces), at, slot ^ near ^ flip, to, size))
            pieces.append(part)

    planes = (8, 16, 24)
    others = [permute(window, m) for m in planes]
    by_x, by_y = permute(window, 2), permute(window, 4)
    first_done = first_work()
    others, by_x, by_y, first_done, second_inputs = lax.optimization_barrier(
        (jnp.concatenate(others), by_x, by_y, first_done, second_inputs)
    )
    others_x, others_y = permute(others, 2), permute(others, 4)
    second_done = second_work(*second_inputs)
    others_x, others_y, second_done, third_inputs = lax.optimization_barrier(
        (others_x, others_y, second_done, third_inputs)
    )

    def halves(near_part, far_part, first):
        far = [far_part[i * rows + first : i * rows + first + half] for i in range(3)]
        return jnp.concatenate([near_part[first : first + half]] + far)

    across_a = permute(halves(by_y, others_y, 0), 2)
    across_b = permute(halves(by_x, others_x, half), 4)
    across_a, across_b, third_done = lax.optimization_barrier(
        (across_a, across_b, third_work(*third_inputs))
    )
    whole = [(0, 0, 0, rows)]
    stacked = [(i * rows, slot, 0, rows) for i, slot in enumerate(planes)]
    add(window, 0, whole)
    add(by_x, 2, whole)
    add(by_y, 4, whole)
    add(others, 0, stacked)
    add(others_x, 2, stacked)
    add(others_y, 4, stacked)
    add(across_a, 6, [(i * half, slot, 0, half) for i, slot in enumerate((0,) + planes)])
    add(across_b, 6, [(i * half, slot, half, half) for i, slot in enumerate((0,) + planes)])
    return pieces, plan, first_done, second_done, third_done


def encode_body(grid, w_enc, enc_hbm, w_hbm, gains, h0, qkv, leading, last, high, low, enc_m, w_qkv, sems):
    pixels, nodes, halo = grid.shape[2], h0.shape[1], last.shape[1]
    first = pl.program_id(0) == 0
    loads = [
        pltpu.make_async_copy(enc_hbm, enc_m, sems.at[0]),
        pltpu.make_async_copy(w_hbm, w_qkv, sems.at[1]),
    ]
    for load in loads:
        pl.when(first)(load.start)
    for i in range(pixels // 512):
        rows = slice(i * 512, (i + 1) * 512)
        pre = dot_tn(grid[0, :, rows], w_enc[...])
        high[rows, :], low[rows, :] = split(pre * sigmoid(pre))
    for load in loads:
        pl.when(first)(load.wait)
    start = (dot(enc_m[...], high[...]) + dot(enc_m[...], low[...])) * 0.25
    h0[0] = start
    hat, _ = norm(start)
    n1 = (hat * gains[0:1, :]).astype(BF)
    qkv[0] = dot(n1, w_qkv[...]).astype(BF)
    leading[0] = qkv[0, 0:halo, D:]
    last[0] = qkv[0, nodes - halo :, D:]


def encode(grid, w_enc, enc_m, w_qkv, gains):
    samples, pixels = grid.shape[0], grid.shape[2]
    nodes = enc_m.shape[0]
    halo = nodes // 16
    return pl.pallas_call(
        encode_body,
        grid=(samples,),
        out_shape=[shape((samples, nodes, D)), shape((samples, nodes, 3 * D), BF)]
        + [shape((samples, halo, 2 * D), BF)] * 2,
        in_specs=[by_sample(C_IN, pixels), same(C_IN, D), HBM, HBM, same(8, D)],
        out_specs=[by_sample(nodes, D), by_sample(nodes, 3 * D)] + [by_sample(halo, 2 * D)] * 2,
        scratch_shapes=[
            pltpu.VMEM((pixels, D), BF),
            pltpu.VMEM((pixels, D), BF),
            pltpu.VMEM(enc_m.shape, BF),
            pltpu.VMEM(w_qkv.shape, BF),
            pltpu.SemaphoreType.DMA((2,)),
        ],
        compiler_params=pltpu.CompilerParams(vmem_limit_bytes=58 << 20),
        cost_estimate=pl.CostEstimate(flops=8 << 30, bytes_accessed=12 << 20, transcendentals=0),
    )(grid, w_enc, enc_m, w_qkv, gains)


def gather_pairs(qkv, before, after, pairs, s):
    halo, nodes = before.shape[1], qkv.shape[1]
    pairs[0:halo, :] = before[s]
    pairs[halo : halo + nodes, :] = qkv[s, :, D:]
    pairs[halo + nodes :, :] = after[s]


def attention_weights(keys, query, log_c):
    x = dot_nt(keys, query) * (SCALE * LOG2E) + log_c[...]
    e = jnp.exp2(x - jnp.max(x, 0, keepdims=True))
    return e * (1.0 / jnp.sum(e, 0, keepdims=True))


def attend_body(qkv, before, after, log_c, out, pairs):
    for s in range(qkv.shape[0]):
        gather_pairs(qkv, before, after, pairs, s)
        for h in range(HEADS):
            lanes = slice(h * HEAD_DIM, (h + 1) * HEAD_DIM)
            keys = pairs[:, lanes]
            values = pairs[:, D + h * HEAD_DIM : D + (h + 1) * HEAD_DIM]
            probs = attention_weights(keys, qkv[s, :, lanes], log_c)
            out_t = dot_tn(values, probs.astype(BF))
            out[s, :, lanes] = out_t.T.astype(BF)


def attend(qkv, before, after, log_c):
    samples, nodes = qkv.shape[:2]
    halo = before.shape[1]
    return pl.pallas_call(
        attend_body,
        grid=(samples,),
        out_shape=shape((samples, nodes, D), BF),
        in_specs=[
            by_sample(nodes, 3 * D),
            by_sample(halo, 2 * D),
            by_sample(halo, 2 * D),
            same(*log_c.shape),
        ],
        out_specs=by_sample(nodes, D),
        scratch_shapes=[pltpu.VMEM((log_c.shape[0], 2 * D), BF)],
        compiler_params=pltpu.CompilerParams(vmem_limit_bytes=58 << 20),
        cost_estimate=pl.CostEstimate(flops=2 << 30, bytes_accessed=8 << 20, transcendentals=0),
    )(qkv, before, after, log_c)


class Layout:
    def __init__(self, shard, devices, fast):
        self.devices = devices
        self.starts, self.win = window_plan(shard, devices)
        self.begins = [(LEAD * D + d * shard) // 1024 * 8 for d in range(devices)]
        self.ends = [-(-(LEAD * D + (d + 1) * shard) // 1024) * 8 for d in range(devices)]
        self.rows = -(-max(e - b for b, e in zip(self.begins, self.ends)) // 32) * 32
        self.small = 4 * (ROWS_ALL - ROW_DEC)
        first = (("out", ROW_OUT, 4 * D), ("up", ROW_UP, 16 * D)) + tuple(
            (f"down{c}", ROW_DOWN + c * D, 4 * D) for c in range(FF // D)
        )
        second = (("enc", ROW_ENC, 4 * C_IN), ("qkv", ROW_QKV, 12 * D), ("small", ROW_DEC, self.small))
        self.fast = fast
        if fast:
            self.apart = 4 * ROW_OUT - self.begins[8]
            extra = -(-(self.apart + self.small) // 32) * 32
            self.sizes = (12 * self.rows, 4 * self.rows + extra)
        else:
            self.sizes = (sum(x[2] for x in first), sum(x[2] for x in second))
        self.plans = self.make(first, 1), self.make(second, 0)

    def make(self, arrays, plane):
        plans, k, at = {}, 0, 0
        for name, row, size in arrays:
            plans[name] = []
            if not self.fast:
                plans[name].append((k, None, at, 0, size))
                k, at = k + 1, at + size
                continue
            if name == "small":
                plans[name].append((k, "both", 4 * self.rows + self.apart, 0, size))
                k += 2
                continue
            for d, (lower, upper) in enumerate(zip(self.begins, self.ends)):
                low, high = max(lower, 4 * row), min(upper, 4 * (row + size // 4))
                if low >= high:
                    continue
                if d == 8 and plane == 0:
                    to = 4 * self.rows + low - lower
                    plans[name].append((k, "both", to, low - 4 * row, high - low))
                    k += 2
                else:
                    place = (d // 8 - plane) * 4 * self.rows + low - lower
                    plans[name].append((k, d % 8, place, low - 4 * row, high - low))
                    k += 1
        return plans, k


def window_copies(here, rows_of_slot, blocks, source, keep, send, sems, action):
    for k, near, to, at, rows in blocks:

        def copy(target, first, sem):
            getattr(
                pltpu.make_async_copy(
                    source.at[pl.ds(at, rows), :], target.at[pl.ds(first, rows), :], sems.at[sem]
                ),
                action,
            )()

        if near is None:
            copy(keep, to, k)
        elif near == "both":
            copy(keep, to, k)
            copy(send, to, k + 1)
        else:
            slot = jnp.bitwise_and(jnp.bitwise_xor(here, near), 7)
            first = pl.multiple_of(lax.shift_right_logical(slot, 1) * rows_of_slot + to, 8)
            for target, side in ((keep, 0), (send, 1)):

                @pl.when(jnp.bitwise_and(slot, 1) == side)
                def _():
                    copy(target, first, k)


def sum_flat(first, second, layout):
    flat = jnp.concatenate(
        [
            jnp.zeros((4 * LEAD, 128), F32),
            second[: 4 * (ROW_OUT - LEAD)],
            first,
            second[4 * (ROW_OUT - LEAD) :],
            jnp.zeros((max(0, layout.begins[-1] + layout.rows - 4 * ROWS_ALL), 128), F32),
        ]
    )
    windows = jnp.concatenate([flat[b : b + layout.rows] for b in layout.begins])
    return lax.psum_scatter(windows, AXES, scatter_dimension=0, tiled=True)


def low(x):
    return x.astype(BF)


def packed(blocks, extra):
    return low(jnp.concatenate([blocks.reshape(-1, 128), extra]))


def add_packed(flat, blocks, extra):
    flat = flat.astype(F32)
    count = flat.shape[0] - extra.shape[0]
    return blocks + flat[:count].reshape(blocks.shape), extra + flat[count:]


def across_planes(x, allowed, k):
    pairs = [(d, d ^ (8 * k)) for d in range(32) if allowed((d ^ (8 * k)) // 8, d % 8)]
    return lax.ppermute(x, AXES, pairs)


def add_halves(layout, keep, other, got, sends):
    half = layout.rows // 2
    keep, other = keep.reshape(24, half, 128), other.reshape(24, half, 128)
    steps = []
    for out, (picks, source, _) in enumerate(sends):
        for i, pick in enumerate(picks):
            steps.append((out, i, pick, source))

    def body(*refs):
        keep_ref, other_ref = refs[:2]
        gots, outs = refs[2 : 2 + len(got)], refs[2 + len(got) : 2 + len(got) + len(sends)]
        slots, sems = refs[-2:]
        copies = []
        for k, (out, i, pick, source) in enumerate(steps):
            pair = [
                pltpu.make_async_copy(ref.at[pick], slots.at[2 * k + j], sems.at[2 * k + j])
                for j, ref in enumerate((keep_ref, other_ref))
            ]
            for copy in pair:
                copy.start()
            copies.append(pair)
        for k, (out, i, pick, source) in enumerate(steps):
            for copy in copies[k]:
                copy.wait()
            value = slots[2 * k] + slots[2 * k + 1]
            if source is not None:
                which, at = source[0], source[1][i]
                value = value + gots[which][at].astype(F32)
            outs[out][i] = value.astype(outs[out].dtype)

    hbm = pl.BlockSpec(memory_space=pl.ANY)
    vmem = pl.BlockSpec(memory_space=pltpu.VMEM)
    return pl.pallas_call(
        body,
        out_shape=[shape((len(p), half, 128), BF if sent else F32) for p, _, sent in sends],
        in_specs=[hbm, hbm] + [vmem] * len(got),
        out_specs=[vmem] * len(sends),
        scratch_shapes=[
            pltpu.VMEM((2 * len(steps), half, 128), F32),
            pltpu.SemaphoreType.DMA((2 * len(steps),)),
        ],
        compiler_params=pltpu.CompilerParams(vmem_limit_bytes=58 << 20),
        cost_estimate=pl.CostEstimate(
            flops=0, bytes_accessed=len(steps) * half * 1536, transcendentals=0
        ),
    )(keep, other, *got)


def first_send(keep, other, layout):
    to_x = [(p * 4 + y * 2 + 1) * 2 for p in range(3) for y in range(2)]
    to_y = [(p * 4 + 2 + x) * 2 + 1 for p in range(3) for x in range(2)]
    return add_halves(layout, keep, other, (), [(to_x, None, True), (to_y, None, True)])


def second_send(keep, other, got_a, got_b, layout):
    sends = []
    for which, (lower, stride) in enumerate(((0, 2), (1, 1))):
        for far in range(2):
            picks = [(p * 4 + far * stride) * 2 + lower for p in range(3)]
            sends.append((picks, (which, [p * 2 + far for p in range(3)]), far == 1))
    return add_halves(layout, keep, other, (got_a, got_b), sends)


def sum_rest(kept, got, second, layout, me):
    rows = layout.rows
    half = rows // 2
    near, mine = me % 8, me // 8

    late = second[0] + permute(second[1], 1)
    apart = late[4 * rows :]
    late = late[: 4 * rows].reshape(2, 2, rows, 128)
    cut = apart.shape[0] // 2
    send_a = packed(late[:, 1, :half], apart[:cut])
    send_b = packed(late[1, :, half:], apart[cut:])
    late_a, apart_a = add_packed(permute(send_a, 2), late[:, 0, :half], apart[:cut])
    late_b, apart_b = add_packed(permute(send_b, 4), late[0, :, half:], apart[cut:])
    got, _, _ = lax.optimization_barrier((got, send_a, send_b))
    kept_a, kept_b = kept[0] + got[0].astype(F32), kept[1] + got[1].astype(F32)

    def plane(k):
        at = jnp.maximum(jnp.bitwise_xor(mine, k) - 1, 0)
        return jnp.concatenate(
            [lax.dynamic_index_in_dim(x, at, 0, False) for x in (kept_a, kept_b)]
        )

    ups = [across_planes(low(plane(k)), lambda p, q: p > 0, k) for k in (1, 2, 3)]

    late_a, apart_a = add_packed(permute(packed(late_a[1], apart_a), 4), late_a[0], apart_a)
    late_b, apart_b = add_packed(permute(packed(late_b[1], apart_b), 2), late_b[0], apart_b)
    apart = jnp.concatenate([apart_a, apart_b])
    lead, small = layout.apart, 4 * ROW_DEC - layout.begins[31]
    size = min(layout.small, rows - small)
    one = jnp.concatenate([apart[:lead], jnp.zeros((rows - lead, 128), F32)])
    three = jnp.concatenate(
        [
            jnp.zeros((small, 128), F32),
            apart[lead : lead + size],
            jnp.zeros((rows - small - size, 128), F32),
        ]
    )
    parts = jnp.stack([jnp.concatenate([late_a, late_b]), one, one, three])

    def part(k):
        return lax.dynamic_index_in_dim(parts, jnp.bitwise_xor(mine, k), 0, False)

    lower = part(0)
    for k in (1, 2, 3):
        got = across_planes(
            low(part(k)), lambda p, q: p == 0 or (p, q) == (1, 0) or (p, q) == (3, 7), k
        )
        lower = lower + got.astype(F32)
    upper = plane(0)
    for up in ups:
        upper = upper + up.astype(F32)
    row = lax.broadcasted_iota(jnp.int32, (rows, 1), 0)
    take = (mine == 0) | ((me == 8) & (row < lead)) | ((me == 31) & (row >= small))
    return jnp.where(take, lower, upper)


def sum_everywhere(x, fast):
    if not fast:
        return lax.psum(x, AXES)
    for k in range(5):
        x = x + permute(x, 1 << k)
    return x


def mlp_body(
    layout,
    me, h0, attended, w_out, w_dec, gains, weight, levels, counted, w_up_hbm, w_down_hbm, dec_mt_hbm, targets_hbm,
    dh1, d_dec, d_gains, loss, keep, send,
    h1, n2, upper, act, h2, n3, pred, d_pred, dm, du, d_y, total_out, d_out, d_up, d_down, w_up, w_down, dec_mt, targets_t, sems, in_sems,
):
    samples, nodes, _ = h0.shape
    here = me[0]
    loads = [
        pltpu.make_async_copy(source, target, in_sems.at[k])
        for k, (source, target) in enumerate(
            ((w_up_hbm, w_up), (w_down_hbm, w_down), (dec_mt_hbm, dec_mt), (targets_hbm, targets_t))
        )
    ]
    for load in loads:
        load.start()
    pixels = dec_mt.shape[1]
    pred[...] = jnp.zeros(pred.shape, BF)
    scale = (2.0 / counted[0:1, 0:1]) * (1.0 / 3.0)
    tile = 512
    tiles = nodes // tile
    for s in range(samples):

        @pl.loop(0, tiles, unroll=True)
        def _(i):
            rows = pl.ds(pl.multiple_of(i * tile, tile), tile)
            flat = pl.ds(pl.multiple_of(s * nodes + i * tile, tile), tile)
            mid = h0[s, rows, :] + dot(attended[s, rows, :], w_out[...])
            h1[flat, :] = mid
            hat, _ = norm(mid)
            in_two = (hat * gains[1:2, :]).astype(BF)
            n2[flat, :] = in_two
            if s == 0:
                loads[0].wait()
                loads[1].wait()
            end = mid
            for c in range(4):
                cols = slice(c * D, (c + 1) * D)
                u = dot(in_two, w_up[:, cols])
                sig = sigmoid(u)
                upper[flat, cols] = slope(u, sig)
                a = (u * sig).astype(BF)
                act[flat, cols] = a
                end = end + dot(a, w_down[cols, :])
            h2[flat, :] = end
            hat, _ = norm(end)
            in_three = (hat * gains[2:3, :]).astype(BF)
            n3[flat, :] = in_three
            high, low = split(dot(in_three, w_dec[...]).T)
            pred[s * CP : s * CP + C_OUT, rows] = high
            pred[(samples + s) * CP : (samples + s) * CP + C_OUT, rows] = low

    loads[2].wait()
    loads[3].wait()
    d_pred[...] = jnp.zeros(d_pred.shape, F32)
    loss[...] = jnp.zeros(loss.shape, F32)

    @pl.loop(0, pixels // 512)
    def _(i):
        part = pl.ds(pl.multiple_of(i * 512, 512), 512)
        counts = dec_mt[:, part]
        y_all = dot(pred[...], counts)
        highs, lows = [], []
        for s in range(samples):
            y = y_all[s * CP : (s + 1) * CP] + y_all[(samples + s) * CP : (samples + s + 1) * CP]
            misfit = y * (1.0 / 3.0) - targets_t[s, :, part]
            g = weight[s : s + 1, part] * levels[...] * misfit
            loss[...] += jnp.sum(g * misfit, axis=0, keepdims=True)
            high, low = split(g * scale)
            highs.append(high)
            lows.append(low)
        d_pred[...] += dot_nt(jnp.concatenate(highs + lows, axis=0), counts)

    total_out[...] = jnp.zeros(total_out.shape, F32)
    d_dec[...] = jnp.zeros(d_dec.shape, F32)
    d_gains[...] = jnp.zeros(d_gains.shape, F32)
    for s in range(samples):
        total = d_pred[s * CP : (s + 1) * CP] + d_pred[(samples + s) * CP : (samples + s + 1) * CP]
        padded = jnp.concatenate([total, jnp.zeros((128 - CP, nodes), F32)], axis=0)
        d_y[...] = padded.T.astype(BF)

        @pl.loop(0, tiles, unroll=True)
        def _(i):
            rows = pl.ds(pl.multiple_of(i * tile, tile), tile)
            flat = pl.ds(pl.multiple_of(s * nodes + i * tile, tile), tile)
            d_part = d_y[rows, 0:C_OUT]
            d_dec[...] += dot_tn(n3[flat, :], d_part)
            grad = dot_nt(d_part, w_dec[...])
            hat, r = norm(h2[flat, :])
            d_gains[2:3, :] += jnp.sum(grad * hat, axis=0, keepdims=True)
            d_end = norm_back(grad, gains[2:3, :], hat, r)
            d_low = d_end.astype(BF)
            dm[flat, :] = d_low
            d_in = jnp.zeros((tile, D), F32)
            for c in range(4):
                cols = slice(c * D, (c + 1) * D)
                d_act = dot_nt(d_low, w_down[cols, :])
                d_u = (d_act * upper[flat, cols]).astype(BF)
                du[flat, cols] = d_u
                d_in = d_in + dot_nt(d_u, w_up[:, cols])
            hat, r = norm(h1[flat, :])
            d_gains[1:2, :] += jnp.sum(d_in * hat, axis=0, keepdims=True)
            d_mid = d_end + norm_back(d_in, gains[1:2, :], hat, r)
            dh1[s, rows, :] = d_mid
            total_out[...] += dot_tn(attended[s, rows, :], d_mid.astype(BF))

    def copies(name, source, action):
        window_copies(
            here, layout.rows, layout.plans[0][0][name], source, keep, send, sems, action
        )

    put_flat(d_out, total_out[...], 0, 4)
    copies("out", d_out, "start")
    for c in range(FF // D):
        cols = slice(c * D, (c + 1) * D)
        put_flat(d_up, dot_tn(n2[...], du[:, cols]), 4 * c, 16)
    copies("up", d_up, "start")
    for c in range(FF // D):
        cols = slice(c * D, (c + 1) * D)
        put_flat(d_down, dot_tn(act[:, cols], dm[...]), 4 * c * D, 4)
        copies(f"down{c}", d_down.at[pl.ds(4 * c * D, 4 * D), :], "start")
    copies("out", d_out, "wait")
    copies("up", d_up, "wait")
    for c in range(FF // D):
        copies(f"down{c}", d_down.at[pl.ds(4 * c * D, 4 * D), :], "wait")


def mlp(me, h0, attended, w_out, w_up, w_down, w_dec, gains, dec_mt, targets_t, weight, levels, counted, layout):
    samples, nodes, _ = h0.shape
    rows = samples * nodes
    count = layout.plans[0][1]
    sent = layout.sizes[0] if layout.fast else 8
    vmem = pl.BlockSpec(memory_space=pltpu.VMEM)
    hbm = pl.BlockSpec(memory_space=pl.ANY)
    return pl.pallas_call(
        functools.partial(mlp_body, layout),
        out_shape=[
            shape((samples, nodes, D)),
            shape((D, C_OUT)),
            shape((8, D)),
            shape((1, 512)),
            shape((layout.sizes[0], 128)),
            shape((sent, 128)),
        ],
        in_specs=[pl.BlockSpec(memory_space=pltpu.SMEM)] + [vmem] * 8 + [hbm] * 4,
        out_specs=[vmem] * 4 + [hbm] * 2,
        scratch_shapes=[
            pltpu.VMEM((rows, D), F32),
            pltpu.VMEM((rows, D), BF),
            pltpu.VMEM((rows, FF), F32),
            pltpu.VMEM((rows, FF), BF),
            pltpu.VMEM((rows, D), F32),
            pltpu.VMEM((rows, D), BF),
            pltpu.VMEM((2 * samples * CP, nodes), BF),
            pltpu.VMEM((2 * samples * CP, nodes), F32),
            pltpu.VMEM((rows, D), BF),
            pltpu.VMEM((rows, FF), BF),
            pltpu.VMEM((nodes, 128), BF),
            pltpu.VMEM((D, D), F32),
            pltpu.VMEM((4 * D, 128), F32),
            pltpu.VMEM((16 * D, 128), F32),
            pltpu.VMEM((4 * FF, 128), F32),
            pltpu.VMEM(w_up.shape, BF),
            pltpu.VMEM(w_down.shape, BF),
            pltpu.VMEM(dec_mt.shape, BF),
            pltpu.VMEM(targets_t.shape, F32),
            pltpu.SemaphoreType.DMA((count,)),
            pltpu.SemaphoreType.DMA((4,)),
        ],
        compiler_params=pltpu.CompilerParams(vmem_limit_bytes=60 << 20),
        cost_estimate=pl.CostEstimate(flops=16 << 30, bytes_accessed=24 << 20, transcendentals=0),
    )(me, h0, attended, w_out, w_dec, gains, weight, levels, counted, w_up, w_down, dec_mt, targets_t)


def attend_back_body(
    qkv, before, after, log_c, dh1, w_out,
    d_qkv, d_rims, d_before, d_after,
    pairs, do_both,
):
    samples, nodes, _ = dh1.shape
    halo = before.shape[1]
    for s in range(samples):
        gather_pairs(qkv, before, after, pairs, s)
        for i in range(nodes // 256):
            rows = slice(i * 256, (i + 1) * 256)
            da = dh1[s, rows, :].astype(BF)
            high, low = split(dot_nt(da, w_out[...]))
            for h in range(HEADS):
                lanes = slice(h * HEAD_DIM, (h + 1) * HEAD_DIM)
                do_both[rows, 2 * h * HEAD_DIM : (2 * h + 1) * HEAD_DIM] = high[:, lanes]
                do_both[rows, (2 * h + 1) * HEAD_DIM : (2 * h + 2) * HEAD_DIM] = low[:, lanes]
        for h in range(HEADS):
            lanes = slice(h * HEAD_DIM, (h + 1) * HEAD_DIM)
            vlanes = slice(D + h * HEAD_DIM, D + (h + 1) * HEAD_DIM)
            query = qkv[s, :, lanes]
            keys = pairs[:, lanes]
            values = pairs[:, vlanes]
            do = do_both[:, 2 * h * HEAD_DIM : (2 * h + 2) * HEAD_DIM]
            probs = attention_weights(keys, query, log_c)
            d_probs = dot_nt(jnp.concatenate([values, values], axis=1), do)
            centre = jnp.sum(probs * d_probs, 0, keepdims=True)
            high, low = split(probs * (d_probs - centre))
            dv2 = dot(probs.astype(BF), do)
            dv = dv2[:, :HEAD_DIM] + dv2[:, HEAD_DIM:]
            dk = (dot(high, query) + dot(low, query)) * SCALE
            dq_t = (dot_tn(keys, high) + dot_tn(keys, low)) * SCALE
            d_qkv[s, :, lanes] = dq_t.T.astype(BF)
            klanes = slice(D + h * HEAD_DIM, D + (h + 1) * HEAD_DIM)
            wide_lanes = slice(2 * D + h * HEAD_DIM, 2 * D + (h + 1) * HEAD_DIM)
            d_qkv[s, :, klanes] = dk[halo : halo + nodes].astype(BF)
            d_qkv[s, :, wide_lanes] = dv[halo : halo + nodes].astype(BF)
            for rim, first in ((0, halo), (1, nodes)):
                d_rims[s, rim, :, lanes] = dk[first : first + halo]
                d_rims[s, rim, :, vlanes] = dv[first : first + halo]
            d_before[s, :, lanes] = dk[:halo].astype(BF)
            d_before[s, :, vlanes] = dv[:halo].astype(BF)
            d_after[s, :, lanes] = dk[halo + nodes :].astype(BF)
            d_after[s, :, vlanes] = dv[halo + nodes :].astype(BF)


def attend_back(qkv, before, after, log_c, dh1, w_out):
    samples, nodes, _ = dh1.shape
    halo = before.shape[1]
    rim = by_sample(halo, 2 * D)
    return pl.pallas_call(
        attend_back_body,
        grid=(samples,),
        out_shape=[
            shape((samples, nodes, 3 * D), BF),
            shape((samples, 2, halo, 2 * D)),
            shape((samples, halo, 2 * D), BF),
            shape((samples, halo, 2 * D), BF),
        ],
        in_specs=[by_sample(nodes, 3 * D), rim, rim, same(*log_c.shape), by_sample(nodes, D), same(D, D)],
        out_specs=[by_sample(nodes, 3 * D), by_sample(2, halo, 2 * D), rim, rim],
        scratch_shapes=[pltpu.VMEM((log_c.shape[0], 2 * D), BF), pltpu.VMEM((nodes, 2 * D), BF)],
        compiler_params=pltpu.CompilerParams(vmem_limit_bytes=58 << 20),
        cost_estimate=pl.CostEstimate(flops=8 << 30, bytes_accessed=20 << 20, transcendentals=0),
    )(qkv, before, after, log_c, dh1, w_out)


def encode_back_body(
    layout, samples,
    me, grid, w_enc, enc_mt, w_qkv, gains, h0, dh1, d_in, d_rims, from_lower, from_upper, d_dec, d_gains,
    keep, send,
    both, dqkv, n1, d_gain, total, total_enc, d_qkv, d_enc, small, sems,
):
    nodes, halo, pixels = h0.shape[1], from_lower.shape[1], grid.shape[2]
    step = pl.program_id(0)
    first, final = step == 0, step == samples - 1

    def copies(name, source, action):
        window_copies(
            me[0], layout.rows, layout.plans[1][0][name], source, keep, send, sems, action
        )

    @pl.when(first)
    def _():
        d_gain[...] = d_gains[...]
        total[...] = jnp.zeros(total.shape, F32)
        total_enc[...] = jnp.zeros(total_enc.shape, F32)

    dqkv[...] = d_in[0]
    low_rim = d_rims[0, 0] + from_lower[0].astype(F32)
    dqkv[0:halo, D:] = low_rim.astype(BF)
    high_rim = d_rims[0, 1] + from_upper[0].astype(F32)
    dqkv[nodes - halo :, D:] = high_rim.astype(BF)
    hat, r = norm(h0[0])
    n1[...] = (hat * gains[0:1, :]).astype(BF)
    grad = dot_nt(dqkv[...], w_qkv[...])
    d_gain[0:1, :] += jnp.sum(grad * hat, axis=0, keepdims=True)
    d_start = dh1[0] + norm_back(grad, gains[0:1, :], hat, r)
    high, low = split(d_start * 0.25)
    both[:, 0:D] = high
    both[:, D:] = low
    for c in range(3):
        total[c] += dot_tn(n1[...], dqkv[:, c * D : (c + 1) * D])

    @pl.when(final)
    def _():
        small[0 : 4 * C_OUT, :] = d_dec[...]
        small[4 * C_OUT :, :] = jnp.zeros((small.shape[0] - 4 * C_OUT, 128), F32)
        for k in range(3):
            for lane in range(D // 128):
                row = 4 * (C_OUT + k) + lane
                small[row : row + 1, :] = d_gain[k : k + 1, lane * 128 : lane * 128 + 128]
        copies("small", small, "start")
        for c in range(3):
            put_flat(d_qkv, total[c], 4 * c, 12)
        copies("qkv", d_qkv, "start")

    for i in range(pixels // 512):
        rows = slice(i * 512, (i + 1) * 512)
        x_t = grid[0, :, rows]
        pre = dot_tn(x_t, w_enc[...])
        spread2 = dot(enc_mt[rows, :], both[...])
        spread = spread2[:, 0:D] + spread2[:, D:]
        d_pre = (spread * slope(pre, sigmoid(pre))).astype(BF)
        total_enc[...] += dot(x_t, d_pre)

    @pl.when(final)
    def _():
        put_flat(d_enc, total_enc[...], 0, 4)
        copies("enc", d_enc, "start")
        copies("small", small, "wait")
        copies("qkv", d_qkv, "wait")
        copies("enc", d_enc, "wait")


def encode_back(me, grid, w_enc, enc_mt, w_qkv, gains, h0, dh1, d_in, d_rims, from_lower, from_upper,
                d_dec, d_gains, layout):
    samples, nodes, _ = h0.shape
    halo, pixels = from_lower.shape[1], grid.shape[2]
    rim = by_sample(halo, 2 * D)
    return pl.pallas_call(
        functools.partial(encode_back_body, layout, samples),
        grid=(samples,),
        out_shape=[
            shape((layout.sizes[1], 128)),
            shape((layout.sizes[1] if layout.fast else 8, 128)),
        ],
        in_specs=[
            SCALAR,
            by_sample(C_IN, pixels),
            same(C_IN, D),
            same(*enc_mt.shape),
            same(*w_qkv.shape),
            same(8, D),
            by_sample(nodes, D),
            by_sample(nodes, D),
            by_sample(nodes, 3 * D),
            by_sample(2, halo, 2 * D),
            rim,
            rim,
            same(*d_dec.shape),
            same(8, D),
        ],
        out_specs=[HBM, HBM],
        scratch_shapes=[
            pltpu.VMEM((nodes, 2 * D), BF),
            pltpu.VMEM((nodes, 3 * D), BF),
            pltpu.VMEM((nodes, D), BF),
            pltpu.VMEM((8, D), F32),
            pltpu.VMEM((3, D, D), F32),
            pltpu.VMEM((C_IN, D), F32),
            pltpu.VMEM((12 * D, 128), F32),
            pltpu.VMEM((4 * C_IN, 128), F32),
            pltpu.VMEM((layout.small, 128), F32),
            pltpu.SemaphoreType.DMA((layout.plans[1][1],)),
        ],
        compiler_params=pltpu.CompilerParams(vmem_limit_bytes=58 << 20),
        cost_estimate=pl.CostEstimate(flops=16 << 30, bytes_accessed=24 << 20, transcendentals=0),
    )(me, grid, w_enc, enc_mt, w_qkv, gains, h0, dh1, d_in, d_rims, from_lower, from_upper, d_dec, d_gains)


def ring(axis, distance):
    count = lax.axis_size(axis)
    return [(i, (i + distance) % count) for i in range(count)]


def window_plan(shard, count):
    starts = [(LEAD * D + d * shard) // (16 * D) * 16 for d in range(count)]
    ends = [-(-(LEAD * D + (d + 1) * shard) // D) for d in range(count)]
    rows = max(-(-(e - s + 1) // 16) * 16 for s, e in zip(starts, ends))
    return starts, rows


def per_device(
    grid, targets, area, sigma_weight, level_weight, valid, enc_index, dec_index, neighbours,
    params, first_moment, second_moment, average,
):
    shard = params.shape[0]
    devices = lax.axis_size(AXES)
    me = lax.axis_index(AXES)
    fast = (lax.axis_size("patch"), lax.axis_size("dp")) == (8, 4)
    layout = Layout(shard, devices, fast)
    starts, win = layout.starts, layout.win
    begin = LEAD * D + me * shard
    shift = begin - begin // (16 * D) * (16 * D)
    place = me.astype(jnp.int32).reshape(1)

    lane_counts = jnp.sum(valid.reshape(-1, D), axis=0).astype(BF)
    payload = lax.dynamic_update_slice(jnp.zeros((win * D,), BF), params.astype(BF), (shift,))
    payload = lax.dynamic_update_slice(payload, lane_counts, ((win - 1) * D,)).reshape(win, D)
    weight = valid.astype(F32) * area[None, :] * sigma_weight[:, None]
    levels = jnp.pad(level_weight, (0, CP - C_OUT)).reshape(CP, 1)
    pixels = dec_index.shape[0]
    first_work = lambda: count_encoder(enc_index, pixels)
    local_count = jnp.sum(valid).astype(F32)

    def second_work(dec_index, neighbours, targets):
        return count_rest(dec_index, neighbours, targets), weight, levels

    def third_work(params):
        positions = me * shard + lax.iota(jnp.int32, shard)
        bounds = segment_bounds() + [(-1, -1)]
        lower = jnp.array([x for x, _ in bounds], jnp.int32)[:, None]
        upper = jnp.array([x for _, x in bounds], jnp.int32)[:, None]
        member = ((positions >= lower) & (positions < upper)).astype(F32)
        return member, jnp.sum(member * (params * params)[None, :], axis=1)

    second_inputs, third_inputs = (dec_index, neighbours, targets), (params,)
    if fast:
        pieces, plan, first_done, second_done, third_done = gather_windows(
            payload, first_work, second_work, second_inputs, third_work, third_inputs
        )
        place_of = place_by_xor
    else:
        everything = lax.all_gather(payload, AXES, axis=0, tiled=False)
        pieces = [everything.reshape(devices * win, D)]
        plan = [(0, d * win, d, 0, win) for d in range(devices)]
        place_of = lambda here, d: d
        first_done, second_done = first_work(), second_work(*second_inputs)
        third_done = third_work(*third_inputs)
    member, old_sums = third_done
    enc_m, enc_mt = first_done
    (dec_mt, log_c, targets_t), weight, levels = second_done
    grid = jnp.swapaxes(grid, 1, 2)

    w_enc, w_qkv, gains = unpack(
        place, pieces, plan, ("enc", "qkv", "gains"), place_of, devices, win, starts
    )
    h0, qkv, leading, last = encode(grid, w_enc, enc_m, w_qkv, gains)
    before = lax.ppermute(last, "patch", ring("patch", 1))
    after = lax.ppermute(leading, "patch", ring("patch", -1))
    w_out, w_up, w_down, w_dec, counted = unpack(
        place, pieces, plan, ("out", "up", "down", "dec", "count"), place_of, devices, win, starts
    )
    w_dec = w_dec.reshape(D, C_OUT)
    attended = attend(qkv, before, after, log_c)
    dh1, d_dec, d_gains, loss_rows, keep, send = mlp(
        place, h0, attended, w_out, w_up, w_down, w_dec, gains, dec_mt, targets_t, weight, levels,
        counted, layout,
    )
    back = attend_back(qkv, before, after, log_c, dh1, w_out)
    if fast:
        other = permute(send, 1)
        other, back = lax.optimization_barrier((other, back))
    d_qkv, d_rims, d_before, d_after = back
    from_upper = lax.ppermute(d_before, "patch", ring("patch", -1))
    from_lower = lax.ppermute(d_after, "patch", ring("patch", 1))
    d_dec = d_dec.reshape(4 * C_OUT, 128)
    if fast:
        send_a, send_b = first_send(keep, other, layout)
        got = permute(send_a, 2), permute(send_b, 4)
        send_a, send_b, d_dec, from_upper, from_lower = lax.optimization_barrier(
            (send_a, send_b, d_dec, from_upper, from_lower)
        )
    second = encode_back(
        place, grid, w_enc, enc_mt, w_qkv, gains, h0, dh1, d_qkv, d_rims, from_lower, from_upper,
        d_dec, d_gains, layout,
    )
    if fast:
        second, got = lax.optimization_barrier((second, got))
        keep_a, send_a, keep_b, send_b = second_send(keep, other, *got, layout)
        got = permute(send_a, 4), permute(send_b, 2)
        grad_window = sum_rest((keep_a, keep_b), got, second, layout, me)
    else:
        grad_window = sum_flat(keep, second[0], layout)
    grad = lax.dynamic_slice(grad_window.reshape(-1), (begin - begin // 1024 * 1024,), (shard,))

    new_first = BETA_ONE * first_moment + (1.0 - BETA_ONE) * grad
    new_second = BETA_TWO * second_moment + (1.0 - BETA_TWO) * grad * grad
    update = (
        new_first
        / (1.0 - BETA_ONE**STEP)
        / (jnp.sqrt(new_second / (1.0 - BETA_TWO**STEP)) + LAMB_EPS)
        + DECAY * params
    )
    sums = jnp.stack([old_sums, jnp.sum(member * (update * update)[None, :], axis=1)])
    own = jnp.stack([jnp.sum(loss_rows), local_count])[:, None]
    sums = jnp.where(jnp.arange(8)[None, :] == 7, own, sums)
    totals = sum_everywhere(sums, fast)
    norms = jnp.sqrt(totals[:, :7])
    step_ratio = jnp.sum(member[:7] * (norms[0] / norms[1])[:, None], axis=0)
    new_params = params - RATE * step_ratio * update
    new_average = EMA_KEEP * average + (1.0 - EMA_KEEP) * new_params
    return (
        totals[:, 7],
        norms,
        new_params,
        new_first,
        new_second,
        new_average,
    )


def solution(mesh):
    flat = P(AXES)
    in_specs = (
        P("dp", "patch", None),
        P("dp", "patch", None),
        P("patch"),
        P("dp"),
        P(),
        P("dp", "patch"),
        P("patch", None),
        P("patch", None),
        P("patch", None),
        flat,
        flat,
        flat,
        flat,
    )
    out_specs = (P(), P(), flat, flat, flat, flat)
    return jax.shard_map(
        per_device, mesh=mesh, in_specs=in_specs, out_specs=out_specs, check_vma=False
    )
```

```python
import functools
import math

import jax
import jax.numpy as jnp
from jax import lax
from jax.experimental import pallas as pl
from jax.experimental.pallas import tpu as pltpu
from jax.sharding import PartitionSpec as P

D = 512
HEADS = 4
HEAD_DIM = 128
FF = 2048
C_OUT = 84
C_IN = 264
STEP = 10
EPS_NORM = 1e-05
BETA_ONE = 0.9
BETA_TWO = 0.999
LAMB_EPS = 1e-06
DECAY = 0.01
RATE = 0.2
EMA_KEEP = 0.8
BF = jnp.bfloat16
F32 = jnp.float32
SCALE = HEAD_DIM ** (-0.5)
LOG2E = 1.4426950408889634
ABSENT = -1e30
CP = 96
AXES = ("patch", "dp")

LEAD = 8
ROW_ENC = LEAD
ROW_QKV = ROW_ENC + C_IN
ROW_OUT = ROW_QKV + 3 * D
ROW_UP = ROW_OUT + D
ROW_DOWN = ROW_UP + 4 * D
ROW_DEC = ROW_DOWN + FF
ROW_GAIN = ROW_DEC + C_OUT
ROW_END = ROW_GAIN + 3
ROWS_ALL = -(-ROW_END // 16) * 16


def matrix_shapes():
    return [(C_IN, D), (D, 3 * D), (D, D), (D, FF), (FF, D), (D, C_OUT), (3, D)]


def segment_bounds():
    bounds = []
    offset = 0
    for row_count, col_count in matrix_shapes():
        bounds.append((offset, offset + row_count * col_count))
        offset += row_count * col_count
    return bounds


NPARAM_USED = segment_bounds()[-1][1]


def dot(a, b):
    return lax.dot_general(a, b, (((1,), (0,)), ((), ())), preferred_element_type=F32)


def dot_nt(a, b):
    return lax.dot_general(a, b, (((1,), (1,)), ((), ())), preferred_element_type=F32)


def dot_tn(a, b):
    return lax.dot_general(a, b, (((0,), (0,)), ((), ())), preferred_element_type=F32)


def split(x):
    high = x.astype(BF)
    return high, (x - high.astype(F32)).astype(BF)


def sigmoid(x):
    return 0.5 * jnp.tanh(0.5 * x) + 0.5


def slope(x, s):
    return s * (1.0 + x * (1.0 - s))


def norm(x):
    c = x - jnp.mean(x, -1, keepdims=True)
    r = lax.rsqrt(jnp.mean(c * c, -1, keepdims=True) + EPS_NORM)
    return c * r, r


def norm_back(grad, gain, hat, r):
    g = grad * gain
    return r * (
        g
        - jnp.mean(g, -1, keepdims=True)
        - hat * jnp.mean(g * hat, -1, keepdims=True)
    )


def put_flat(ref, value, first, period):
    for lane in range(D // 128):
        ref[pl.ds(first + lane, value.shape[0], stride=period), :] = value[
            :, lane * 128 : lane * 128 + 128
        ]


def lane_pieces(begin, size, width):
    pieces = []
    while size > 0:
        row, lane = begin // width, begin % width
        count = min(width - lane, size)
        pieces.append((row, lane, count))
        begin, size = begin + count, size - count
    return pieces


PERIOD = 128 // math.gcd(128, C_OUT)
FLAT_PERIOD = PERIOD * C_OUT // 128
GROUPS = D // PERIOD


def narrow_to_flat(narrow, flat):
    for r in range(FLAT_PERIOD):
        parts = [
            narrow[pl.ds(row, GROUPS, stride=PERIOD), :][:, lane : lane + count]
            for row, lane, count in lane_pieces(128 * r, 128, C_OUT)
        ]
        flat[pl.ds(r, GROUPS, stride=FLAT_PERIOD), :] = jnp.concatenate(parts, axis=1)


def flat_to_narrow(flat, narrow):
    for b in range(PERIOD):
        parts = [
            flat[pl.ds(row, GROUPS, stride=FLAT_PERIOD), :][:, lane : lane + count]
            for row, lane, count in lane_pieces(C_OUT * b, C_OUT, 128)
        ]
        parts.append(jnp.zeros((GROUPS, 128 - C_OUT), F32))
        narrow[pl.ds(b, GROUPS, stride=PERIOD), :] = jnp.concatenate(parts, axis=1)


def kernel_call(body, out_shape, scratch=(), flops=0, nbytes=0):
    return pl.pallas_call(
        body,
        out_shape=out_shape,
        scratch_shapes=list(scratch),
        compiler_params=pltpu.CompilerParams(vmem_limit_bytes=58 << 20),
        cost_estimate=pl.CostEstimate(flops=flops, bytes_accessed=nbytes, transcendentals=0),
    )


def by_sample(*dims):
    return pl.BlockSpec((1,) + dims, lambda s: (s,) + (0,) * len(dims))


def same(*dims):
    return pl.BlockSpec(dims, lambda s: (0,) * len(dims))


HBM = pl.BlockSpec(memory_space=pl.ANY)
SCALAR = pl.BlockSpec(memory_space=pltpu.SMEM)


def shape(dims, dtype=F32):
    return jax.ShapeDtypeStruct(tuple(dims), dtype)


def count_rows(index_t, base, rows, cols):
    ids = lax.broadcasted_iota(jnp.int32, (rows, cols), 0) + base
    total = jnp.zeros((rows, cols), F32)
    for k in range(index_t.shape[0]):
        total = total + jnp.where(index_t[k : k + 1, :] == ids, 1.0, 0.0)
    return total


def count_encoder_body(enc, enc_t, enc_m, enc_mt):
    nodes, pixels = enc_m.shape

    @pl.loop(0, nodes // 32)
    def _(i):
        rows = pl.ds(pl.multiple_of(i * 32, 32), 32)
        index = enc[rows, :]
        ids = lax.broadcasted_iota(jnp.int32, (32, pixels), 1)
        total = jnp.zeros((32, pixels), F32)
        for k in range(index.shape[1]):
            total = total + jnp.where(index[:, k : k + 1] == ids, 1.0, 0.0)
        enc_m[rows, :] = total.astype(BF)

    @pl.loop(0, pixels // 64)
    def _(i):
        rows = pl.ds(pl.multiple_of(i * 64, 64), 64)
        enc_mt[rows, :] = count_rows(enc_t, i * 64, 64, nodes).astype(BF)


def count_rest_body(dec_t, nbr_t, targets, dec_mt, log_c, targets_t):
    nodes, pixels = dec_mt.shape

    @pl.loop(0, nodes // 32)
    def _(i):
        rows = pl.ds(pl.multiple_of(i * 32, 32), 32)
        dec_mt[rows, :] = count_rows(dec_t, i * 32, 32, pixels).astype(BF)

    @pl.loop(0, log_c.shape[0] // 64)
    def _(i):
        rows = pl.ds(pl.multiple_of(i * 64, 64), 64)
        total = count_rows(nbr_t, i * 64, 64, nodes)
        log_c[rows, :] = jnp.where(total > 0.0, jnp.log2(jnp.maximum(total, 1.0)), ABSENT)

    for s in range(targets.shape[1]):
        targets_t[s, 0:C_OUT, :] = targets[:, s, :]
        targets_t[s, C_OUT:, :] = jnp.zeros((CP - C_OUT, pixels), F32)


def count_encoder(enc_index, pixels):
    nodes = enc_index.shape[0]
    return kernel_call(
        count_encoder_body,
        [shape((nodes, pixels), BF), shape((pixels, nodes), BF)],
        nbytes=5 << 20,
        flops=1 << 29,
    )(enc_index, enc_index.T)


def count_rest(dec_index, neighbours, targets):
    nodes, pixels = neighbours.shape[0], dec_index.shape[0]
    ext = nodes + 2 * (nodes // 16)
    return kernel_call(
        count_rest_body,
        [shape((nodes, pixels), BF), shape((ext, nodes)), shape((targets.shape[1], CP, pixels))],
        nbytes=8 << 20,
        flops=1 << 29,
    )(dec_index.T, neighbours.T, targets)


def tile_sources(starts, rows):
    return [
        [(d, tile * 16 - s) for d, s in enumerate(starts) if s <= tile * 16 < s + rows]
        for tile in range(ROWS_ALL // 16)
    ]


def assemble(read, window_rows, sources, first_row, rows, put):
    tile, last = first_row // 16, (first_row + rows) // 16
    while tile < last:
        source = sources[tile]
        if len(source) == 1:
            count = 1
            while (
                tile + count < last
                and len(sources[tile + count]) == 1
                and sources[tile + count][0][0] == source[0][0]
                and count < 8
            ):
                count += 1
            d, off = source[0]
            value = read(d, off, 16 * count)
        else:
            count = 1
            value = None
            for d, off in source:
                part = read(d, off, 16).astype(F32)
                if off + 16 == window_rows:
                    part = jnp.where(
                        lax.broadcasted_iota(jnp.int32, part.shape, 0) < 15, part, 0.0
                    )
                value = part if value is None else value + part
            value = value.astype(BF)
        put(tile * 16 - first_row, value)
        tile += count


def wide(stage, ref, period):
    for lane in range(D // 128):
        for c in range(period):
            lanes = slice(c * D + lane * 128, c * D + lane * 128 + 128)
            ref[:, lanes] = stage[lane, pl.ds(c, ref.shape[0], stride=period), :].astype(BF)


def unpack_body(plan, parts, sources, place_of, owner_of, count, *refs):
    me, pieces, refs = refs[0], refs[1 : count + 1], refs[count + 1 :]
    outs, (windows, stage, flat, narrow, sems) = refs[: len(parts)], refs[len(parts) :]
    here = me[0]
    used = set()
    for part in parts:
        if part == "count":
            used = set(range(windows.shape[0]))
        else:
            row, rows = PARTS[part][:2]
            used |= {d for source in sources[row // 16 : (row + rows) // 16] for d, _ in source}
    ranges = [d for d in sorted(used) if d - 1 not in used], [d for d in sorted(used) if d + 1 not in used]
    for piece, at, slot, to, rows in plan:
        copy = pltpu.make_async_copy(
            pieces[piece].at[pl.ds(at, rows), :], windows.at[slot, pl.ds(to, rows), :], sems.at[slot]
        )
        owner = owner_of(here, slot)
        needed = functools.reduce(
            jnp.logical_or, [(owner >= lo) & (owner <= hi) for lo, hi in zip(*ranges)]
        )
        if len(used) == windows.shape[0]:
            copy.start()
        else:
            pl.when(needed)(copy.start)
    window_rows = windows.shape[1]
    waited = set()

    def wait_for(d):
        if d not in waited:
            waited.add(d)
            slot = place_of(here, d)
            pltpu.make_async_copy(windows.at[slot], windows.at[slot], sems.at[slot]).wait()

    def read(d, off, rows):
        wait_for(d)
        return windows[place_of(here, d), off : off + rows, :]

    for part, ref in zip(parts, outs):
        if part == "count":
            for d in range(windows.shape[0]):
                wait_for(d)
            total = jnp.sum(windows[:, window_rows - 16 :, :].astype(F32), axis=0)[15:16, :]
            ref[...] = jnp.sum(total, axis=1, keepdims=True) + jnp.zeros((8, 128), F32)
            continue
        first, rows, period, _ = PARTS[part]

        def direct(off, value):
            ref[off : off + value.shape[0], :] = value

        def staged(off, value):
            wide_value = value.astype(F32)
            for lane in range(D // 128):
                stage[lane, off : off + value.shape[0], :] = wide_value[
                    :, lane * 128 : lane * 128 + 128
                ]

        if part == "gains":
            assemble(read, window_rows, sources, first, rows, staged)
            row = ROW_GAIN - first
            for lane in range(D // 128):
                ref[:, lane * 128 : lane * 128 + 128] = stage[lane, row : row + 8, :]
        elif period == 1:
            assemble(read, window_rows, sources, first, rows, direct)
        else:
            assemble(read, window_rows, sources, first, rows, staged)
            if part == "enc":
                for lane in range(D // 128):
                    lanes = slice(lane * 128, lane * 128 + 128)
                    ref[:, lanes] = stage[lane, LEAD:ROW_QKV, :].astype(BF)
            elif part == "dec":
                row = ROW_DEC - first
                for lane in range(D // 128):
                    flat[pl.ds(lane, C_OUT, stride=4), :] = stage[lane, row : row + C_OUT, :]
                flat_to_narrow(flat, narrow)
                ref[...] = narrow[:, 0:C_OUT].astype(BF)
            else:
                wide(stage, ref, period)


PARTS = {
    "enc": (0, ROW_QKV, 0, (C_IN, D)),
    "qkv": (ROW_QKV, 3 * D, 3, (D, 3 * D)),
    "out": (ROW_OUT, D, 1, (D, D)),
    "up": (ROW_UP, 4 * D, 4, (D, FF)),
    "down": (ROW_DOWN, FF, 1, (FF, D)),
    "dec": (ROW_DEC // 16 * 16, -(-ROW_GAIN // 16) * 16 - ROW_DEC // 16 * 16, 0, (D, C_OUT)),
    "gains": (ROW_GAIN // 16 * 16, 16, 0, (8, D)),
}


def unpack(me, pieces, plan, parts, place_of, slots, rows, starts):
    sources = tile_sources(starts, rows)
    outs = [
        shape((8, 128)) if p == "count" else shape(PARTS[p][3], F32 if p == "gains" else BF)
        for p in parts
    ]
    return pl.pallas_call(
        functools.partial(unpack_body, plan, parts, sources, place_of, place_of, len(pieces)),
        out_shape=outs,
        in_specs=[pl.BlockSpec(memory_space=pltpu.SMEM)]
        + [pl.BlockSpec(memory_space=pl.ANY)] * len(pieces),
        scratch_shapes=[
            pltpu.VMEM((slots, rows, D), BF),
            pltpu.VMEM((D // 128, 4 * D, 128), F32),
            pltpu.VMEM((4 * C_OUT, 128), F32),
            pltpu.VMEM((D, 128), F32),
            pltpu.SemaphoreType.DMA((slots,)),
        ],
        compiler_params=pltpu.CompilerParams(vmem_limit_bytes=58 << 20),
        cost_estimate=pl.CostEstimate(
            flops=0, bytes_accessed=slots * rows * D * 4, transcendentals=0
        ),
    )(me, *pieces)


def permute(x, mask):
    count = lax.axis_size(AXES)
    return lax.ppermute(x, AXES, [(d, d ^ mask) for d in range(count)])


def place_by_xor(here, d):
    return jnp.bitwise_xor(here, d)


def gather_windows(window, first_work, second_work, second_inputs, third_work, third_inputs):
    rows = window.shape[0]
    half = rows // 2
    pieces, plan = [], []

    def add(piece, near, parts):
        for part, flip in ((piece, 0), (permute(piece, 1), 1)):
            for at, slot, to, size in parts:
                plan.append((len(pieces), at, slot ^ near ^ flip, to, size))
            pieces.append(part)

    planes = (8, 16, 24)
    others = [permute(window, m) for m in planes]
    by_x, by_y = permute(window, 2), permute(window, 4)
    first_done = first_work()
    others, by_x, by_y, first_done, second_inputs = lax.optimization_barrier(
        (jnp.concatenate(others), by_x, by_y, first_done, second_inputs)
    )
    others_x, others_y = permute(others, 2), permute(others, 4)
    second_done = second_work(*second_inputs)
    others_x, others_y, second_done, third_inputs = lax.optimization_barrier(
        (others_x, others_y, second_done, third_inputs)
    )

    def halves(near_part, far_part, first):
        far = [far_part[i * rows + first : i * rows + first + half] for i in range(3)]
        return jnp.concatenate([near_part[first : first + half]] + far)

    across_a = permute(halves(by_y, others_y, 0), 2)
    across_b = permute(halves(by_x, others_x, half), 4)
    across_a, across_b, third_done = lax.optimization_barrier(
        (across_a, across_b, third_work(*third_inputs))
    )
    whole = [(0, 0, 0, rows)]
    stacked = [(i * rows, slot, 0, rows) for i, slot in enumerate(planes)]
    add(window, 0, whole)
    add(by_x, 2, whole)
    add(by_y, 4, whole)
    add(others, 0, stacked)
    add(others_x, 2, stacked)
    add(others_y, 4, stacked)
    add(across_a, 6, [(i * half, slot, 0, half) for i, slot in enumerate((0,) + planes)])
    add(across_b, 6, [(i * half, slot, half, half) for i, slot in enumerate((0,) + planes)])
    return pieces, plan, first_done, second_done, third_done


def encode_body(grid, w_enc, enc_hbm, w_hbm, gains, h0, qkv, leading, last, high, low, enc_m, w_qkv, sems):
    pixels, nodes, halo = grid.shape[2], h0.shape[1], last.shape[1]
    first = pl.program_id(0) == 0
    loads = [
        pltpu.make_async_copy(enc_hbm, enc_m, sems.at[0]),
        pltpu.make_async_copy(w_hbm, w_qkv, sems.at[1]),
    ]
    for load in loads:
        pl.when(first)(load.start)
    for i in range(pixels // 512):
        rows = slice(i * 512, (i + 1) * 512)
        pre = dot_tn(grid[0, :, rows], w_enc[...])
        high[rows, :], low[rows, :] = split(pre * sigmoid(pre))
    for load in loads:
        pl.when(first)(load.wait)
    start = (dot(enc_m[...], high[...]) + dot(enc_m[...], low[...])) * 0.25
    h0[0] = start
    hat, _ = norm(start)
    n1 = (hat * gains[0:1, :]).astype(BF)
    qkv[0] = dot(n1, w_qkv[...]).astype(BF)
    leading[0] = qkv[0, 0:halo, D:]
    last[0] = qkv[0, nodes - halo :, D:]


def encode(grid, w_enc, enc_m, w_qkv, gains):
    samples, pixels = grid.shape[0], grid.shape[2]
    nodes = enc_m.shape[0]
    halo = nodes // 16
    return pl.pallas_call(
        encode_body,
        grid=(samples,),
        out_shape=[shape((samples, nodes, D)), shape((samples, nodes, 3 * D), BF)]
        + [shape((samples, halo, 2 * D), BF)] * 2,
        in_specs=[by_sample(C_IN, pixels), same(C_IN, D), HBM, HBM, same(8, D)],
        out_specs=[by_sample(nodes, D), by_sample(nodes, 3 * D)] + [by_sample(halo, 2 * D)] * 2,
        scratch_shapes=[
            pltpu.VMEM((pixels, D), BF),
            pltpu.VMEM((pixels, D), BF),
            pltpu.VMEM(enc_m.shape, BF),
            pltpu.VMEM(w_qkv.shape, BF),
            pltpu.SemaphoreType.DMA((2,)),
        ],
        compiler_params=pltpu.CompilerParams(vmem_limit_bytes=58 << 20),
        cost_estimate=pl.CostEstimate(flops=8 << 30, bytes_accessed=12 << 20, transcendentals=0),
    )(grid, w_enc, enc_m, w_qkv, gains)


def gather_pairs(qkv, before, after, pairs, s):
    halo, nodes = before.shape[1], qkv.shape[1]
    pairs[0:halo, :] = before[s]
    pairs[halo : halo + nodes, :] = qkv[s, :, D:]
    pairs[halo + nodes :, :] = after[s]


def attention_weights(keys, query, log_c):
    x = dot_nt(keys, query) * (SCALE * LOG2E) + log_c[...]
    e = jnp.exp2(x - jnp.max(x, 0, keepdims=True))
    return e * (1.0 / jnp.sum(e, 0, keepdims=True))


def attend_body(qkv, before, after, log_c, out, pairs):
    for s in range(qkv.shape[0]):
        gather_pairs(qkv, before, after, pairs, s)
        for h in range(HEADS):
            lanes = slice(h * HEAD_DIM, (h + 1) * HEAD_DIM)
            keys = pairs[:, lanes]
            values = pairs[:, D + h * HEAD_DIM : D + (h + 1) * HEAD_DIM]
            probs = attention_weights(keys, qkv[s, :, lanes], log_c)
            out_t = dot_tn(values, probs.astype(BF))
            out[s, :, lanes] = out_t.T.astype(BF)


def attend(qkv, before, after, log_c):
    samples, nodes = qkv.shape[:2]
    halo = before.shape[1]
    return pl.pallas_call(
        attend_body,
        grid=(samples,),
        out_shape=shape((samples, nodes, D), BF),
        in_specs=[
            by_sample(nodes, 3 * D),
            by_sample(halo, 2 * D),
            by_sample(halo, 2 * D),
            same(*log_c.shape),
        ],
        out_specs=by_sample(nodes, D),
        scratch_shapes=[pltpu.VMEM((log_c.shape[0], 2 * D), BF)],
        compiler_params=pltpu.CompilerParams(vmem_limit_bytes=58 << 20),
        cost_estimate=pl.CostEstimate(flops=2 << 30, bytes_accessed=8 << 20, transcendentals=0),
    )(qkv, before, after, log_c)


class Layout:
    def __init__(self, shard, devices, fast):
        self.devices = devices
        self.starts, self.win = window_plan(shard, devices)
        self.begins = [(LEAD * D + d * shard) // 1024 * 8 for d in range(devices)]
        self.ends = [-(-(LEAD * D + (d + 1) * shard) // 1024) * 8 for d in range(devices)]
        self.rows = -(-max(e - b for b, e in zip(self.begins, self.ends)) // 32) * 32
        self.small = 4 * (ROW_END - ROW_DEC) + 4
        first = (("out", ROW_OUT, 4 * D), ("up", ROW_UP, 16 * D)) + tuple(
            (f"down{c}", ROW_DOWN + c * D, 4 * D) for c in range(FF // D)
        ) + (("small", ROW_DEC, self.small),)
        second = (("enc", ROW_ENC, 4 * C_IN), ("qkv", ROW_QKV, 12 * D), ("gain", ROW_GAIN, 8))
        self.fast = fast
        if fast:
            self.apart = 4 * ROW_OUT - self.begins[8]
            extra = -(-(self.apart + 8) // 32) * 32
            self.sizes = (12 * self.rows, 4 * self.rows + extra)
        else:
            self.sizes = (sum(x[2] for x in first), sum(x[2] for x in second))
        self.plans = self.make(first, 1), self.make(second, 0)

    def make(self, arrays, plane):
        plans, k, at = {}, 0, 0
        for name, row, size in arrays:
            plans[name] = []
            if not self.fast:
                plans[name].append((k, None, at, 0, size))
                k, at = k + 1, at + size
                continue
            if name == "gain":
                plans[name].append((k, "both", 4 * self.rows + self.apart, 0, size))
                k += 2
                continue
            for d, (lower, upper) in enumerate(zip(self.begins, self.ends)):
                low, high = max(lower, 4 * row), min(upper, 4 * (row + size // 4))
                if low >= high:
                    continue
                if d == 8 and plane == 0:
                    to = 4 * self.rows + low - lower
                    plans[name].append((k, "both", to, low - 4 * row, high - low))
                    k += 2
                else:
                    place = (d // 8 - plane) * 4 * self.rows + low - lower
                    plans[name].append((k, d % 8, place, low - 4 * row, high - low))
                    k += 1
        return plans, k


def window_copies(here, rows_of_slot, blocks, source, keep, send, sems, action):
    for k, near, to, at, rows in blocks:

        def copy(target, first, sem):
            getattr(
                pltpu.make_async_copy(
                    source.at[pl.ds(at, rows), :], target.at[pl.ds(first, rows), :], sems.at[sem]
                ),
                action,
            )()

        if near is None:
            copy(keep, to, k)
        elif near == "both":
            copy(keep, to, k)
            copy(send, to, k + 1)
        else:
            slot = jnp.bitwise_and(jnp.bitwise_xor(here, near), 7)
            first = pl.multiple_of(lax.shift_right_logical(slot, 1) * rows_of_slot + to, 8)
            for target, side in ((keep, 0), (send, 1)):

                @pl.when(jnp.bitwise_and(slot, 1) == side)
                def _():
                    copy(target, first, k)


def sum_flat(first, second, layout):
    flat = jnp.concatenate(
        [
            jnp.zeros((4 * LEAD, 128), F32),
            second[: 4 * (ROW_OUT - LEAD)],
            first,
            jnp.zeros((max(0, layout.begins[-1] + layout.rows - 4 * ROW_DEC - layout.small), 128), F32),
        ]
    )
    gain = second[4 * (ROW_OUT - LEAD) :]
    flat = lax.dynamic_update_slice(
        flat, gain[0:4] + flat[4 * ROW_GAIN : 4 * ROW_GAIN + 4], (4 * ROW_GAIN, 0)
    )
    windows = jnp.concatenate([flat[b : b + layout.rows] for b in layout.begins])
    return lax.psum_scatter(windows, AXES, scatter_dimension=0, tiled=True)


def low(x):
    return x.astype(BF)


def packed(blocks, extra):
    return low(jnp.concatenate([blocks.reshape(-1, 128), extra]))


def add_packed(flat, blocks, extra):
    flat = flat.astype(F32)
    count = flat.shape[0] - extra.shape[0]
    return blocks + flat[:count].reshape(blocks.shape), extra + flat[count:]


def across_planes(x, allowed, k):
    pairs = [(d, d ^ (8 * k)) for d in range(32) if allowed((d ^ (8 * k)) // 8, d % 8)]
    return lax.ppermute(x, AXES, pairs)


def add_halves(layout, keep, other, got, sends):
    half = layout.rows // 2
    keep, other = keep.reshape(24, half, 128), other.reshape(24, half, 128)
    steps = []
    for out, (picks, source, _) in enumerate(sends):
        for i, pick in enumerate(picks):
            steps.append((out, i, pick, source))

    def body(*refs):
        keep_ref, other_ref = refs[:2]
        gots, outs = refs[2 : 2 + len(got)], refs[2 + len(got) : 2 + len(got) + len(sends)]
        slots, sems = refs[-2:]
        copies = []
        for k, (out, i, pick, source) in enumerate(steps):
            pair = [
                pltpu.make_async_copy(ref.at[pick], slots.at[2 * k + j], sems.at[2 * k + j])
                for j, ref in enumerate((keep_ref, other_ref))
            ]
            for copy in pair:
                copy.start()
            copies.append(pair)
        for k, (out, i, pick, source) in enumerate(steps):
            for copy in copies[k]:
                copy.wait()
            value = slots[2 * k] + slots[2 * k + 1]
            if source is not None:
                which, at = source[0], source[1][i]
                value = value + gots[which][at].astype(F32)
            outs[out][i] = value.astype(outs[out].dtype)

    hbm = pl.BlockSpec(memory_space=pl.ANY)
    vmem = pl.BlockSpec(memory_space=pltpu.VMEM)
    return pl.pallas_call(
        body,
        out_shape=[shape((len(p), half, 128), BF if sent else F32) for p, _, sent in sends],
        in_specs=[hbm, hbm] + [vmem] * len(got),
        out_specs=[vmem] * len(sends),
        scratch_shapes=[
            pltpu.VMEM((2 * len(steps), half, 128), F32),
            pltpu.SemaphoreType.DMA((2 * len(steps),)),
        ],
        compiler_params=pltpu.CompilerParams(vmem_limit_bytes=58 << 20),
        cost_estimate=pl.CostEstimate(
            flops=0, bytes_accessed=len(steps) * half * 1536, transcendentals=0
        ),
    )(keep, other, *got)


def first_send(keep, other, layout):
    to_x = [(p * 4 + y * 2 + 1) * 2 for p in range(3) for y in range(2)]
    to_y = [(p * 4 + 2 + x) * 2 + 1 for p in range(3) for x in range(2)]
    return add_halves(layout, keep, other, (), [(to_x, None, True), (to_y, None, True)])


def second_send(keep, other, got_a, got_b, layout):
    sends = []
    for which, (lower, stride) in enumerate(((0, 2), (1, 1))):
        for far in range(2):
            picks = [(p * 4 + far * stride) * 2 + lower for p in range(3)]
            sends.append((picks, (which, [p * 2 + far for p in range(3)]), far == 1))
    return add_halves(layout, keep, other, (got_a, got_b), sends)


def sum_rest(kept, got, second, layout, me):
    rows = layout.rows
    half = rows // 2
    near, mine = me % 8, me // 8

    late = second[0] + permute(second[1], 1)
    apart = late[4 * rows :]
    late = late[: 4 * rows].reshape(2, 2, rows, 128)
    cut = apart.shape[0] // 2
    send_a = packed(late[:, 1, :half], apart[:cut])
    send_b = packed(late[1, :, half:], apart[cut:])
    late_a, apart_a = add_packed(permute(send_a, 2), late[:, 0, :half], apart[:cut])
    late_b, apart_b = add_packed(permute(send_b, 4), late[0, :, half:], apart[cut:])
    got, _, _ = lax.optimization_barrier((got, send_a, send_b))
    kept_a, kept_b = kept[0] + got[0].astype(F32), kept[1] + got[1].astype(F32)

    def plane(k):
        at = jnp.maximum(jnp.bitwise_xor(mine, k) - 1, 0)
        return jnp.concatenate(
            [lax.dynamic_index_in_dim(x, at, 0, False) for x in (kept_a, kept_b)]
        )

    ups = [across_planes(low(plane(k)), lambda p, q: p > 0, k) for k in (1, 2, 3)]

    late_a, apart_a = add_packed(permute(packed(late_a[1], apart_a), 4), late_a[0], apart_a)
    late_b, apart_b = add_packed(permute(packed(late_b[1], apart_b), 2), late_b[0], apart_b)
    apart = jnp.concatenate([apart_a, apart_b])
    lead, gain = layout.apart, 4 * ROW_GAIN - layout.begins[31]
    one = jnp.concatenate([apart[:lead], jnp.zeros((rows - lead, 128), F32)])
    three = jnp.concatenate(
        [
            jnp.zeros((gain, 128), F32),
            apart[lead : lead + 4],
            jnp.zeros((rows - gain - 4, 128), F32),
        ]
    )
    parts = jnp.stack([jnp.concatenate([late_a, late_b]), one, one, three])

    def part(k):
        return lax.dynamic_index_in_dim(parts, jnp.bitwise_xor(mine, k), 0, False)

    lower = part(0)
    for k in (1, 2, 3):
        got = across_planes(
            low(part(k)), lambda p, q: p == 0 or (p, q) == (1, 0) or (p, q) == (3, 7), k
        )
        lower = lower + got.astype(F32)
    upper = plane(0)
    for up in ups:
        upper = upper + up.astype(F32)
    row = lax.broadcasted_iota(jnp.int32, (rows, 1), 0)
    take = (mine == 0) | ((me == 8) & (row < lead))
    add = (me == 31) & (row >= gain) & (row < gain + 4)
    return jnp.where(take, lower, jnp.where(add, upper + lower, upper))


def sum_everywhere(x, fast):
    if not fast:
        return lax.psum(x, AXES)
    for k in range(5):
        x = x + permute(x, 1 << k)
    return x


def mlp_body(
    layout,
    me, h0, attended, w_out, w_dec, gains, weight, valid, levels, counted, w_up_hbm, w_down_hbm, dec_mt_hbm, targets_hbm,
    dh1, loss, keep, send,
    loss_lanes, d_dec, d_gains, small, h1, n2, upper, act, h2, n3, pred, d_pred, dm, du, d_y, total_out, d_out, d_up, d_down, w_up, w_down, dec_mt, targets_t, sems, in_sems,
):
    samples, nodes, _ = h0.shape
    here = me[0]
    loads = [
        pltpu.make_async_copy(source, target, in_sems.at[k])
        for k, (source, target) in enumerate(
            ((w_up_hbm, w_up), (w_down_hbm, w_down), (dec_mt_hbm, dec_mt), (targets_hbm, targets_t))
        )
    ]
    for load in loads:
        load.start()
    pixels = dec_mt.shape[1]
    pred[...] = jnp.zeros(pred.shape, BF)
    scale = (2.0 / counted[0:1, 0:1]) * (1.0 / 3.0)
    tile = 512
    tiles = nodes // tile
    for s in range(samples):

        @pl.loop(0, tiles, unroll=True)
        def _(i):
            rows = pl.ds(pl.multiple_of(i * tile, tile), tile)
            flat = pl.ds(pl.multiple_of(s * nodes + i * tile, tile), tile)
            mid = h0[s, rows, :] + dot(attended[s, rows, :], w_out[...])
            h1[flat, :] = mid
            hat, _ = norm(mid)
            in_two = (hat * gains[1:2, :]).astype(BF)
            n2[flat, :] = in_two
            if s == 0:
                loads[0].wait()
                loads[1].wait()
            end = mid
            for c in range(4):
                cols = slice(c * D, (c + 1) * D)
                u = dot(in_two, w_up[:, cols])
                sig = sigmoid(u)
                upper[flat, cols] = slope(u, sig)
                a = (u * sig).astype(BF)
                act[flat, cols] = a
                end = end + dot(a, w_down[cols, :])
            h2[flat, :] = end
            hat, _ = norm(end)
            in_three = (hat * gains[2:3, :]).astype(BF)
            n3[flat, :] = in_three
            high, low = split(dot(in_three, w_dec[...]).T)
            pred[s * CP : s * CP + C_OUT, rows] = high
            pred[(samples + s) * CP : (samples + s) * CP + C_OUT, rows] = low

    loads[2].wait()
    loads[3].wait()
    d_pred[...] = jnp.zeros(d_pred.shape, F32)
    loss_lanes[...] = jnp.zeros(loss_lanes.shape, F32)

    @pl.loop(0, pixels // 1024)
    def _(i):
        part = pl.ds(pl.multiple_of(i * 1024, 1024), 1024)
        counts = dec_mt[:, part]
        y_all = dot(pred[...], counts)
        highs, lows = [], []
        for s in range(samples):
            y = y_all[s * CP : (s + 1) * CP] + y_all[(samples + s) * CP : (samples + s + 1) * CP]
            misfit = y * (1.0 / 3.0) - targets_t[s, :, part]
            g = weight[s : s + 1, part] * levels[...] * misfit
            loss_lanes[...] += jnp.sum(g * misfit, axis=0, keepdims=True)
            high, low = split(g * scale)
            highs.append(high)
            lows.append(low)
        d_pred[...] += dot_nt(jnp.concatenate(highs + lows, axis=0), counts)

    loss[0:1, :] = jnp.sum(loss_lanes[...], axis=1, keepdims=True) + jnp.zeros((1, 128), F32)
    valid_rows = jnp.sum(valid[...].astype(F32), axis=0, keepdims=True)
    loss[1:2, :] = jnp.sum(valid_rows, axis=1, keepdims=True) + jnp.zeros((1, 128), F32)
    total_out[...] = jnp.zeros(total_out.shape, F32)
    d_dec[...] = jnp.zeros(d_dec.shape, F32)
    d_gains[...] = jnp.zeros(d_gains.shape, F32)
    for s in range(samples):
        total = d_pred[s * CP : (s + 1) * CP] + d_pred[(samples + s) * CP : (samples + s + 1) * CP]
        padded = jnp.concatenate([total, jnp.zeros((128 - CP, nodes), F32)], axis=0)
        d_y[...] = padded.T.astype(BF)

        @pl.loop(0, tiles, unroll=True)
        def _(i):
            rows = pl.ds(pl.multiple_of(i * tile, tile), tile)
            flat = pl.ds(pl.multiple_of(s * nodes + i * tile, tile), tile)
            d_part = d_y[rows, 0:C_OUT]
            d_dec[:, 0:C_OUT] += dot_tn(n3[flat, :], d_part)
            grad = dot_nt(d_part, w_dec[...])
            hat, r = norm(h2[flat, :])
            d_gains[2:3, :] += jnp.sum(grad * hat, axis=0, keepdims=True)
            d_end = norm_back(grad, gains[2:3, :], hat, r)
            d_low = d_end.astype(BF)
            dm[flat, :] = d_low
            d_in = jnp.zeros((tile, D), F32)
            for c in range(4):
                cols = slice(c * D, (c + 1) * D)
                d_act = dot_nt(d_low, w_down[cols, :])
                d_u = (d_act * upper[flat, cols]).astype(BF)
                du[flat, cols] = d_u
                d_in = d_in + dot_nt(d_u, w_up[:, cols])
            hat, r = norm(h1[flat, :])
            d_gains[1:2, :] += jnp.sum(d_in * hat, axis=0, keepdims=True)
            d_mid = d_end + norm_back(d_in, gains[1:2, :], hat, r)
            dh1[s, rows, :] = d_mid
            total_out[...] += dot_tn(attended[s, rows, :], d_mid.astype(BF))

    def copies(name, source, action):
        window_copies(
            here, layout.rows, layout.plans[0][0][name], source, keep, send, sems, action
        )

    narrow_to_flat(d_dec, small)
    small[4 * C_OUT :, :] = jnp.zeros((small.shape[0] - 4 * C_OUT, 128), F32)
    for k in (1, 2):
        for lane in range(D // 128):
            row = 4 * (C_OUT + k) + lane
            small[row : row + 1, :] = d_gains[k : k + 1, lane * 128 : lane * 128 + 128]
    copies("small", small, "start")
    put_flat(d_out, total_out[...], 0, 4)
    copies("out", d_out, "start")
    for c in range(FF // D):
        cols = slice(c * D, (c + 1) * D)
        put_flat(d_up, dot_tn(n2[...], du[:, cols]), 4 * c, 16)
    copies("up", d_up, "start")
    for c in range(FF // D):
        cols = slice(c * D, (c + 1) * D)
        put_flat(d_down, dot_tn(act[:, cols], dm[...]), 4 * c * D, 4)
        copies(f"down{c}", d_down.at[pl.ds(4 * c * D, 4 * D), :], "start")
    copies("small", small, "wait")
    copies("out", d_out, "wait")
    copies("up", d_up, "wait")
    for c in range(FF // D):
        copies(f"down{c}", d_down.at[pl.ds(4 * c * D, 4 * D), :], "wait")


def mlp(me, h0, attended, w_out, w_up, w_down, w_dec, gains, dec_mt, targets_t, weight, valid, levels, counted,
        layout):
    samples, nodes, _ = h0.shape
    rows = samples * nodes
    count = layout.plans[0][1]
    sent = layout.sizes[0] if layout.fast else 8
    vmem = pl.BlockSpec(memory_space=pltpu.VMEM)
    hbm = pl.BlockSpec(memory_space=pl.ANY)
    return pl.pallas_call(
        functools.partial(mlp_body, layout),
        out_shape=[
            shape((samples, nodes, D)),
            shape((2, 128)),
            shape((layout.sizes[0], 128)),
            shape((sent, 128)),
        ],
        in_specs=[pl.BlockSpec(memory_space=pltpu.SMEM)] + [vmem] * 9 + [hbm] * 4,
        out_specs=[vmem] * 2 + [hbm] * 2,
        scratch_shapes=[
            pltpu.VMEM((1, 1024), F32),
            pltpu.VMEM((D, 128), F32),
            pltpu.VMEM((8, D), F32),
            pltpu.VMEM((layout.small, 128), F32),
            pltpu.VMEM((rows, D), F32),
            pltpu.VMEM((rows, D), BF),
            pltpu.VMEM((rows, FF), F32),
            pltpu.VMEM((rows, FF), BF),
            pltpu.VMEM((rows, D), F32),
            pltpu.VMEM((rows, D), BF),
            pltpu.VMEM((2 * samples * CP, nodes), BF),
            pltpu.VMEM((2 * samples * CP, nodes), F32),
            pltpu.VMEM((rows, D), BF),
            pltpu.VMEM((rows, FF), BF),
            pltpu.VMEM((nodes, 128), BF),
            pltpu.VMEM((D, D), F32),
            pltpu.VMEM((4 * D, 128), F32),
            pltpu.VMEM((16 * D, 128), F32),
            pltpu.VMEM((4 * FF, 128), F32),
            pltpu.VMEM(w_up.shape, BF),
            pltpu.VMEM(w_down.shape, BF),
            pltpu.VMEM(dec_mt.shape, BF),
            pltpu.VMEM(targets_t.shape, F32),
            pltpu.SemaphoreType.DMA((count,)),
            pltpu.SemaphoreType.DMA((4,)),
        ],
        compiler_params=pltpu.CompilerParams(vmem_limit_bytes=60 << 20),
        cost_estimate=pl.CostEstimate(flops=16 << 30, bytes_accessed=24 << 20, transcendentals=0),
    )(me, h0, attended, w_out, w_dec, gains, weight, valid, levels, counted, w_up, w_down, dec_mt, targets_t)


def attend_back_body(
    qkv, before, after, log_c, dh1, w_out,
    d_qkv, d_rims, d_before, d_after,
    pairs, do_both,
):
    samples, nodes, _ = dh1.shape
    halo = before.shape[1]
    for s in range(samples):
        gather_pairs(qkv, before, after, pairs, s)
        for i in range(nodes // 256):
            rows = slice(i * 256, (i + 1) * 256)
            da = dh1[s, rows, :].astype(BF)
            high, low = split(dot_nt(da, w_out[...]))
            for h in range(HEADS):
                lanes = slice(h * HEAD_DIM, (h + 1) * HEAD_DIM)
                do_both[rows, 2 * h * HEAD_DIM : (2 * h + 1) * HEAD_DIM] = high[:, lanes]
                do_both[rows, (2 * h + 1) * HEAD_DIM : (2 * h + 2) * HEAD_DIM] = low[:, lanes]
        for h in range(HEADS):
            lanes = slice(h * HEAD_DIM, (h + 1) * HEAD_DIM)
            vlanes = slice(D + h * HEAD_DIM, D + (h + 1) * HEAD_DIM)
            query = qkv[s, :, lanes]
            keys = pairs[:, lanes]
            values = pairs[:, vlanes]
            do = do_both[:, 2 * h * HEAD_DIM : (2 * h + 2) * HEAD_DIM]
            probs = attention_weights(keys, query, log_c)
            d_probs = dot_nt(jnp.concatenate([values, values], axis=1), do)
            centre = jnp.sum(probs * d_probs, 0, keepdims=True)
            high, low = split(probs * (d_probs - centre))
            dv2 = dot(probs.astype(BF), do)
            dv = dv2[:, :HEAD_DIM] + dv2[:, HEAD_DIM:]
            dk = (dot(high, query) + dot(low, query)) * SCALE
            dq_t = (dot_tn(keys, high) + dot_tn(keys, low)) * SCALE
            d_qkv[s, :, lanes] = dq_t.T.astype(BF)
            klanes = slice(D + h * HEAD_DIM, D + (h + 1) * HEAD_DIM)
            wide_lanes = slice(2 * D + h * HEAD_DIM, 2 * D + (h + 1) * HEAD_DIM)
            d_qkv[s, :, klanes] = dk[halo : halo + nodes].astype(BF)
            d_qkv[s, :, wide_lanes] = dv[halo : halo + nodes].astype(BF)
            for rim, first in ((0, halo), (1, nodes)):
                d_rims[s, rim, :, lanes] = dk[first : first + halo]
                d_rims[s, rim, :, vlanes] = dv[first : first + halo]
            d_before[s, :, lanes] = dk[:halo].astype(BF)
            d_before[s, :, vlanes] = dv[:halo].astype(BF)
            d_after[s, :, lanes] = dk[halo + nodes :].astype(BF)
            d_after[s, :, vlanes] = dv[halo + nodes :].astype(BF)


def attend_back(qkv, before, after, log_c, dh1, w_out):
    samples, nodes, _ = dh1.shape
    halo = before.shape[1]
    rim = by_sample(halo, 2 * D)
    return pl.pallas_call(
        attend_back_body,
        grid=(samples,),
        out_shape=[
            shape((samples, nodes, 3 * D), BF),
            shape((samples, 2, halo, 2 * D)),
            shape((samples, halo, 2 * D), BF),
            shape((samples, halo, 2 * D), BF),
        ],
        in_specs=[by_sample(nodes, 3 * D), rim, rim, same(*log_c.shape), by_sample(nodes, D), same(D, D)],
        out_specs=[by_sample(nodes, 3 * D), by_sample(2, halo, 2 * D), rim, rim],
        scratch_shapes=[pltpu.VMEM((log_c.shape[0], 2 * D), BF), pltpu.VMEM((nodes, 2 * D), BF)],
        compiler_params=pltpu.CompilerParams(vmem_limit_bytes=58 << 20),
        cost_estimate=pl.CostEstimate(flops=8 << 30, bytes_accessed=20 << 20, transcendentals=0),
    )(qkv, before, after, log_c, dh1, w_out)


def encode_back_body(
    layout, samples,
    me, grid, w_enc, enc_mt, w_qkv, gains, h0, dh1, d_in, d_rims, from_lower, from_upper,
    keep, send,
    both, dqkv, n1, d_gain, total, total_enc, d_qkv, d_enc, gain_rows, sems,
):
    nodes, halo, pixels = h0.shape[1], from_lower.shape[1], grid.shape[2]
    step = pl.program_id(0)
    first, final = step == 0, step == samples - 1

    def copies(name, source, action):
        window_copies(
            me[0], layout.rows, layout.plans[1][0][name], source, keep, send, sems, action
        )

    @pl.when(first)
    def _():
        d_gain[...] = jnp.zeros(d_gain.shape, F32)
        total[...] = jnp.zeros(total.shape, F32)
        total_enc[...] = jnp.zeros(total_enc.shape, F32)

    dqkv[...] = d_in[0]
    low_rim = d_rims[0, 0] + from_lower[0].astype(F32)
    dqkv[0:halo, D:] = low_rim.astype(BF)
    high_rim = d_rims[0, 1] + from_upper[0].astype(F32)
    dqkv[nodes - halo :, D:] = high_rim.astype(BF)
    hat, r = norm(h0[0])
    n1[...] = (hat * gains[0:1, :]).astype(BF)
    grad = dot_nt(dqkv[...], w_qkv[...])
    d_gain[0:1, :] += jnp.sum(grad * hat, axis=0, keepdims=True)
    d_start = dh1[0] + norm_back(grad, gains[0:1, :], hat, r)
    high, low = split(d_start * 0.25)
    both[:, 0:D] = high
    both[:, D:] = low
    for c in range(3):
        total[c] += dot_tn(n1[...], dqkv[:, c * D : (c + 1) * D])

    @pl.when(final)
    def _():
        gain_rows[...] = jnp.zeros((8, 128), F32)
        for lane in range(D // 128):
            gain_rows[lane : lane + 1, :] = d_gain[0:1, lane * 128 : lane * 128 + 128]
        copies("gain", gain_rows, "start")
        for c in range(3):
            put_flat(d_qkv, total[c], 4 * c, 12)
        copies("qkv", d_qkv, "start")

    for i in range(pixels // 512):
        rows = slice(i * 512, (i + 1) * 512)
        x_t = grid[0, :, rows]
        pre = dot_tn(x_t, w_enc[...])
        spread2 = dot(enc_mt[rows, :], both[...])
        spread = spread2[:, 0:D] + spread2[:, D:]
        d_pre = (spread * slope(pre, sigmoid(pre))).astype(BF)
        total_enc[...] += dot(x_t, d_pre)

    @pl.when(final)
    def _():
        put_flat(d_enc, total_enc[...], 0, 4)
        copies("enc", d_enc, "start")
        copies("gain", gain_rows, "wait")
        copies("qkv", d_qkv, "wait")
        copies("enc", d_enc, "wait")


def encode_back(me, grid, w_enc, enc_mt, w_qkv, gains, h0, dh1, d_in, d_rims, from_lower, from_upper,
                layout):
    samples, nodes, _ = h0.shape
    halo, pixels = from_lower.shape[1], grid.shape[2]
    rim = by_sample(halo, 2 * D)
    return pl.pallas_call(
        functools.partial(encode_back_body, layout, samples),
        grid=(samples,),
        out_shape=[
            shape((layout.sizes[1], 128)),
            shape((layout.sizes[1] if layout.fast else 8, 128)),
        ],
        in_specs=[
            SCALAR,
            by_sample(C_IN, pixels),
            same(C_IN, D),
            same(*enc_mt.shape),
            same(*w_qkv.shape),
            same(8, D),
            by_sample(nodes, D),
            by_sample(nodes, D),
            by_sample(nodes, 3 * D),
            by_sample(2, halo, 2 * D),
            rim,
            rim,
        ],
        out_specs=[HBM, HBM],
        scratch_shapes=[
            pltpu.VMEM((nodes, 2 * D), BF),
            pltpu.VMEM((nodes, 3 * D), BF),
            pltpu.VMEM((nodes, D), BF),
            pltpu.VMEM((8, D), F32),
            pltpu.VMEM((3, D, D), F32),
            pltpu.VMEM((C_IN, D), F32),
            pltpu.VMEM((12 * D, 128), F32),
            pltpu.VMEM((4 * C_IN, 128), F32),
            pltpu.VMEM((8, 128), F32),
            pltpu.SemaphoreType.DMA((layout.plans[1][1],)),
        ],
        compiler_params=pltpu.CompilerParams(vmem_limit_bytes=58 << 20),
        cost_estimate=pl.CostEstimate(flops=16 << 30, bytes_accessed=24 << 20, transcendentals=0),
    )(me, grid, w_enc, enc_mt, w_qkv, gains, h0, dh1, d_in, d_rims, from_lower, from_upper)


def ring(axis, distance):
    count = lax.axis_size(axis)
    return [(i, (i + distance) % count) for i in range(count)]


def window_plan(shard, count):
    starts = [(LEAD * D + d * shard) // (16 * D) * 16 for d in range(count)]
    ends = [-(-(LEAD * D + (d + 1) * shard) // D) for d in range(count)]
    rows = max(-(-(e - s + 1) // 16) * 16 for s, e in zip(starts, ends))
    return starts, rows


def per_device(
    grid, targets, area, sigma_weight, level_weight, valid, enc_index, dec_index, neighbours,
    params, first_moment, second_moment, average,
):
    shard = params.shape[0]
    devices = lax.axis_size(AXES)
    me = lax.axis_index(AXES)
    fast = (lax.axis_size("patch"), lax.axis_size("dp")) == (8, 4)
    layout = Layout(shard, devices, fast)
    starts, win = layout.starts, layout.win
    begin = LEAD * D + me * shard
    shift = begin - begin // (16 * D) * (16 * D)
    place = me.astype(jnp.int32).reshape(1)

    lane_counts = jnp.sum(valid.reshape(-1, D), axis=0).astype(BF)
    payload = lax.dynamic_update_slice(jnp.zeros((win * D,), BF), params.astype(BF), (shift,))
    payload = lax.dynamic_update_slice(payload, lane_counts, ((win - 1) * D,)).reshape(win, D)
    weight = valid.astype(F32) * area[None, :] * sigma_weight[:, None]
    levels = jnp.pad(level_weight, (0, CP - C_OUT)).reshape(CP, 1)
    pixels = dec_index.shape[0]
    first_work = lambda: count_encoder(enc_index, pixels)

    def second_work(dec_index, neighbours, targets):
        return count_rest(dec_index, neighbours, targets), weight, levels

    def third_work(params):
        positions = me * shard + lax.iota(jnp.int32, shard)
        bounds = segment_bounds() + [(-1, -1)]
        lower = jnp.array([x for x, _ in bounds], jnp.int32)[:, None]
        upper = jnp.array([x for _, x in bounds], jnp.int32)[:, None]
        member = ((positions >= lower) & (positions < upper)).astype(F32)
        return member, jnp.sum(member * (params * params)[None, :], axis=1)

    targets = jnp.transpose(targets, (2, 0, 1))
    second_inputs, third_inputs = (dec_index, neighbours, targets), (params,)
    if fast:
        pieces, plan, first_done, second_done, third_done = gather_windows(
            payload, first_work, second_work, second_inputs, third_work, third_inputs
        )
        place_of = place_by_xor
    else:
        everything = lax.all_gather(payload, AXES, axis=0, tiled=False)
        pieces = [everything.reshape(devices * win, D)]
        plan = [(0, d * win, d, 0, win) for d in range(devices)]
        place_of = lambda here, d: d
        first_done, second_done = first_work(), second_work(*second_inputs)
        third_done = third_work(*third_inputs)
    member, old_sums = third_done
    enc_m, enc_mt = first_done
    (dec_mt, log_c, targets_t), weight, levels = second_done
    grid = jnp.swapaxes(grid, 1, 2)

    w_enc, w_qkv, gains = unpack(
        place, pieces, plan, ("enc", "qkv", "gains"), place_of, devices, win, starts
    )
    h0, qkv, leading, last = encode(grid, w_enc, enc_m, w_qkv, gains)
    before = lax.ppermute(last, "patch", ring("patch", 1))
    after = lax.ppermute(leading, "patch", ring("patch", -1))
    w_out, w_up, w_down, w_dec, counted = unpack(
        place, pieces, plan, ("out", "up", "down", "dec", "count"), place_of, devices, win, starts
    )
    attended = attend(qkv, before, after, log_c)
    dh1, own, keep, send = mlp(
        place, h0, attended, w_out, w_up, w_down, w_dec, gains, dec_mt, targets_t, weight, valid, levels,
        counted, layout,
    )
    back = attend_back(qkv, before, after, log_c, dh1, w_out)
    if fast:
        other = permute(send, 1)
        other, back = lax.optimization_barrier((other, back))
    d_qkv, d_rims, d_before, d_after = back
    from_upper = lax.ppermute(d_before, "patch", ring("patch", -1))
    from_lower = lax.ppermute(d_after, "patch", ring("patch", 1))
    if fast:
        send_a, send_b = first_send(keep, other, layout)
        got = permute(send_a, 2), permute(send_b, 4)
        send_a, send_b, from_upper, from_lower = lax.optimization_barrier(
            (send_a, send_b, from_upper, from_lower)
        )
    second = encode_back(
        place, grid, w_enc, enc_mt, w_qkv, gains, h0, dh1, d_qkv, d_rims, from_lower, from_upper,
        layout,
    )
    if fast:
        second, got = lax.optimization_barrier((second, got))
        keep_a, send_a, keep_b, send_b = second_send(keep, other, *got, layout)
        got = permute(send_a, 4), permute(send_b, 2)
        grad_window = sum_rest((keep_a, keep_b), got, second, layout, me)
    else:
        grad_window = sum_flat(keep, second[0], layout)
    grad = lax.dynamic_slice(grad_window.reshape(-1), (begin - begin // 1024 * 1024,), (shard,))

    new_first = BETA_ONE * first_moment + (1.0 - BETA_ONE) * grad
    new_second = BETA_TWO * second_moment + (1.0 - BETA_TWO) * grad * grad
    update = (
        new_first
        / (1.0 - BETA_ONE**STEP)
        / (jnp.sqrt(new_second / (1.0 - BETA_TWO**STEP)) + LAMB_EPS)
        + DECAY * params
    )
    sums = jnp.stack([old_sums, jnp.sum(member * (update * update)[None, :], axis=1)])
    own = own[:, 0:1]
    sums = jnp.where(jnp.arange(8)[None, :] == 7, own, sums)
    totals = sum_everywhere(sums, fast)
    norms = jnp.sqrt(totals[:, :7])
    step_ratio = jnp.sum(member[:7] * (norms[0] / norms[1])[:, None], axis=0)
    new_params = params - RATE * step_ratio * update
    new_average = EMA_KEEP * average + (1.0 - EMA_KEEP) * new_params
    return (
        totals[:, 7],
        norms,
        new_params,
        new_first,
        new_second,
        new_average,
    )


def solution(mesh):
    flat = P(AXES)
    in_specs = (
        P("dp", "patch", None),
        P("dp", "patch", None),
        P("patch"),
        P("dp"),
        P(),
        P("dp", "patch"),
        P("patch", None),
        P("patch", None),
        P("patch", None),
        flat,
        flat,
        flat,
        flat,
    )
    out_specs = (P(), P(), flat, flat, flat, flat)
    return jax.shard_map(
        per_device, mesh=mesh, in_specs=in_specs, out_specs=out_specs, check_vma=False
    )
```

```python
import functools
import math

import jax
import jax.numpy as jnp
from jax import lax
from jax.experimental import pallas as pl
from jax.experimental.pallas import tpu as pltpu
from jax.sharding import PartitionSpec as P

D = 512
HEADS = 4
HEAD_DIM = 128
FF = 2048
C_OUT = 84
C_IN = 264
STEP = 10
EPS_NORM = 1e-05
BETA_ONE = 0.9
BETA_TWO = 0.999
LAMB_EPS = 1e-06
DECAY = 0.01
RATE = 0.2
EMA_KEEP = 0.8
BF = jnp.bfloat16
F32 = jnp.float32
SCALE = HEAD_DIM ** (-0.5)
LOG2E = 1.4426950408889634
ABSENT = -1e30
CP = 96
AXES = ("patch", "dp")

LEAD = 8
ROW_ENC = LEAD
ROW_QKV = ROW_ENC + C_IN
ROW_OUT = ROW_QKV + 3 * D
ROW_UP = ROW_OUT + D
ROW_DOWN = ROW_UP + 4 * D
ROW_DEC = ROW_DOWN + FF
ROW_GAIN = ROW_DEC + C_OUT
ROW_END = ROW_GAIN + 3
ROWS_ALL = -(-ROW_END // 16) * 16


def matrix_shapes():
    return [(C_IN, D), (D, 3 * D), (D, D), (D, FF), (FF, D), (D, C_OUT), (3, D)]


def segment_bounds():
    bounds = []
    offset = 0
    for row_count, col_count in matrix_shapes():
        bounds.append((offset, offset + row_count * col_count))
        offset += row_count * col_count
    return bounds


NPARAM_USED = segment_bounds()[-1][1]


def dot(a, b):
    return lax.dot_general(a, b, (((1,), (0,)), ((), ())), preferred_element_type=F32)


def dot_nt(a, b):
    return lax.dot_general(a, b, (((1,), (1,)), ((), ())), preferred_element_type=F32)


def dot_tn(a, b):
    return lax.dot_general(a, b, (((0,), (0,)), ((), ())), preferred_element_type=F32)


def split(x):
    high = x.astype(BF)
    return high, (x - high.astype(F32)).astype(BF)


def sigmoid(x):
    return 0.5 * jnp.tanh(0.5 * x) + 0.5


def slope(x, s):
    return s * (1.0 + x * (1.0 - s))


def norm(x):
    c = x - jnp.mean(x, -1, keepdims=True)
    r = lax.rsqrt(jnp.mean(c * c, -1, keepdims=True) + EPS_NORM)
    return c * r, r


def norm_back(grad, gain, hat, r):
    g = grad * gain
    return r * (
        g
        - jnp.mean(g, -1, keepdims=True)
        - hat * jnp.mean(g * hat, -1, keepdims=True)
    )


def put_flat(ref, value, first, period):
    for lane in range(D // 128):
        ref[pl.ds(first + lane, value.shape[0], stride=period), :] = value[
            :, lane * 128 : lane * 128 + 128
        ]


def lane_pieces(begin, size, width):
    pieces = []
    while size > 0:
        row, lane = begin // width, begin % width
        count = min(width - lane, size)
        pieces.append((row, lane, count))
        begin, size = begin + count, size - count
    return pieces


PERIOD = 128 // math.gcd(128, C_OUT)
FLAT_PERIOD = PERIOD * C_OUT // 128
GROUPS = D // PERIOD


def narrow_to_flat(narrow, flat):
    for r in range(FLAT_PERIOD):
        parts = [
            narrow[pl.ds(row, GROUPS, stride=PERIOD), :][:, lane : lane + count]
            for row, lane, count in lane_pieces(128 * r, 128, C_OUT)
        ]
        flat[pl.ds(r, GROUPS, stride=FLAT_PERIOD), :] = jnp.concatenate(parts, axis=1)


def flat_to_narrow(flat, narrow):
    for b in range(PERIOD):
        parts = [
            flat[pl.ds(row, GROUPS, stride=FLAT_PERIOD), :][:, lane : lane + count]
            for row, lane, count in lane_pieces(C_OUT * b, C_OUT, 128)
        ]
        parts.append(jnp.zeros((GROUPS, 128 - C_OUT), F32))
        narrow[pl.ds(b, GROUPS, stride=PERIOD), :] = jnp.concatenate(parts, axis=1)


def kernel_call(body, out_shape, scratch=(), flops=0, nbytes=0):
    return pl.pallas_call(
        body,
        out_shape=out_shape,
        scratch_shapes=list(scratch),
        compiler_params=pltpu.CompilerParams(vmem_limit_bytes=58 << 20),
        cost_estimate=pl.CostEstimate(flops=flops, bytes_accessed=nbytes, transcendentals=0),
    )


def by_sample(*dims):
    return pl.BlockSpec((1,) + dims, lambda s: (s,) + (0,) * len(dims))


def same(*dims):
    return pl.BlockSpec(dims, lambda s: (0,) * len(dims))


HBM = pl.BlockSpec(memory_space=pl.ANY)
SCALAR = pl.BlockSpec(memory_space=pltpu.SMEM)


def shape(dims, dtype=F32):
    return jax.ShapeDtypeStruct(tuple(dims), dtype)


def count_rows(index_t, base, rows, cols):
    ids = lax.broadcasted_iota(jnp.int32, (rows, cols), 0) + base
    total = jnp.zeros((rows, cols), F32)
    for k in range(index_t.shape[0]):
        total = total + jnp.where(index_t[k : k + 1, :] == ids, 1.0, 0.0)
    return total


def count_encoder_body(enc, enc_t, enc_m, enc_mt):
    nodes, pixels = enc_m.shape

    @pl.loop(0, nodes // 32)
    def _(i):
        rows = pl.ds(pl.multiple_of(i * 32, 32), 32)
        index = enc[rows, :]
        ids = lax.broadcasted_iota(jnp.int32, (32, pixels), 1)
        total = jnp.zeros((32, pixels), F32)
        for k in range(index.shape[1]):
            total = total + jnp.where(index[:, k : k + 1] == ids, 1.0, 0.0)
        enc_m[rows, :] = total.astype(BF)

    @pl.loop(0, pixels // 64)
    def _(i):
        rows = pl.ds(pl.multiple_of(i * 64, 64), 64)
        enc_mt[rows, :] = count_rows(enc_t, i * 64, 64, nodes).astype(BF)


def count_rest_body(dec_t, nbr_t, targets, dec_mt, log_c, targets_t):
    nodes, pixels = dec_mt.shape

    @pl.loop(0, nodes // 32)
    def _(i):
        rows = pl.ds(pl.multiple_of(i * 32, 32), 32)
        dec_mt[rows, :] = count_rows(dec_t, i * 32, 32, pixels).astype(BF)

    @pl.loop(0, log_c.shape[0] // 64)
    def _(i):
        rows = pl.ds(pl.multiple_of(i * 64, 64), 64)
        total = count_rows(nbr_t, i * 64, 64, nodes)
        log_c[rows, :] = jnp.where(total > 0.0, jnp.log2(jnp.maximum(total, 1.0)), ABSENT)

    for s in range(targets.shape[1]):
        targets_t[s, 0:C_OUT, :] = targets[:, s, :]
        targets_t[s, C_OUT:, :] = jnp.zeros((CP - C_OUT, pixels), F32)


def count_encoder(enc_index, pixels):
    nodes = enc_index.shape[0]
    return kernel_call(
        count_encoder_body,
        [shape((nodes, pixels), BF), shape((pixels, nodes), BF)],
        nbytes=5 << 20,
        flops=1 << 29,
    )(enc_index, enc_index.T)


def count_rest(dec_index, neighbours, targets):
    nodes, pixels = neighbours.shape[0], dec_index.shape[0]
    ext = nodes + 2 * (nodes // 16)
    return kernel_call(
        count_rest_body,
        [shape((nodes, pixels), BF), shape((ext, nodes)), shape((targets.shape[1], CP, pixels))],
        nbytes=8 << 20,
        flops=1 << 29,
    )(dec_index.T, neighbours.T, targets)


def tile_sources(starts, rows):
    return [
        [(d, tile * 16 - s) for d, s in enumerate(starts) if s <= tile * 16 < s + rows]
        for tile in range(ROWS_ALL // 16)
    ]


def assemble(read, window_rows, sources, first_row, rows, put):
    tile, last = first_row // 16, (first_row + rows) // 16
    while tile < last:
        source = sources[tile]
        if len(source) == 1:
            count = 1
            while (
                tile + count < last
                and len(sources[tile + count]) == 1
                and sources[tile + count][0][0] == source[0][0]
                and count < 8
            ):
                count += 1
            d, off = source[0]
            value = read(d, off, 16 * count)
        else:
            count = 1
            value = None
            for d, off in source:
                part = read(d, off, 16).astype(F32)
                if off + 16 == window_rows:
                    part = jnp.where(
                        lax.broadcasted_iota(jnp.int32, part.shape, 0) < 15, part, 0.0
                    )
                value = part if value is None else value + part
            value = value.astype(BF)
        put(tile * 16 - first_row, value)
        tile += count


def wide(stage, ref, period):
    for lane in range(D // 128):
        for c in range(period):
            lanes = slice(c * D + lane * 128, c * D + lane * 128 + 128)
            ref[:, lanes] = stage[lane, pl.ds(c, ref.shape[0], stride=period), :].astype(BF)


def unpack_body(plan, parts, sources, place_of, owner_of, count, *refs):
    me, pieces, refs = refs[0], refs[1 : count + 1], refs[count + 1 :]
    outs, (windows, stage, flat, narrow, sems) = refs[: len(parts)], refs[len(parts) :]
    here = me[0]
    used = set()
    for part in parts:
        if part == "count":
            used = set(range(windows.shape[0]))
        else:
            row, rows = PARTS[part][:2]
            used |= {d for source in sources[row // 16 : (row + rows) // 16] for d, _ in source}
    ranges = [d for d in sorted(used) if d - 1 not in used], [d for d in sorted(used) if d + 1 not in used]
    for piece, at, slot, to, rows in plan:
        copy = pltpu.make_async_copy(
            pieces[piece].at[pl.ds(at, rows), :], windows.at[slot, pl.ds(to, rows), :], sems.at[slot]
        )
        owner = owner_of(here, slot)
        needed = functools.reduce(
            jnp.logical_or, [(owner >= lo) & (owner <= hi) for lo, hi in zip(*ranges)]
        )
        if len(used) == windows.shape[0]:
            copy.start()
        else:
            pl.when(needed)(copy.start)
    window_rows = windows.shape[1]
    waited = set()

    def wait_for(d):
        if d not in waited:
            waited.add(d)
            slot = place_of(here, d)
            pltpu.make_async_copy(windows.at[slot], windows.at[slot], sems.at[slot]).wait()

    def read(d, off, rows):
        wait_for(d)
        return windows[place_of(here, d), off : off + rows, :]

    for part, ref in zip(parts, outs):
        if part == "count":
            for d in range(windows.shape[0]):
                wait_for(d)
            total = jnp.sum(windows[:, window_rows - 16 :, :].astype(F32), axis=0)[15:16, :]
            ref[...] = jnp.sum(total, axis=1, keepdims=True) + jnp.zeros((8, 128), F32)
            continue
        first, rows, period, _ = PARTS[part]

        def direct(off, value):
            ref[off : off + value.shape[0], :] = value

        def staged(off, value):
            wide_value = value.astype(F32)
            for lane in range(D // 128):
                stage[lane, off : off + value.shape[0], :] = wide_value[
                    :, lane * 128 : lane * 128 + 128
                ]

        if part == "gains":
            assemble(read, window_rows, sources, first, rows, staged)
            row = ROW_GAIN - first
            for lane in range(D // 128):
                ref[:, lane * 128 : lane * 128 + 128] = stage[lane, row : row + 8, :]
        elif period == 1:
            assemble(read, window_rows, sources, first, rows, direct)
        else:
            assemble(read, window_rows, sources, first, rows, staged)
            if part == "enc":
                for lane in range(D // 128):
                    lanes = slice(lane * 128, lane * 128 + 128)
                    ref[:, lanes] = stage[lane, LEAD:ROW_QKV, :].astype(BF)
            elif part == "dec":
                row = ROW_DEC - first
                for lane in range(D // 128):
                    flat[pl.ds(lane, C_OUT, stride=4), :] = stage[lane, row : row + C_OUT, :]
                flat_to_narrow(flat, narrow)
                ref[...] = narrow[:, 0:C_OUT].astype(BF)
            else:
                wide(stage, ref, period)


PARTS = {
    "enc": (0, ROW_QKV, 0, (C_IN, D)),
    "qkv": (ROW_QKV, 3 * D, 3, (D, 3 * D)),
    "out": (ROW_OUT, D, 1, (D, D)),
    "up": (ROW_UP, 4 * D, 4, (D, FF)),
    "down": (ROW_DOWN, FF, 1, (FF, D)),
    "dec": (ROW_DEC // 16 * 16, -(-ROW_GAIN // 16) * 16 - ROW_DEC // 16 * 16, 0, (D, C_OUT)),
    "gains": (ROW_GAIN // 16 * 16, 16, 0, (8, D)),
}


def unpack(me, pieces, plan, parts, place_of, slots, rows, starts):
    sources = tile_sources(starts, rows)
    outs = [
        shape((8, 128)) if p == "count" else shape(PARTS[p][3], F32 if p == "gains" else BF)
        for p in parts
    ]
    return pl.pallas_call(
        functools.partial(unpack_body, plan, parts, sources, place_of, place_of, len(pieces)),
        out_shape=outs,
        in_specs=[pl.BlockSpec(memory_space=pltpu.SMEM)]
        + [pl.BlockSpec(memory_space=pl.ANY)] * len(pieces),
        scratch_shapes=[
            pltpu.VMEM((slots, rows, D), BF),
            pltpu.VMEM((D // 128, 4 * D, 128), F32),
            pltpu.VMEM((4 * C_OUT, 128), F32),
            pltpu.VMEM((D, 128), F32),
            pltpu.SemaphoreType.DMA((slots,)),
        ],
        compiler_params=pltpu.CompilerParams(vmem_limit_bytes=58 << 20),
        cost_estimate=pl.CostEstimate(
            flops=0, bytes_accessed=slots * rows * D * 4, transcendentals=0
        ),
    )(me, *pieces)


def permute(x, mask):
    count = lax.axis_size(AXES)
    return lax.ppermute(x, AXES, [(d, d ^ mask) for d in range(count)])


def place_by_xor(here, d):
    return jnp.bitwise_xor(here, d)


def gather_windows(window, first_work, second_work, second_inputs, third_work, third_inputs):
    rows = window.shape[0]
    half = rows // 2
    pieces, plan = [], []

    def add(piece, near, parts):
        for part, flip in ((piece, 0), (permute(piece, 1), 1)):
            for at, slot, to, size in parts:
                plan.append((len(pieces), at, slot ^ near ^ flip, to, size))
            pieces.append(part)

    planes = (8, 16, 24)
    others = [permute(window, m) for m in planes]
    by_x, by_y = permute(window, 2), permute(window, 4)
    first_done = first_work()
    others, by_x, by_y, first_done, second_inputs = lax.optimization_barrier(
        (jnp.concatenate(others), by_x, by_y, first_done, second_inputs)
    )
    others_x, others_y = permute(others, 2), permute(others, 4)
    second_done = second_work(*second_inputs)
    others_x, others_y, second_done, third_inputs = lax.optimization_barrier(
        (others_x, others_y, second_done, third_inputs)
    )

    def halves(near_part, far_part, first):
        far = [far_part[i * rows + first : i * rows + first + half] for i in range(3)]
        return jnp.concatenate([near_part[first : first + half]] + far)

    across_a = permute(halves(by_y, others_y, 0), 2)
    across_b = permute(halves(by_x, others_x, half), 4)
    across_a, across_b, third_done = lax.optimization_barrier(
        (across_a, across_b, third_work(*third_inputs))
    )
    whole = [(0, 0, 0, rows)]
    stacked = [(i * rows, slot, 0, rows) for i, slot in enumerate(planes)]
    add(window, 0, whole)
    add(by_x, 2, whole)
    add(by_y, 4, whole)
    add(others, 0, stacked)
    add(others_x, 2, stacked)
    add(others_y, 4, stacked)
    add(across_a, 6, [(i * half, slot, 0, half) for i, slot in enumerate((0,) + planes)])
    add(across_b, 6, [(i * half, slot, half, half) for i, slot in enumerate((0,) + planes)])
    return pieces, plan, first_done, second_done, third_done


def encode_body(grid, w_enc, enc_hbm, w_hbm, gains, h0, qkv, leading, last, high, low, enc_m, w_qkv, sems):
    pixels, nodes, halo = grid.shape[2], h0.shape[1], last.shape[1]
    first = pl.program_id(0) == 0
    loads = [
        pltpu.make_async_copy(enc_hbm, enc_m, sems.at[0]),
        pltpu.make_async_copy(w_hbm, w_qkv, sems.at[1]),
    ]
    for load in loads:
        pl.when(first)(load.start)
    for i in range(pixels // 512):
        rows = slice(i * 512, (i + 1) * 512)
        pre = dot_tn(grid[0, :, rows], w_enc[...])
        high[rows, :], low[rows, :] = split(pre * sigmoid(pre))
    for load in loads:
        pl.when(first)(load.wait)
    start = (dot(enc_m[...], high[...]) + dot(enc_m[...], low[...])) * 0.25
    h0[0] = start
    hat, _ = norm(start)
    n1 = (hat * gains[0:1, :]).astype(BF)
    qkv[0] = dot(n1, w_qkv[...]).astype(BF)
    leading[0] = qkv[0, 0:halo, D:]
    last[0] = qkv[0, nodes - halo :, D:]


def encode(grid, w_enc, enc_m, w_qkv, gains):
    samples, pixels = grid.shape[0], grid.shape[2]
    nodes = enc_m.shape[0]
    halo = nodes // 16
    return pl.pallas_call(
        encode_body,
        grid=(samples,),
        out_shape=[shape((samples, nodes, D)), shape((samples, nodes, 3 * D), BF)]
        + [shape((samples, halo, 2 * D), BF)] * 2,
        in_specs=[by_sample(C_IN, pixels), same(C_IN, D), HBM, HBM, same(8, D)],
        out_specs=[by_sample(nodes, D), by_sample(nodes, 3 * D)] + [by_sample(halo, 2 * D)] * 2,
        scratch_shapes=[
            pltpu.VMEM((pixels, D), BF),
            pltpu.VMEM((pixels, D), BF),
            pltpu.VMEM(enc_m.shape, BF),
            pltpu.VMEM(w_qkv.shape, BF),
            pltpu.SemaphoreType.DMA((2,)),
        ],
        compiler_params=pltpu.CompilerParams(vmem_limit_bytes=58 << 20),
        cost_estimate=pl.CostEstimate(flops=8 << 30, bytes_accessed=12 << 20, transcendentals=0),
    )(grid, w_enc, enc_m, w_qkv, gains)


def gather_pairs(qkv, before, after, pairs, s):
    halo, nodes = before.shape[1], qkv.shape[1]
    pairs[0:halo, :] = before[s]
    pairs[halo : halo + nodes, :] = qkv[s, :, D:]
    pairs[halo + nodes :, :] = after[s]


def attention_weights(keys, query, log_c):
    x = dot_nt(keys, query) * (SCALE * LOG2E) + log_c[...]
    e = jnp.exp2(x - jnp.max(x, 0, keepdims=True))
    return e * (1.0 / jnp.sum(e, 0, keepdims=True))


def attend_body(qkv, before, after, log_c, out, pairs):
    for s in range(qkv.shape[0]):
        gather_pairs(qkv, before, after, pairs, s)
        for h in range(HEADS):
            lanes = slice(h * HEAD_DIM, (h + 1) * HEAD_DIM)
            keys = pairs[:, lanes]
            values = pairs[:, D + h * HEAD_DIM : D + (h + 1) * HEAD_DIM]
            probs = attention_weights(keys, qkv[s, :, lanes], log_c)
            out_t = dot_tn(values, probs.astype(BF))
            out[s, :, lanes] = out_t.T.astype(BF)


def attend(qkv, before, after, log_c):
    samples, nodes = qkv.shape[:2]
    halo = before.shape[1]
    return pl.pallas_call(
        attend_body,
        grid=(samples,),
        out_shape=shape((samples, nodes, D), BF),
        in_specs=[
            by_sample(nodes, 3 * D),
            by_sample(halo, 2 * D),
            by_sample(halo, 2 * D),
            same(*log_c.shape),
        ],
        out_specs=by_sample(nodes, D),
        scratch_shapes=[pltpu.VMEM((log_c.shape[0], 2 * D), BF)],
        compiler_params=pltpu.CompilerParams(vmem_limit_bytes=58 << 20),
        cost_estimate=pl.CostEstimate(flops=2 << 30, bytes_accessed=8 << 20, transcendentals=0),
    )(qkv, before, after, log_c)


class Layout:
    def __init__(self, shard, devices, fast):
        self.devices = devices
        self.starts, self.win = window_plan(shard, devices)
        self.begins = [(LEAD * D + d * shard) // 1024 * 8 for d in range(devices)]
        self.ends = [-(-(LEAD * D + (d + 1) * shard) // 1024) * 8 for d in range(devices)]
        self.rows = -(-max(e - b for b, e in zip(self.begins, self.ends)) // 32) * 32
        self.small = 4 * (ROW_END - ROW_DEC) + 4
        first = (("out", ROW_OUT, 4 * D), ("up", ROW_UP, 16 * D)) + tuple(
            (f"down{c}", ROW_DOWN + c * D, 4 * D) for c in range(FF // D)
        ) + (("small", ROW_DEC, self.small),)
        second = (("enc", ROW_ENC, 4 * C_IN), ("qkv", ROW_QKV, 12 * D), ("gain", ROW_GAIN, 8))
        self.fast = fast
        if fast:
            self.apart = 4 * ROW_OUT - self.begins[8]
            extra = -(-(self.apart + 8) // 32) * 32
            self.sizes = (12 * self.rows, 4 * self.rows + extra)
        else:
            self.sizes = (sum(x[2] for x in first), sum(x[2] for x in second))
        self.plans = self.make(first, 1), self.make(second, 0)

    def make(self, arrays, plane):
        plans, k, at = {}, 0, 0
        for name, row, size in arrays:
            plans[name] = []
            if not self.fast:
                plans[name].append((k, None, at, 0, size))
                k, at = k + 1, at + size
                continue
            if name == "gain":
                plans[name].append((k, "both", 4 * self.rows + self.apart, 0, size))
                k += 2
                continue
            for d, (lower, upper) in enumerate(zip(self.begins, self.ends)):
                low, high = max(lower, 4 * row), min(upper, 4 * (row + size // 4))
                if low >= high:
                    continue
                if d == 8 and plane == 0:
                    to = 4 * self.rows + low - lower
                    plans[name].append((k, "both", to, low - 4 * row, high - low))
                    k += 2
                else:
                    place = (d // 8 - plane) * 4 * self.rows + low - lower
                    plans[name].append((k, d % 8, place, low - 4 * row, high - low))
                    k += 1
        return plans, k


def window_copies(here, rows_of_slot, blocks, source, keep, send, sems, action):
    for k, near, to, at, rows in blocks:

        def copy(target, first, sem):
            getattr(
                pltpu.make_async_copy(
                    source.at[pl.ds(at, rows), :], target.at[pl.ds(first, rows), :], sems.at[sem]
                ),
                action,
            )()

        if near is None:
            copy(keep, to, k)
        elif near == "both":
            copy(keep, to, k)
            copy(send, to, k + 1)
        else:
            slot = jnp.bitwise_and(jnp.bitwise_xor(here, near), 7)
            first = pl.multiple_of(lax.shift_right_logical(slot, 1) * rows_of_slot + to, 8)
            for target, side in ((keep, 0), (send, 1)):

                @pl.when(jnp.bitwise_and(slot, 1) == side)
                def _():
                    copy(target, first, k)


def sum_flat(first, second, layout):
    flat = jnp.concatenate(
        [
            jnp.zeros((4 * LEAD, 128), F32),
            second[: 4 * (ROW_OUT - LEAD)],
            first,
            jnp.zeros((max(0, layout.begins[-1] + layout.rows - 4 * ROW_DEC - layout.small), 128), F32),
        ]
    )
    gain = second[4 * (ROW_OUT - LEAD) :]
    flat = lax.dynamic_update_slice(
        flat, gain[0:4] + flat[4 * ROW_GAIN : 4 * ROW_GAIN + 4], (4 * ROW_GAIN, 0)
    )
    windows = jnp.concatenate([flat[b : b + layout.rows] for b in layout.begins])
    return lax.psum_scatter(windows, AXES, scatter_dimension=0, tiled=True)


def low(x):
    return x.astype(BF)


def packed(blocks, extra):
    return low(jnp.concatenate([blocks.reshape(-1, 128), extra]))


def add_packed(flat, blocks, extra):
    flat = flat.astype(F32)
    count = flat.shape[0] - extra.shape[0]
    return blocks + flat[:count].reshape(blocks.shape), extra + flat[count:]


def across_planes(x, allowed, k):
    pairs = [(d, d ^ (8 * k)) for d in range(32) if allowed((d ^ (8 * k)) // 8, d % 8)]
    return lax.ppermute(x, AXES, pairs)


def add_halves(layout, keep, other, got, sends):
    half = layout.rows // 2
    keep, other = keep.reshape(24, half, 128), other.reshape(24, half, 128)
    steps = []
    for out, (picks, source, _) in enumerate(sends):
        for i, pick in enumerate(picks):
            steps.append((out, i, pick, source))

    def body(*refs):
        keep_ref, other_ref = refs[:2]
        gots, outs = refs[2 : 2 + len(got)], refs[2 + len(got) : 2 + len(got) + len(sends)]
        slots, sems = refs[-2:]
        copies = []
        for k, (out, i, pick, source) in enumerate(steps):
            pair = [
                pltpu.make_async_copy(ref.at[pick], slots.at[2 * k + j], sems.at[2 * k + j])
                for j, ref in enumerate((keep_ref, other_ref))
            ]
            for copy in pair:
                copy.start()
            copies.append(pair)
        for k, (out, i, pick, source) in enumerate(steps):
            for copy in copies[k]:
                copy.wait()
            value = slots[2 * k] + slots[2 * k + 1]
            if source is not None:
                which, at = source[0], source[1][i]
                value = value + gots[which][at].astype(F32)
            outs[out][i] = value.astype(outs[out].dtype)

    hbm = pl.BlockSpec(memory_space=pl.ANY)
    vmem = pl.BlockSpec(memory_space=pltpu.VMEM)
    return pl.pallas_call(
        body,
        out_shape=[shape((len(p), half, 128), BF if sent else F32) for p, _, sent in sends],
        in_specs=[hbm, hbm] + [vmem] * len(got),
        out_specs=[vmem] * len(sends),
        scratch_shapes=[
            pltpu.VMEM((2 * len(steps), half, 128), F32),
            pltpu.SemaphoreType.DMA((2 * len(steps),)),
        ],
        compiler_params=pltpu.CompilerParams(vmem_limit_bytes=58 << 20),
        cost_estimate=pl.CostEstimate(
            flops=0, bytes_accessed=len(steps) * half * 1536, transcendentals=0
        ),
    )(keep, other, *got)


def first_send(keep, other, layout):
    to_x = [(p * 4 + y * 2 + 1) * 2 for p in range(3) for y in range(2)]
    to_y = [(p * 4 + 2 + x) * 2 + 1 for p in range(3) for x in range(2)]
    return add_halves(layout, keep, other, (), [(to_x, None, True), (to_y, None, True)])


def second_send(keep, other, got_a, got_b, layout):
    sends = []
    for which, (lower, stride) in enumerate(((0, 2), (1, 1))):
        for far in range(2):
            picks = [(p * 4 + far * stride) * 2 + lower for p in range(3)]
            sends.append((picks, (which, [p * 2 + far for p in range(3)]), far == 1))
    return add_halves(layout, keep, other, (got_a, got_b), sends)


def sum_rest(kept, got, second, layout, me):
    rows = layout.rows
    half = rows // 2
    near, mine = me % 8, me // 8

    late = second[0] + permute(second[1], 1)
    apart = late[4 * rows :]
    late = late[: 4 * rows].reshape(2, 2, rows, 128)
    cut = apart.shape[0] // 2
    send_a = packed(late[:, 1, :half], apart[:cut])
    send_b = packed(late[1, :, half:], apart[cut:])
    late_a, apart_a = add_packed(permute(send_a, 2), late[:, 0, :half], apart[:cut])
    late_b, apart_b = add_packed(permute(send_b, 4), late[0, :, half:], apart[cut:])
    got, _, _ = lax.optimization_barrier((got, send_a, send_b))
    kept_a, kept_b = kept[0] + got[0].astype(F32), kept[1] + got[1].astype(F32)

    def plane(k):
        at = jnp.maximum(jnp.bitwise_xor(mine, k) - 1, 0)
        return jnp.concatenate(
            [lax.dynamic_index_in_dim(x, at, 0, False) for x in (kept_a, kept_b)]
        )

    ups = [across_planes(low(plane(k)), lambda p, q: p > 0, k) for k in (1, 2, 3)]

    late_a, apart_a = add_packed(permute(packed(late_a[1], apart_a), 4), late_a[0], apart_a)
    late_b, apart_b = add_packed(permute(packed(late_b[1], apart_b), 2), late_b[0], apart_b)
    apart = jnp.concatenate([apart_a, apart_b])
    lead, gain = layout.apart, 4 * ROW_GAIN - layout.begins[31]
    one = jnp.concatenate([apart[:lead], jnp.zeros((rows - lead, 128), F32)])
    three = jnp.concatenate(
        [
            jnp.zeros((gain, 128), F32),
            apart[lead : lead + 4],
            jnp.zeros((rows - gain - 4, 128), F32),
        ]
    )
    parts = jnp.stack([jnp.concatenate([late_a, late_b]), one, one, three])

    def part(k):
        return lax.dynamic_index_in_dim(parts, jnp.bitwise_xor(mine, k), 0, False)

    lower = part(0)
    for k in (1, 2, 3):
        got = across_planes(
            low(part(k)), lambda p, q: p == 0 or (p, q) == (1, 0) or (p, q) == (3, 7), k
        )
        lower = lower + got.astype(F32)
    upper = plane(0)
    for up in ups:
        upper = upper + up.astype(F32)
    row = lax.broadcasted_iota(jnp.int32, (rows, 1), 0)
    take = (mine == 0) | ((me == 8) & (row < lead))
    add = (me == 31) & (row >= gain) & (row < gain + 4)
    return jnp.where(take, lower, jnp.where(add, upper + lower, upper))


def sum_everywhere(x, fast):
    if not fast:
        return lax.psum(x, AXES)
    for k in range(5):
        x = x + permute(x, 1 << k)
    return x


def mlp_body(
    layout,
    me, h0, attended, w_out, w_dec, gains, weight, valid, levels, counted, w_up_hbm, w_down_hbm, dec_mt_hbm, targets_hbm,
    dh1, loss, keep, send,
    loss_lanes, d_dec, d_gains, small, h1, n2, upper, act, h2, n3, pred, d_pred, dm, du, d_y, total_out, d_out, d_up, d_down, w_up, w_down, dec_mt, targets_t, sems, in_sems,
):
    samples, nodes, _ = h0.shape
    here = me[0]
    loads = [
        pltpu.make_async_copy(source, target, in_sems.at[k])
        for k, (source, target) in enumerate(
            ((w_up_hbm, w_up), (w_down_hbm, w_down), (dec_mt_hbm, dec_mt), (targets_hbm, targets_t))
        )
    ]
    for load in loads:
        load.start()
    pixels = dec_mt.shape[1]
    pred[...] = jnp.zeros(pred.shape, BF)
    scale = (2.0 / counted[0:1, 0:1]) * (1.0 / 3.0)
    tile = 512
    tiles = nodes // tile
    for s in range(samples):

        @pl.loop(0, tiles, unroll=True)
        def _(i):
            rows = pl.ds(pl.multiple_of(i * tile, tile), tile)
            flat = pl.ds(pl.multiple_of(s * nodes + i * tile, tile), tile)
            mid = h0[s, rows, :] + dot(attended[s, rows, :], w_out[...])
            h1[flat, :] = mid
            hat, _ = norm(mid)
            in_two = (hat * gains[1:2, :]).astype(BF)
            n2[flat, :] = in_two
            if s == 0:
                loads[0].wait()
                loads[1].wait()
            end = mid
            for c in range(4):
                cols = slice(c * D, (c + 1) * D)
                u = dot(in_two, w_up[:, cols])
                sig = sigmoid(u)
                upper[flat, cols] = slope(u, sig)
                a = (u * sig).astype(BF)
                act[flat, cols] = a
                end = end + dot(a, w_down[cols, :])
            h2[flat, :] = end
            hat, _ = norm(end)
            in_three = (hat * gains[2:3, :]).astype(BF)
            n3[flat, :] = in_three
            high, low = split(dot(in_three, w_dec[...]).T)
            pred[s * CP : s * CP + C_OUT, rows] = high
            pred[(samples + s) * CP : (samples + s) * CP + C_OUT, rows] = low

    loads[2].wait()
    loads[3].wait()
    d_pred[...] = jnp.zeros(d_pred.shape, F32)
    loss_lanes[...] = jnp.zeros(loss_lanes.shape, F32)

    @pl.loop(0, pixels // 1024)
    def _(i):
        part = pl.ds(pl.multiple_of(i * 1024, 1024), 1024)
        counts = dec_mt[:, part]
        y_all = dot(pred[...], counts)
        highs, lows = [], []
        for s in range(samples):
            y = y_all[s * CP : (s + 1) * CP] + y_all[(samples + s) * CP : (samples + s + 1) * CP]
            misfit = y * (1.0 / 3.0) - targets_t[s, :, part]
            g = weight[s : s + 1, part] * levels[...] * misfit
            loss_lanes[...] += jnp.sum(g * misfit, axis=0, keepdims=True)
            high, low = split(g * scale)
            highs.append(high)
            lows.append(low)
        d_pred[...] += dot_nt(jnp.concatenate(highs + lows, axis=0), counts)

    loss[0:1, :] = jnp.sum(loss_lanes[...], axis=1, keepdims=True) + jnp.zeros((1, 128), F32)
    valid_rows = jnp.sum(valid[...].astype(F32), axis=0, keepdims=True)
    loss[1:2, :] = jnp.sum(valid_rows, axis=1, keepdims=True) + jnp.zeros((1, 128), F32)
    total_out[...] = jnp.zeros(total_out.shape, F32)
    d_dec[...] = jnp.zeros(d_dec.shape, F32)
    d_gains[...] = jnp.zeros(d_gains.shape, F32)
    for s in range(samples):
        total = d_pred[s * CP : (s + 1) * CP] + d_pred[(samples + s) * CP : (samples + s + 1) * CP]
        padded = jnp.concatenate([total, jnp.zeros((128 - CP, nodes), F32)], axis=0)
        d_y[...] = padded.T.astype(BF)

        @pl.loop(0, tiles, unroll=True)
        def _(i):
            rows = pl.ds(pl.multiple_of(i * tile, tile), tile)
            flat = pl.ds(pl.multiple_of(s * nodes + i * tile, tile), tile)
            d_part = d_y[rows, 0:C_OUT]
            d_dec[:, 0:C_OUT] += dot_tn(n3[flat, :], d_part)
            grad = dot_nt(d_part, w_dec[...])
            hat, r = norm(h2[flat, :])
            d_gains[2:3, :] += jnp.sum(grad * hat, axis=0, keepdims=True)
            d_end = norm_back(grad, gains[2:3, :], hat, r)
            d_low = d_end.astype(BF)
            dm[flat, :] = d_low
            d_in = jnp.zeros((tile, D), F32)
            for c in range(4):
                cols = slice(c * D, (c + 1) * D)
                d_act = dot_nt(d_low, w_down[cols, :])
                d_u = (d_act * upper[flat, cols]).astype(BF)
                du[flat, cols] = d_u
                d_in = d_in + dot_nt(d_u, w_up[:, cols])
            hat, r = norm(h1[flat, :])
            d_gains[1:2, :] += jnp.sum(d_in * hat, axis=0, keepdims=True)
            d_mid = d_end + norm_back(d_in, gains[1:2, :], hat, r)
            dh1[s, rows, :] = d_mid
            total_out[...] += dot_tn(attended[s, rows, :], d_mid.astype(BF))

    def copies(name, source, action):
        window_copies(
            here, layout.rows, layout.plans[0][0][name], source, keep, send, sems, action
        )

    narrow_to_flat(d_dec, small)
    small[4 * C_OUT :, :] = jnp.zeros((small.shape[0] - 4 * C_OUT, 128), F32)
    for k in (1, 2):
        for lane in range(D // 128):
            row = 4 * (C_OUT + k) + lane
            small[row : row + 1, :] = d_gains[k : k + 1, lane * 128 : lane * 128 + 128]
    copies("small", small, "start")
    put_flat(d_out, total_out[...], 0, 4)
    copies("out", d_out, "start")
    for c in range(FF // D):
        cols = slice(c * D, (c + 1) * D)
        put_flat(d_up, dot_tn(n2[...], du[:, cols]), 4 * c, 16)
    copies("up", d_up, "start")
    for c in range(FF // D):
        cols = slice(c * D, (c + 1) * D)
        put_flat(d_down, dot_tn(act[:, cols], dm[...]), 4 * c * D, 4)
        copies(f"down{c}", d_down.at[pl.ds(4 * c * D, 4 * D), :], "start")
    copies("small", small, "wait")
    copies("out", d_out, "wait")
    copies("up", d_up, "wait")
    for c in range(FF // D):
        copies(f"down{c}", d_down.at[pl.ds(4 * c * D, 4 * D), :], "wait")


def mlp(me, h0, attended, w_out, w_up, w_down, w_dec, gains, dec_mt, targets_t, weight, valid, levels, counted,
        layout):
    samples, nodes, _ = h0.shape
    rows = samples * nodes
    count = layout.plans[0][1]
    sent = layout.sizes[0] if layout.fast else 8
    vmem = pl.BlockSpec(memory_space=pltpu.VMEM)
    hbm = pl.BlockSpec(memory_space=pl.ANY)
    return pl.pallas_call(
        functools.partial(mlp_body, layout),
        out_shape=[
            shape((samples, nodes, D)),
            shape((2, 128)),
            shape((layout.sizes[0], 128)),
            shape((sent, 128)),
        ],
        in_specs=[pl.BlockSpec(memory_space=pltpu.SMEM)] + [vmem] * 9 + [hbm] * 4,
        out_specs=[vmem] * 2 + [hbm] * 2,
        scratch_shapes=[
            pltpu.VMEM((1, 1024), F32),
            pltpu.VMEM((D, 128), F32),
            pltpu.VMEM((8, D), F32),
            pltpu.VMEM((layout.small, 128), F32),
            pltpu.VMEM((rows, D), F32),
            pltpu.VMEM((rows, D), BF),
            pltpu.VMEM((rows, FF), F32),
            pltpu.VMEM((rows, FF), BF),
            pltpu.VMEM((rows, D), F32),
            pltpu.VMEM((rows, D), BF),
            pltpu.VMEM((2 * samples * CP, nodes), BF),
            pltpu.VMEM((2 * samples * CP, nodes), F32),
            pltpu.VMEM((rows, D), BF),
            pltpu.VMEM((rows, FF), BF),
            pltpu.VMEM((nodes, 128), BF),
            pltpu.VMEM((D, D), F32),
            pltpu.VMEM((4 * D, 128), F32),
            pltpu.VMEM((16 * D, 128), F32),
            pltpu.VMEM((4 * FF, 128), F32),
            pltpu.VMEM(w_up.shape, BF),
            pltpu.VMEM(w_down.shape, BF),
            pltpu.VMEM(dec_mt.shape, BF),
            pltpu.VMEM(targets_t.shape, F32),
            pltpu.SemaphoreType.DMA((count,)),
            pltpu.SemaphoreType.DMA((4,)),
        ],
        compiler_params=pltpu.CompilerParams(vmem_limit_bytes=60 << 20),
        cost_estimate=pl.CostEstimate(flops=16 << 30, bytes_accessed=24 << 20, transcendentals=0),
    )(me, h0, attended, w_out, w_dec, gains, weight, valid, levels, counted, w_up, w_down, dec_mt, targets_t)


def attend_back_body(
    qkv, before, after, log_c, dh1, w_out,
    d_qkv, d_rims, d_before, d_after,
    pairs, do_both,
):
    samples, nodes, _ = dh1.shape
    halo = before.shape[1]
    for s in range(samples):
        gather_pairs(qkv, before, after, pairs, s)
        for i in range(nodes // 256):
            rows = slice(i * 256, (i + 1) * 256)
            da = dh1[s, rows, :].astype(BF)
            high, low = split(dot_nt(da, w_out[...]))
            for h in range(HEADS):
                lanes = slice(h * HEAD_DIM, (h + 1) * HEAD_DIM)
                do_both[rows, 2 * h * HEAD_DIM : (2 * h + 1) * HEAD_DIM] = high[:, lanes]
                do_both[rows, (2 * h + 1) * HEAD_DIM : (2 * h + 2) * HEAD_DIM] = low[:, lanes]
        for h in range(HEADS):
            lanes = slice(h * HEAD_DIM, (h + 1) * HEAD_DIM)
            vlanes = slice(D + h * HEAD_DIM, D + (h + 1) * HEAD_DIM)
            query = qkv[s, :, lanes]
            keys = pairs[:, lanes]
            values = pairs[:, vlanes]
            do = do_both[:, 2 * h * HEAD_DIM : (2 * h + 2) * HEAD_DIM]
            probs = attention_weights(keys, query, log_c)
            d_probs = dot_nt(jnp.concatenate([values, values], axis=1), do)
            centre = jnp.sum(probs * d_probs, 0, keepdims=True)
            high, low = split(probs * (d_probs - centre))
            dv2 = dot(probs.astype(BF), do)
            dv = dv2[:, :HEAD_DIM] + dv2[:, HEAD_DIM:]
            dk = (dot(high, query) + dot(low, query)) * SCALE
            dq_t = (dot_tn(keys, high) + dot_tn(keys, low)) * SCALE
            d_qkv[s, :, lanes] = dq_t.T.astype(BF)
            klanes = slice(D + h * HEAD_DIM, D + (h + 1) * HEAD_DIM)
            wide_lanes = slice(2 * D + h * HEAD_DIM, 2 * D + (h + 1) * HEAD_DIM)
            d_qkv[s, :, klanes] = dk[halo : halo + nodes].astype(BF)
            d_qkv[s, :, wide_lanes] = dv[halo : halo + nodes].astype(BF)
            for rim, first in ((0, halo), (1, nodes)):
                d_rims[s, rim, :, lanes] = dk[first : first + halo]
                d_rims[s, rim, :, vlanes] = dv[first : first + halo]
            d_before[s, :, lanes] = dk[:halo].astype(BF)
            d_before[s, :, vlanes] = dv[:halo].astype(BF)
            d_after[s, :, lanes] = dk[halo + nodes :].astype(BF)
            d_after[s, :, vlanes] = dv[halo + nodes :].astype(BF)


def attend_back(qkv, before, after, log_c, dh1, w_out):
    samples, nodes, _ = dh1.shape
    halo = before.shape[1]
    rim = by_sample(halo, 2 * D)
    return pl.pallas_call(
        attend_back_body,
        grid=(samples,),
        out_shape=[
            shape((samples, nodes, 3 * D), BF),
            shape((samples, 2, halo, 2 * D)),
            shape((samples, halo, 2 * D), BF),
            shape((samples, halo, 2 * D), BF),
        ],
        in_specs=[by_sample(nodes, 3 * D), rim, rim, same(*log_c.shape), by_sample(nodes, D), same(D, D)],
        out_specs=[by_sample(nodes, 3 * D), by_sample(2, halo, 2 * D), rim, rim],
        scratch_shapes=[pltpu.VMEM((log_c.shape[0], 2 * D), BF), pltpu.VMEM((nodes, 2 * D), BF)],
        compiler_params=pltpu.CompilerParams(vmem_limit_bytes=58 << 20),
        cost_estimate=pl.CostEstimate(flops=8 << 30, bytes_accessed=20 << 20, transcendentals=0),
    )(qkv, before, after, log_c, dh1, w_out)


def encode_back_body(
    layout, samples,
    me, grid, w_enc, enc_mt, w_qkv, gains, h0, dh1, d_in, d_rims, from_lower, from_upper,
    keep, send,
    both, dqkv, n1, d_gain, total, total_enc, d_qkv, d_enc, gain_rows, sems,
):
    nodes, halo, pixels = h0.shape[1], from_lower.shape[1], grid.shape[2]
    step = pl.program_id(0)
    first, final = step == 0, step == samples - 1

    def copies(name, source, action):
        window_copies(
            me[0], layout.rows, layout.plans[1][0][name], source, keep, send, sems, action
        )

    @pl.when(first)
    def _():
        d_gain[...] = jnp.zeros(d_gain.shape, F32)
        total[...] = jnp.zeros(total.shape, F32)
        total_enc[...] = jnp.zeros(total_enc.shape, F32)

    dqkv[...] = d_in[0]
    low_rim = d_rims[0, 0] + from_lower[0].astype(F32)
    dqkv[0:halo, D:] = low_rim.astype(BF)
    high_rim = d_rims[0, 1] + from_upper[0].astype(F32)
    dqkv[nodes - halo :, D:] = high_rim.astype(BF)
    hat, r = norm(h0[0])
    n1[...] = (hat * gains[0:1, :]).astype(BF)
    grad = dot_nt(dqkv[...], w_qkv[...])
    d_gain[0:1, :] += jnp.sum(grad * hat, axis=0, keepdims=True)
    d_start = dh1[0] + norm_back(grad, gains[0:1, :], hat, r)
    high, low = split(d_start * 0.25)
    both[:, 0:D] = high
    both[:, D:] = low
    for c in range(3):
        total[c] += dot_tn(n1[...], dqkv[:, c * D : (c + 1) * D])

    @pl.when(final)
    def _():
        gain_rows[...] = jnp.zeros((8, 128), F32)
        for lane in range(D // 128):
            gain_rows[lane : lane + 1, :] = d_gain[0:1, lane * 128 : lane * 128 + 128]
        copies("gain", gain_rows, "start")
        for c in range(3):
            put_flat(d_qkv, total[c], 4 * c, 12)
        copies("qkv", d_qkv, "start")

    for i in range(pixels // 512):
        rows = slice(i * 512, (i + 1) * 512)
        x_t = grid[0, :, rows]
        pre = dot_tn(x_t, w_enc[...])
        spread2 = dot(enc_mt[rows, :], both[...])
        spread = spread2[:, 0:D] + spread2[:, D:]
        d_pre = (spread * slope(pre, sigmoid(pre))).astype(BF)
        total_enc[...] += dot(x_t, d_pre)

    @pl.when(final)
    def _():
        put_flat(d_enc, total_enc[...], 0, 4)
        copies("enc", d_enc, "start")
        copies("gain", gain_rows, "wait")
        copies("qkv", d_qkv, "wait")
        copies("enc", d_enc, "wait")


def encode_back(me, grid, w_enc, enc_mt, w_qkv, gains, h0, dh1, d_in, d_rims, from_lower, from_upper,
                layout):
    samples, nodes, _ = h0.shape
    halo, pixels = from_lower.shape[1], grid.shape[2]
    rim = by_sample(halo, 2 * D)
    return pl.pallas_call(
        functools.partial(encode_back_body, layout, samples),
        grid=(samples,),
        out_shape=[
            shape((layout.sizes[1], 128)),
            shape((layout.sizes[1] if layout.fast else 8, 128)),
        ],
        in_specs=[
            SCALAR,
            by_sample(C_IN, pixels),
            same(C_IN, D),
            same(*enc_mt.shape),
            same(*w_qkv.shape),
            same(8, D),
            by_sample(nodes, D),
            by_sample(nodes, D),
            by_sample(nodes, 3 * D),
            by_sample(2, halo, 2 * D),
            rim,
            rim,
        ],
        out_specs=[HBM, HBM],
        scratch_shapes=[
            pltpu.VMEM((nodes, 2 * D), BF),
            pltpu.VMEM((nodes, 3 * D), BF),
            pltpu.VMEM((nodes, D), BF),
            pltpu.VMEM((8, D), F32),
            pltpu.VMEM((3, D, D), F32),
            pltpu.VMEM((C_IN, D), F32),
            pltpu.VMEM((12 * D, 128), F32),
            pltpu.VMEM((4 * C_IN, 128), F32),
            pltpu.VMEM((8, 128), F32),
            pltpu.SemaphoreType.DMA((layout.plans[1][1],)),
        ],
        compiler_params=pltpu.CompilerParams(vmem_limit_bytes=58 << 20),
        cost_estimate=pl.CostEstimate(flops=16 << 30, bytes_accessed=24 << 20, transcendentals=0),
    )(me, grid, w_enc, enc_mt, w_qkv, gains, h0, dh1, d_in, d_rims, from_lower, from_upper)


def ring(axis, distance):
    count = lax.axis_size(axis)
    return [(i, (i + distance) % count) for i in range(count)]


def window_plan(shard, count):
    starts = [(LEAD * D + d * shard) // (16 * D) * 16 for d in range(count)]
    ends = [-(-(LEAD * D + (d + 1) * shard) // D) for d in range(count)]
    rows = max(-(-(e - s + 1) // 16) * 16 for s, e in zip(starts, ends))
    return starts, rows


def per_device(
    grid, targets, area, sigma_weight, level_weight, valid, enc_index, dec_index, neighbours,
    params, first_moment, second_moment, average,
):
    shard = params.shape[0]
    devices = lax.axis_size(AXES)
    me = lax.axis_index(AXES)
    fast = (lax.axis_size("patch"), lax.axis_size("dp")) == (8, 4)
    layout = Layout(shard, devices, fast)
    starts, win = layout.starts, layout.win
    begin = LEAD * D + me * shard
    shift = begin - begin // (16 * D) * (16 * D)
    place = me.astype(jnp.int32).reshape(1)

    lane_counts = jnp.sum(valid.reshape(-1, D), axis=0).astype(BF)
    room = 16 * D
    padded = jnp.pad(params.astype(BF), (room, win * D - shard))
    payload = lax.dynamic_slice(padded, (room - shift,), (win * D,))
    payload = lax.dynamic_update_slice(payload, lane_counts, ((win - 1) * D,)).reshape(win, D)
    weight = valid.astype(F32) * area[None, :] * sigma_weight[:, None]
    levels = jnp.pad(level_weight, (0, CP - C_OUT)).reshape(CP, 1)
    pixels = dec_index.shape[0]
    first_work = lambda: count_encoder(enc_index, pixels)

    def second_work(dec_index, neighbours, targets):
        return count_rest(dec_index, neighbours, targets), weight, levels

    def third_work(params):
        positions = me * shard + lax.iota(jnp.int32, shard)
        bounds = segment_bounds() + [(-1, -1)]
        lower = jnp.array([x for x, _ in bounds], jnp.int32)[:, None]
        upper = jnp.array([x for _, x in bounds], jnp.int32)[:, None]
        member = ((positions >= lower) & (positions < upper)).astype(F32)
        return member, jnp.sum(member * (params * params)[None, :], axis=1)

    targets = jnp.transpose(targets, (2, 0, 1))
    second_inputs, third_inputs = (dec_index, neighbours, targets), (params,)
    if fast:
        pieces, plan, first_done, second_done, third_done = gather_windows(
            payload, first_work, second_work, second_inputs, third_work, third_inputs
        )
        place_of = place_by_xor
    else:
        everything = lax.all_gather(payload, AXES, axis=0, tiled=False)
        pieces = [everything.reshape(devices * win, D)]
        plan = [(0, d * win, d, 0, win) for d in range(devices)]
        place_of = lambda here, d: d
        first_done, second_done = first_work(), second_work(*second_inputs)
        third_done = third_work(*third_inputs)
    member, old_sums = third_done
    enc_m, enc_mt = first_done
    (dec_mt, log_c, targets_t), weight, levels = second_done
    grid = jnp.swapaxes(grid, 1, 2)

    w_enc, w_qkv, gains = unpack(
        place, pieces, plan, ("enc", "qkv", "gains"), place_of, devices, win, starts
    )
    h0, qkv, leading, last = encode(grid, w_enc, enc_m, w_qkv, gains)
    before = lax.ppermute(last, "patch", ring("patch", 1))
    after = lax.ppermute(leading, "patch", ring("patch", -1))
    w_out, w_up, w_down, w_dec, counted = unpack(
        place, pieces, plan, ("out", "up", "down", "dec", "count"), place_of, devices, win, starts
    )
    attended = attend(qkv, before, after, log_c)
    dh1, own, keep, send = mlp(
        place, h0, attended, w_out, w_up, w_down, w_dec, gains, dec_mt, targets_t, weight, valid, levels,
        counted, layout,
    )
    back = attend_back(qkv, before, after, log_c, dh1, w_out)
    if fast:
        other = permute(send, 1)
        other, back = lax.optimization_barrier((other, back))
    d_qkv, d_rims, d_before, d_after = back
    from_upper = lax.ppermute(d_before, "patch", ring("patch", -1))
    from_lower = lax.ppermute(d_after, "patch", ring("patch", 1))
    if fast:
        send_a, send_b = first_send(keep, other, layout)
        got = permute(send_a, 2), permute(send_b, 4)
        send_a, send_b, from_upper, from_lower = lax.optimization_barrier(
            (send_a, send_b, from_upper, from_lower)
        )
    second = encode_back(
        place, grid, w_enc, enc_mt, w_qkv, gains, h0, dh1, d_qkv, d_rims, from_lower, from_upper,
        layout,
    )
    if fast:
        second, got = lax.optimization_barrier((second, got))
        keep_a, send_a, keep_b, send_b = second_send(keep, other, *got, layout)
        got = permute(send_a, 4), permute(send_b, 2)
        grad_window = sum_rest((keep_a, keep_b), got, second, layout, me)
    else:
        grad_window = sum_flat(keep, second[0], layout)
    grad = lax.dynamic_slice(grad_window.reshape(-1), (begin - begin // 1024 * 1024,), (shard,))

    new_first = BETA_ONE * first_moment + (1.0 - BETA_ONE) * grad
    new_second = BETA_TWO * second_moment + (1.0 - BETA_TWO) * grad * grad
    update = (
        new_first
        / (1.0 - BETA_ONE**STEP)
        / (jnp.sqrt(new_second / (1.0 - BETA_TWO**STEP)) + LAMB_EPS)
        + DECAY * params
    )
    sums = jnp.stack([old_sums, jnp.sum(member * (update * update)[None, :], axis=1)])
    own = own[:, 0:1]
    sums = jnp.where(jnp.arange(8)[None, :] == 7, own, sums)
    totals = sum_everywhere(sums, fast)
    norms = jnp.sqrt(totals[:, :7])
    step_ratio = jnp.sum(member[:7] * (norms[0] / norms[1])[:, None], axis=0)
    new_params = params - RATE * step_ratio * update
    new_average = EMA_KEEP * average + (1.0 - EMA_KEEP) * new_params
    return (
        totals[:, 7],
        norms,
        new_params,
        new_first,
        new_second,
        new_average,
    )


def solution(mesh):
    flat = P(AXES)
    in_specs = (
        P("dp", "patch", None),
        P("dp", "patch", None),
        P("patch"),
        P("dp"),
        P(),
        P("dp", "patch"),
        P("patch", None),
        P("patch", None),
        P("patch", None),
        flat,
        flat,
        flat,
        flat,
    )
    out_specs = (P(), P(), flat, flat, flat, flat)
    return jax.shard_map(
        per_device, mesh=mesh, in_specs=in_specs, out_specs=out_specs, check_vma=False
    )
```

```python
import functools
import math

import jax
import jax.numpy as jnp
from jax import lax
from jax.experimental import pallas as pl
from jax.experimental.pallas import tpu as pltpu
from jax.sharding import PartitionSpec as P

D = 512
HEADS = 4
HEAD_DIM = 128
FF = 2048
C_OUT = 84
C_IN = 264
STEP = 10
EPS_NORM = 1e-05
BETA_ONE = 0.9
BETA_TWO = 0.999
LAMB_EPS = 1e-06
DECAY = 0.01
RATE = 0.2
EMA_KEEP = 0.8
BF = jnp.bfloat16
F32 = jnp.float32
SCALE = HEAD_DIM ** (-0.5)
LOG2E = 1.4426950408889634
ABSENT = -1e30
CP = 96
AXES = ("patch", "dp")

LEAD = 8
ROW_ENC = LEAD
ROW_QKV = ROW_ENC + C_IN
ROW_OUT = ROW_QKV + 3 * D
ROW_UP = ROW_OUT + D
ROW_DOWN = ROW_UP + 4 * D
ROW_DEC = ROW_DOWN + FF
ROW_GAIN = ROW_DEC + C_OUT
ROW_END = ROW_GAIN + 3
ROWS_ALL = -(-ROW_END // 16) * 16


def matrix_shapes():
    return [(C_IN, D), (D, 3 * D), (D, D), (D, FF), (FF, D), (D, C_OUT), (3, D)]


def segment_bounds():
    bounds = []
    offset = 0
    for row_count, col_count in matrix_shapes():
        bounds.append((offset, offset + row_count * col_count))
        offset += row_count * col_count
    return bounds


NPARAM_USED = segment_bounds()[-1][1]


def dot(a, b):
    return lax.dot_general(a, b, (((1,), (0,)), ((), ())), preferred_element_type=F32)


def dot_nt(a, b):
    return lax.dot_general(a, b, (((1,), (1,)), ((), ())), preferred_element_type=F32)


def dot_tn(a, b):
    return lax.dot_general(a, b, (((0,), (0,)), ((), ())), preferred_element_type=F32)


def split(x):
    high = x.astype(BF)
    return high, (x - high.astype(F32)).astype(BF)


def sigmoid(x):
    return 0.5 * jnp.tanh(0.5 * x) + 0.5


def slope(x, s):
    return s * (1.0 + x * (1.0 - s))


def norm(x):
    c = x - jnp.mean(x, -1, keepdims=True)
    r = lax.rsqrt(jnp.mean(c * c, -1, keepdims=True) + EPS_NORM)
    return c * r, r


def norm_back(grad, gain, hat, r):
    g = grad * gain
    return r * (
        g
        - jnp.mean(g, -1, keepdims=True)
        - hat * jnp.mean(g * hat, -1, keepdims=True)
    )


def put_flat(ref, value, first, period):
    for lane in range(D // 128):
        ref[pl.ds(first + lane, value.shape[0], stride=period), :] = value[
            :, lane * 128 : lane * 128 + 128
        ]


def lane_pieces(begin, size, width):
    pieces = []
    while size > 0:
        row, lane = begin // width, begin % width
        count = min(width - lane, size)
        pieces.append((row, lane, count))
        begin, size = begin + count, size - count
    return pieces


PERIOD = 128 // math.gcd(128, C_OUT)
FLAT_PERIOD = PERIOD * C_OUT // 128
GROUPS = D // PERIOD


def narrow_to_flat(narrow, flat):
    for r in range(FLAT_PERIOD):
        parts = [
            narrow[pl.ds(row, GROUPS, stride=PERIOD), :][:, lane : lane + count]
            for row, lane, count in lane_pieces(128 * r, 128, C_OUT)
        ]
        flat[pl.ds(r, GROUPS, stride=FLAT_PERIOD), :] = jnp.concatenate(parts, axis=1)


def flat_to_narrow(flat, narrow):
    for b in range(PERIOD):
        parts = [
            flat[pl.ds(row, GROUPS, stride=FLAT_PERIOD), :][:, lane : lane + count]
            for row, lane, count in lane_pieces(C_OUT * b, C_OUT, 128)
        ]
        parts.append(jnp.zeros((GROUPS, 128 - C_OUT), F32))
        narrow[pl.ds(b, GROUPS, stride=PERIOD), :] = jnp.concatenate(parts, axis=1)


def kernel_call(body, out_shape, scratch=(), flops=0, nbytes=0):
    return pl.pallas_call(
        body,
        out_shape=out_shape,
        scratch_shapes=list(scratch),
        compiler_params=pltpu.CompilerParams(vmem_limit_bytes=58 << 20),
        cost_estimate=pl.CostEstimate(flops=flops, bytes_accessed=nbytes, transcendentals=0),
    )


def by_sample(*dims):
    return pl.BlockSpec((1,) + dims, lambda s: (s,) + (0,) * len(dims))


def same(*dims):
    return pl.BlockSpec(dims, lambda s: (0,) * len(dims))


HBM = pl.BlockSpec(memory_space=pl.ANY)
SCALAR = pl.BlockSpec(memory_space=pltpu.SMEM)


def shape(dims, dtype=F32):
    return jax.ShapeDtypeStruct(tuple(dims), dtype)


def count_rows(index_t, base, rows, cols):
    ids = lax.broadcasted_iota(jnp.int32, (rows, cols), 0) + base
    total = jnp.zeros((rows, cols), F32)
    for k in range(index_t.shape[0]):
        total = total + jnp.where(index_t[k : k + 1, :] == ids, 1.0, 0.0)
    return total


def count_encoder_body(enc, enc_t, enc_m, enc_mt):
    nodes, pixels = enc_m.shape

    @pl.loop(0, nodes // 32)
    def _(i):
        rows = pl.ds(pl.multiple_of(i * 32, 32), 32)
        index = enc[rows, :]
        ids = lax.broadcasted_iota(jnp.int32, (32, pixels), 1)
        total = jnp.zeros((32, pixels), F32)
        for k in range(index.shape[1]):
            total = total + jnp.where(index[:, k : k + 1] == ids, 1.0, 0.0)
        enc_m[rows, :] = total.astype(BF)

    @pl.loop(0, pixels // 64)
    def _(i):
        rows = pl.ds(pl.multiple_of(i * 64, 64), 64)
        enc_mt[rows, :] = count_rows(enc_t, i * 64, 64, nodes).astype(BF)


def count_rest_body(dec_t, nbr_t, targets, dec_mt, log_c, targets_t):
    nodes, pixels = dec_mt.shape

    @pl.loop(0, nodes // 32)
    def _(i):
        rows = pl.ds(pl.multiple_of(i * 32, 32), 32)
        dec_mt[rows, :] = count_rows(dec_t, i * 32, 32, pixels).astype(BF)

    @pl.loop(0, log_c.shape[0] // 64)
    def _(i):
        rows = pl.ds(pl.multiple_of(i * 64, 64), 64)
        total = count_rows(nbr_t, i * 64, 64, nodes)
        log_c[rows, :] = jnp.where(total > 0.0, jnp.log2(jnp.maximum(total, 1.0)), ABSENT)

    for s in range(targets.shape[1]):
        targets_t[s, 0:C_OUT, :] = targets[:, s, :]
        targets_t[s, C_OUT:, :] = jnp.zeros((CP - C_OUT, pixels), F32)


def count_encoder(enc_index, pixels):
    nodes = enc_index.shape[0]
    return kernel_call(
        count_encoder_body,
        [shape((nodes, pixels), BF), shape((pixels, nodes), BF)],
        nbytes=5 << 20,
        flops=1 << 29,
    )(enc_index, enc_index.T)


def count_rest(dec_index, neighbours, targets):
    nodes, pixels = neighbours.shape[0], dec_index.shape[0]
    ext = nodes + 2 * (nodes // 16)
    return kernel_call(
        count_rest_body,
        [shape((nodes, pixels), BF), shape((ext, nodes)), shape((targets.shape[1], CP, pixels))],
        nbytes=8 << 20,
        flops=1 << 29,
    )(dec_index.T, neighbours.T, targets)


def tile_sources(starts, rows):
    return [
        [(d, tile * 16 - s) for d, s in enumerate(starts) if s <= tile * 16 < s + rows]
        for tile in range(ROWS_ALL // 16)
    ]


def assemble(read, window_rows, sources, first_row, rows, put):
    tile, last = first_row // 16, (first_row + rows) // 16
    while tile < last:
        source = sources[tile]
        if len(source) == 1:
            count = 1
            while (
                tile + count < last
                and len(sources[tile + count]) == 1
                and sources[tile + count][0][0] == source[0][0]
                and count < 8
            ):
                count += 1
            d, off = source[0]
            value = read(d, off, 16 * count)
        else:
            count = 1
            value = None
            for d, off in source:
                part = read(d, off, 16).astype(F32)
                if off + 16 == window_rows:
                    part = jnp.where(
                        lax.broadcasted_iota(jnp.int32, part.shape, 0) < 15, part, 0.0
                    )
                value = part if value is None else value + part
            value = value.astype(BF)
        put(tile * 16 - first_row, value)
        tile += count


def wide(stage, ref, period):
    for lane in range(D // 128):
        for c in range(period):
            lanes = slice(c * D + lane * 128, c * D + lane * 128 + 128)
            ref[:, lanes] = stage[lane, pl.ds(c, ref.shape[0], stride=period), :].astype(BF)


def unpack_body(plan, parts, sources, place_of, owner_of, count, *refs):
    me, pieces, refs = refs[0], refs[1 : count + 1], refs[count + 1 :]
    outs, (windows, stage, flat, narrow, sems) = refs[: len(parts)], refs[len(parts) :]
    here = me[0]
    used = set()
    for part in parts:
        if part == "count":
            used = set(range(windows.shape[0]))
        else:
            row, rows = PARTS[part][:2]
            used |= {d for source in sources[row // 16 : (row + rows) // 16] for d, _ in source}
    ranges = [d for d in sorted(used) if d - 1 not in used], [d for d in sorted(used) if d + 1 not in used]
    for piece, at, slot, to, rows in plan:
        copy = pltpu.make_async_copy(
            pieces[piece].at[pl.ds(at, rows), :], windows.at[slot, pl.ds(to, rows), :], sems.at[slot]
        )
        owner = owner_of(here, slot)
        needed = functools.reduce(
            jnp.logical_or, [(owner >= lo) & (owner <= hi) for lo, hi in zip(*ranges)]
        )
        if len(used) == windows.shape[0]:
            copy.start()
        else:
            pl.when(needed)(copy.start)
    window_rows = windows.shape[1]
    waited = set()

    def wait_for(d):
        if d not in waited:
            waited.add(d)
            slot = place_of(here, d)
            pltpu.make_async_copy(windows.at[slot], windows.at[slot], sems.at[slot]).wait()

    def read(d, off, rows):
        wait_for(d)
        return windows[place_of(here, d), off : off + rows, :]

    for part, ref in zip(parts, outs):
        if part == "count":
            for d in range(windows.shape[0]):
                wait_for(d)
            total = jnp.sum(windows[:, window_rows - 16 :, :].astype(F32), axis=0)[15:16, :]
            ref[...] = jnp.sum(total, axis=1, keepdims=True) + jnp.zeros((8, 128), F32)
            continue
        first, rows, period, _ = PARTS[part]

        def direct(off, value):
            ref[off : off + value.shape[0], :] = value

        def staged(off, value):
            wide_value = value.astype(F32)
            for lane in range(D // 128):
                stage[lane, off : off + value.shape[0], :] = wide_value[
                    :, lane * 128 : lane * 128 + 128
                ]

        if part == "gains":
            assemble(read, window_rows, sources, first, rows, staged)
            row = ROW_GAIN - first
            for lane in range(D // 128):
                ref[:, lane * 128 : lane * 128 + 128] = stage[lane, row : row + 8, :]
        elif period == 1:
            assemble(read, window_rows, sources, first, rows, direct)
        else:
            assemble(read, window_rows, sources, first, rows, staged)
            if part == "enc":
                for lane in range(D // 128):
                    lanes = slice(lane * 128, lane * 128 + 128)
                    ref[:, lanes] = stage[lane, LEAD:ROW_QKV, :].astype(BF)
            elif part == "dec":
                row = ROW_DEC - first
                for lane in range(D // 128):
                    flat[pl.ds(lane, C_OUT, stride=4), :] = stage[lane, row : row + C_OUT, :]
                flat_to_narrow(flat, narrow)
                ref[...] = narrow[:, 0:C_OUT].astype(BF)
            else:
                wide(stage, ref, period)


PARTS = {
    "enc": (0, ROW_QKV, 0, (C_IN, D)),
    "qkv": (ROW_QKV, 3 * D, 3, (D, 3 * D)),
    "out": (ROW_OUT, D, 1, (D, D)),
    "up": (ROW_UP, 4 * D, 4, (D, FF)),
    "down": (ROW_DOWN, FF, 1, (FF, D)),
    "dec": (ROW_DEC // 16 * 16, -(-ROW_GAIN // 16) * 16 - ROW_DEC // 16 * 16, 0, (D, C_OUT)),
    "gains": (ROW_GAIN // 16 * 16, 16, 0, (8, D)),
}


def unpack(me, pieces, plan, parts, place_of, slots, rows, starts):
    sources = tile_sources(starts, rows)
    outs = [
        shape((8, 128)) if p == "count" else shape(PARTS[p][3], F32 if p == "gains" else BF)
        for p in parts
    ]
    return pl.pallas_call(
        functools.partial(unpack_body, plan, parts, sources, place_of, place_of, len(pieces)),
        out_shape=outs,
        in_specs=[pl.BlockSpec(memory_space=pltpu.SMEM)]
        + [pl.BlockSpec(memory_space=pl.ANY)] * len(pieces),
        scratch_shapes=[
            pltpu.VMEM((slots, rows, D), BF),
            pltpu.VMEM((D // 128, 4 * D, 128), F32),
            pltpu.VMEM((4 * C_OUT, 128), F32),
            pltpu.VMEM((D, 128), F32),
            pltpu.SemaphoreType.DMA((slots,)),
        ],
        compiler_params=pltpu.CompilerParams(vmem_limit_bytes=58 << 20),
        cost_estimate=pl.CostEstimate(
            flops=0, bytes_accessed=slots * rows * D * 4, transcendentals=0
        ),
    )(me, *pieces)


def permute(x, mask):
    count = lax.axis_size(AXES)
    return lax.ppermute(x, AXES, [(d, d ^ mask) for d in range(count)])


def place_by_xor(here, d):
    return jnp.bitwise_xor(here, d)


def gather_windows(window, first_work, second_work, second_inputs, third_work, third_inputs):
    rows = window.shape[0]
    half = rows // 2
    pieces, plan = [], []

    def add(piece, near, parts):
        for part, flip in ((piece, 0), (permute(piece, 1), 1)):
            for at, slot, to, size in parts:
                plan.append((len(pieces), at, slot ^ near ^ flip, to, size))
            pieces.append(part)

    planes = (8, 16, 24)
    others = [permute(window, m) for m in planes]
    by_x, by_y = permute(window, 2), permute(window, 4)
    first_done = first_work()
    others, by_x, by_y, first_done, second_inputs = lax.optimization_barrier(
        (jnp.concatenate(others), by_x, by_y, first_done, second_inputs)
    )
    others_x, others_y = permute(others, 2), permute(others, 4)
    second_done = second_work(*second_inputs)
    others_x, others_y, second_done, third_inputs = lax.optimization_barrier(
        (others_x, others_y, second_done, third_inputs)
    )

    def halves(near_part, far_part, first):
        far = [far_part[i * rows + first : i * rows + first + half] for i in range(3)]
        return jnp.concatenate([near_part[first : first + half]] + far)

    across_a = permute(halves(by_y, others_y, 0), 2)
    across_b = permute(halves(by_x, others_x, half), 4)
    across_a, across_b, third_done = lax.optimization_barrier(
        (across_a, across_b, third_work(*third_inputs))
    )
    whole = [(0, 0, 0, rows)]
    stacked = [(i * rows, slot, 0, rows) for i, slot in enumerate(planes)]
    add(window, 0, whole)
    add(by_x, 2, whole)
    add(by_y, 4, whole)
    add(others, 0, stacked)
    add(others_x, 2, stacked)
    add(others_y, 4, stacked)
    add(across_a, 6, [(i * half, slot, 0, half) for i, slot in enumerate((0,) + planes)])
    add(across_b, 6, [(i * half, slot, half, half) for i, slot in enumerate((0,) + planes)])
    return pieces, plan, first_done, second_done, third_done


def encode_body(grid, w_enc, enc_hbm, w_hbm, gains, h0, qkv, leading, last, high, low, enc_m, w_qkv, sems):
    pixels, nodes, halo = grid.shape[2], h0.shape[1], last.shape[1]
    first = pl.program_id(0) == 0
    loads = [
        pltpu.make_async_copy(enc_hbm, enc_m, sems.at[0]),
        pltpu.make_async_copy(w_hbm, w_qkv, sems.at[1]),
    ]
    for load in loads:
        pl.when(first)(load.start)
    for i in range(pixels // 512):
        rows = slice(i * 512, (i + 1) * 512)
        pre = dot_tn(grid[0, :, rows], w_enc[...])
        high[rows, :], low[rows, :] = split(pre * sigmoid(pre))
    for load in loads:
        pl.when(first)(load.wait)
    start = (dot(enc_m[...], high[...]) + dot(enc_m[...], low[...])) * 0.25
    h0[0] = start
    hat, _ = norm(start)
    n1 = (hat * gains[0:1, :]).astype(BF)
    qkv[0] = dot(n1, w_qkv[...]).astype(BF)
    leading[0] = qkv[0, 0:halo, D:]
    last[0] = qkv[0, nodes - halo :, D:]


def encode(grid, w_enc, enc_m, w_qkv, gains):
    samples, pixels = grid.shape[0], grid.shape[2]
    nodes = enc_m.shape[0]
    halo = nodes // 16
    return pl.pallas_call(
        encode_body,
        grid=(samples,),
        out_shape=[shape((samples, nodes, D)), shape((samples, nodes, 3 * D), BF)]
        + [shape((samples, halo, 2 * D), BF)] * 2,
        in_specs=[by_sample(C_IN, pixels), same(C_IN, D), HBM, HBM, same(8, D)],
        out_specs=[by_sample(nodes, D), by_sample(nodes, 3 * D)] + [by_sample(halo, 2 * D)] * 2,
        scratch_shapes=[
            pltpu.VMEM((pixels, D), BF),
            pltpu.VMEM((pixels, D), BF),
            pltpu.VMEM(enc_m.shape, BF),
            pltpu.VMEM(w_qkv.shape, BF),
            pltpu.SemaphoreType.DMA((2,)),
        ],
        compiler_params=pltpu.CompilerParams(vmem_limit_bytes=58 << 20),
        cost_estimate=pl.CostEstimate(flops=8 << 30, bytes_accessed=12 << 20, transcendentals=0),
    )(grid, w_enc, enc_m, w_qkv, gains)


def gather_pairs(qkv, before, after, pairs, s):
    halo, nodes = before.shape[1], qkv.shape[1]
    pairs[0:halo, :] = before[s]
    pairs[halo : halo + nodes, :] = qkv[s, :, D:]
    pairs[halo + nodes :, :] = after[s]


def attention_weights(keys, query, log_c):
    x = dot_nt(keys, query) * (SCALE * LOG2E) + log_c[...]
    e = jnp.exp2(x - jnp.max(x, 0, keepdims=True))
    return e * (1.0 / jnp.sum(e, 0, keepdims=True))


def attend_body(qkv, before, after, log_c, out, pairs):
    for s in range(qkv.shape[0]):
        gather_pairs(qkv, before, after, pairs, s)
        for h in range(HEADS):
            lanes = slice(h * HEAD_DIM, (h + 1) * HEAD_DIM)
            keys = pairs[:, lanes]
            values = pairs[:, D + h * HEAD_DIM : D + (h + 1) * HEAD_DIM]
            probs = attention_weights(keys, qkv[s, :, lanes], log_c)
            out_t = dot_tn(values, probs.astype(BF))
            out[s, :, lanes] = out_t.T.astype(BF)


def attend(qkv, before, after, log_c):
    samples, nodes = qkv.shape[:2]
    halo = before.shape[1]
    return pl.pallas_call(
        attend_body,
        grid=(samples,),
        out_shape=shape((samples, nodes, D), BF),
        in_specs=[
            by_sample(nodes, 3 * D),
            by_sample(halo, 2 * D),
            by_sample(halo, 2 * D),
            same(*log_c.shape),
        ],
        out_specs=by_sample(nodes, D),
        scratch_shapes=[pltpu.VMEM((log_c.shape[0], 2 * D), BF)],
        compiler_params=pltpu.CompilerParams(vmem_limit_bytes=58 << 20),
        cost_estimate=pl.CostEstimate(flops=2 << 30, bytes_accessed=8 << 20, transcendentals=0),
    )(qkv, before, after, log_c)


class Layout:
    def __init__(self, shard, devices, fast):
        self.devices = devices
        self.starts, self.win = window_plan(shard, devices)
        self.begins = [(LEAD * D + d * shard) // 1024 * 8 for d in range(devices)]
        self.ends = [-(-(LEAD * D + (d + 1) * shard) // 1024) * 8 for d in range(devices)]
        self.rows = -(-max(e - b for b, e in zip(self.begins, self.ends)) // 32) * 32
        self.small = 4 * (ROW_END - ROW_DEC) + 4
        first = (("out", ROW_OUT, 4 * D), ("up", ROW_UP, 16 * D)) + tuple(
            (f"down{c}", ROW_DOWN + c * D, 4 * D) for c in range(FF // D)
        ) + (("small", ROW_DEC, self.small),)
        second = (("enc", ROW_ENC, 4 * C_IN), ("qkv", ROW_QKV, 12 * D), ("gain", ROW_GAIN, 8))
        self.fast = fast
        if fast:
            self.apart = 4 * ROW_OUT - self.begins[8]
            extra = -(-(self.apart + 8) // 32) * 32
            self.sizes = (12 * self.rows, 4 * self.rows + extra)
        else:
            self.sizes = (sum(x[2] for x in first), sum(x[2] for x in second))
        self.plans = self.make(first, 1), self.make(second, 0)

    def make(self, arrays, plane):
        plans, k, at = {}, 0, 0
        for name, row, size in arrays:
            plans[name] = []
            if not self.fast:
                plans[name].append((k, None, at, 0, size))
                k, at = k + 1, at + size
                continue
            if name == "gain":
                plans[name].append((k, "both", 4 * self.rows + self.apart, 0, size))
                k += 2
                continue
            for d, (lower, upper) in enumerate(zip(self.begins, self.ends)):
                low, high = max(lower, 4 * row), min(upper, 4 * (row + size // 4))
                if low >= high:
                    continue
                if d == 8 and plane == 0:
                    to = 4 * self.rows + low - lower
                    plans[name].append((k, "both", to, low - 4 * row, high - low))
                    k += 2
                else:
                    place = (d // 8 - plane) * 4 * self.rows + low - lower
                    plans[name].append((k, d % 8, place, low - 4 * row, high - low))
                    k += 1
        return plans, k


def window_copies(here, rows_of_slot, blocks, source, keep, send, sems, action):
    for k, near, to, at, rows in blocks:

        def copy(target, first, sem):
            getattr(
                pltpu.make_async_copy(
                    source.at[pl.ds(at, rows), :], target.at[pl.ds(first, rows), :], sems.at[sem]
                ),
                action,
            )()

        if near is None:
            copy(keep, to, k)
        elif near == "both":
            copy(keep, to, k)
            copy(send, to, k + 1)
        else:
            slot = jnp.bitwise_and(jnp.bitwise_xor(here, near), 7)
            first = pl.multiple_of(lax.shift_right_logical(slot, 1) * rows_of_slot + to, 8)
            for target, side in ((keep, 0), (send, 1)):

                @pl.when(jnp.bitwise_and(slot, 1) == side)
                def _():
                    copy(target, first, k)


def sum_flat(first, second, layout):
    flat = jnp.concatenate(
        [
            jnp.zeros((4 * LEAD, 128), F32),
            second[: 4 * (ROW_OUT - LEAD)],
            first,
            jnp.zeros((max(0, layout.begins[-1] + layout.rows - 4 * ROW_DEC - layout.small), 128), F32),
        ]
    )
    gain = second[4 * (ROW_OUT - LEAD) :]
    flat = lax.dynamic_update_slice(
        flat, gain[0:4] + flat[4 * ROW_GAIN : 4 * ROW_GAIN + 4], (4 * ROW_GAIN, 0)
    )
    windows = jnp.concatenate([flat[b : b + layout.rows] for b in layout.begins])
    return lax.psum_scatter(windows, AXES, scatter_dimension=0, tiled=True)


def low(x):
    return x.astype(BF)


def packed(blocks, extra):
    return low(jnp.concatenate([blocks.reshape(-1, 128), extra]))


def add_packed(flat, blocks, extra):
    flat = flat.astype(F32)
    count = flat.shape[0] - extra.shape[0]
    return blocks + flat[:count].reshape(blocks.shape), extra + flat[count:]


def across_planes(x, allowed, k):
    pairs = [(d, d ^ (8 * k)) for d in range(32) if allowed((d ^ (8 * k)) // 8, d % 8)]
    return lax.ppermute(x, AXES, pairs)


def add_halves(layout, keep, other, got, sends):
    half = layout.rows // 2
    keep, other = keep.reshape(24, half, 128), other.reshape(24, half, 128)
    steps = []
    for out, (picks, source, _) in enumerate(sends):
        for i, pick in enumerate(picks):
            steps.append((out, i, pick, source))

    def body(*refs):
        keep_ref, other_ref = refs[:2]
        gots, outs = refs[2 : 2 + len(got)], refs[2 + len(got) : 2 + len(got) + len(sends)]
        slots, sems = refs[-2:]
        copies = []
        for k, (out, i, pick, source) in enumerate(steps):
            pair = [
                pltpu.make_async_copy(ref.at[pick], slots.at[2 * k + j], sems.at[2 * k + j])
                for j, ref in enumerate((keep_ref, other_ref))
            ]
            for copy in pair:
                copy.start()
            copies.append(pair)
        for k, (out, i, pick, source) in enumerate(steps):
            for copy in copies[k]:
                copy.wait()
            value = slots[2 * k] + slots[2 * k + 1]
            if source is not None:
                which, at = source[0], source[1][i]
                value = value + gots[which][at].astype(F32)
            outs[out][i] = value.astype(outs[out].dtype)

    hbm = pl.BlockSpec(memory_space=pl.ANY)
    vmem = pl.BlockSpec(memory_space=pltpu.VMEM)
    return pl.pallas_call(
        body,
        out_shape=[shape((len(p), half, 128), BF if sent else F32) for p, _, sent in sends],
        in_specs=[hbm, hbm] + [vmem] * len(got),
        out_specs=[vmem] * len(sends),
        scratch_shapes=[
            pltpu.VMEM((2 * len(steps), half, 128), F32),
            pltpu.SemaphoreType.DMA((2 * len(steps),)),
        ],
        compiler_params=pltpu.CompilerParams(vmem_limit_bytes=58 << 20),
        cost_estimate=pl.CostEstimate(
            flops=0, bytes_accessed=len(steps) * half * 1536, transcendentals=0
        ),
    )(keep, other, *got)


def first_send(keep, other, layout):
    to_x = [(p * 4 + y * 2 + 1) * 2 for p in range(3) for y in range(2)]
    to_y = [(p * 4 + 2 + x) * 2 + 1 for p in range(3) for x in range(2)]
    return add_halves(layout, keep, other, (), [(to_x, None, True), (to_y, None, True)])


def second_send(keep, other, got_a, got_b, layout):
    sends = []
    for which, (lower, stride) in enumerate(((0, 2), (1, 1))):
        for far in range(2):
            picks = [(p * 4 + far * stride) * 2 + lower for p in range(3)]
            sends.append((picks, (which, [p * 2 + far for p in range(3)]), far == 1))
    return add_halves(layout, keep, other, (got_a, got_b), sends)


def sum_rest(kept, got, second, layout, me):
    rows = layout.rows
    half = rows // 2
    near, mine = me % 8, me // 8

    late = second[0] + permute(second[1], 1)
    apart = late[4 * rows :]
    late = late[: 4 * rows].reshape(2, 2, rows, 128)
    cut = apart.shape[0] // 2
    send_a = packed(late[:, 1, :half], apart[:cut])
    send_b = packed(late[1, :, half:], apart[cut:])
    late_a, apart_a = add_packed(permute(send_a, 2), late[:, 0, :half], apart[:cut])
    late_b, apart_b = add_packed(permute(send_b, 4), late[0, :, half:], apart[cut:])
    got, _, _ = lax.optimization_barrier((got, send_a, send_b))
    kept_a, kept_b = kept[0] + got[0].astype(F32), kept[1] + got[1].astype(F32)

    def plane(k):
        at = jnp.maximum(jnp.bitwise_xor(mine, k) - 1, 0)
        return jnp.concatenate(
            [lax.dynamic_index_in_dim(x, at, 0, False) for x in (kept_a, kept_b)]
        )

    ups = [across_planes(low(plane(k)), lambda p, q: p > 0, k) for k in (1, 2, 3)]

    late_a, apart_a = add_packed(permute(packed(late_a[1], apart_a), 4), late_a[0], apart_a)
    late_b, apart_b = add_packed(permute(packed(late_b[1], apart_b), 2), late_b[0], apart_b)
    apart = jnp.concatenate([apart_a, apart_b])
    lead, gain = layout.apart, 4 * ROW_GAIN - layout.begins[31]
    one = jnp.concatenate([apart[:lead], jnp.zeros((rows - lead, 128), F32)])
    three = jnp.concatenate(
        [
            jnp.zeros((gain, 128), F32),
            apart[lead : lead + 4],
            jnp.zeros((rows - gain - 4, 128), F32),
        ]
    )
    parts = jnp.stack([jnp.concatenate([late_a, late_b]), one, one, three])

    def part(k):
        return lax.dynamic_index_in_dim(parts, jnp.bitwise_xor(mine, k), 0, False)

    lower = part(0)
    for k in (1, 2, 3):
        got = across_planes(
            low(part(k)), lambda p, q: p == 0 or (p, q) == (1, 0) or (p, q) == (3, 7), k
        )
        lower = lower + got.astype(F32)
    upper = plane(0)
    for up in ups:
        upper = upper + up.astype(F32)
    row = lax.broadcasted_iota(jnp.int32, (rows, 1), 0)
    take = (mine == 0) | ((me == 8) & (row < lead))
    add = (me == 31) & (row >= gain) & (row < gain + 4)
    return jnp.where(take, lower, jnp.where(add, upper + lower, upper))


def sum_everywhere(x, fast):
    if not fast:
        return lax.psum(x, AXES)
    for k in range(5):
        x = x + permute(x, 1 << k)
    return x


def mlp_body(
    layout,
    me, h0, attended, w_out, w_dec, gains, weight, valid, levels, counted, w_up_hbm, w_down_hbm, dec_mt_hbm, targets_hbm,
    dh1, loss, keep, send,
    loss_lanes, d_dec, d_gains, small, h1, n2, upper, act, h2, n3, pred, d_pred, dm, du, d_y, total_out, d_out, d_up, d_down, w_up, w_down, dec_mt, targets_t, sems, in_sems,
):
    samples, nodes, _ = h0.shape
    here = me[0]
    loads = [
        pltpu.make_async_copy(source, target, in_sems.at[k])
        for k, (source, target) in enumerate(
            ((w_up_hbm, w_up), (w_down_hbm, w_down), (dec_mt_hbm, dec_mt), (targets_hbm, targets_t))
        )
    ]
    for load in loads:
        load.start()
    pixels = dec_mt.shape[1]
    pred[...] = jnp.zeros(pred.shape, BF)
    scale = (2.0 / counted[0:1, 0:1]) * (1.0 / 3.0)
    tile = 512
    tiles = nodes // tile
    both = samples * nodes
    mid = h0[...].reshape(both, D) + dot(attended[...].reshape(both, D), w_out[...])
    h1[...] = mid
    hat, _ = norm(mid)
    n2[...] = (hat * gains[1:2, :]).astype(BF)
    loads[0].wait()
    loads[1].wait()
    for c in range(4):
        cols = slice(c * D, (c + 1) * D)
        u = dot(n2[...], w_up[:, cols])
        sig = sigmoid(u)
        upper[:, cols] = slope(u, sig)
        act[:, cols] = (u * sig).astype(BF)
    end = mid + dot(act[...], w_down[...])
    h2[...] = end
    hat, _ = norm(end)
    in_three = (hat * gains[2:3, :]).astype(BF)
    n3[...] = in_three
    y = dot(in_three, w_dec[...])
    for s in range(samples):
        high, low = split(y[s * nodes : (s + 1) * nodes].T)
        pred[s * CP : s * CP + C_OUT, :] = high
        pred[(samples + s) * CP : (samples + s) * CP + C_OUT, :] = low

    loads[2].wait()
    loads[3].wait()
    d_pred[...] = jnp.zeros(d_pred.shape, F32)
    loss_lanes[...] = jnp.zeros(loss_lanes.shape, F32)

    @pl.loop(0, pixels // 1024)
    def _(i):
        part = pl.ds(pl.multiple_of(i * 1024, 1024), 1024)
        counts = dec_mt[:, part]
        y_all = dot(pred[...], counts)
        highs, lows = [], []
        for s in range(samples):
            y = y_all[s * CP : (s + 1) * CP] + y_all[(samples + s) * CP : (samples + s + 1) * CP]
            misfit = y * (1.0 / 3.0) - targets_t[s, :, part]
            g = weight[s : s + 1, part] * levels[...] * misfit
            loss_lanes[...] += jnp.sum(g * misfit, axis=0, keepdims=True)
            high, low = split(g * scale)
            highs.append(high)
            lows.append(low)
        d_pred[...] += dot_nt(jnp.concatenate(highs + lows, axis=0), counts)

    loss[0:1, :] = jnp.sum(loss_lanes[...], axis=1, keepdims=True) + jnp.zeros((1, 128), F32)
    valid_rows = jnp.sum(valid[...].astype(F32), axis=0, keepdims=True)
    loss[1:2, :] = jnp.sum(valid_rows, axis=1, keepdims=True) + jnp.zeros((1, 128), F32)
    total_out[...] = jnp.zeros(total_out.shape, F32)
    d_dec[...] = jnp.zeros(d_dec.shape, F32)
    d_gains[...] = jnp.zeros(d_gains.shape, F32)
    for s in range(samples):
        total = d_pred[s * CP : (s + 1) * CP] + d_pred[(samples + s) * CP : (samples + s + 1) * CP]
        padded = jnp.concatenate([total, jnp.zeros((128 - CP, nodes), F32)], axis=0)
        d_y[...] = padded.T.astype(BF)

        @pl.loop(0, tiles, unroll=True)
        def _(i):
            rows = pl.ds(pl.multiple_of(i * tile, tile), tile)
            flat = pl.ds(pl.multiple_of(s * nodes + i * tile, tile), tile)
            d_part = d_y[rows, 0:C_OUT]
            d_dec[:, 0:C_OUT] += dot_tn(n3[flat, :], d_part)
            grad = dot_nt(d_part, w_dec[...])
            hat, r = norm(h2[flat, :])
            d_gains[2:3, :] += jnp.sum(grad * hat, axis=0, keepdims=True)
            d_end = norm_back(grad, gains[2:3, :], hat, r)
            d_low = d_end.astype(BF)
            dm[flat, :] = d_low
            d_in = jnp.zeros((tile, D), F32)
            for c in range(4):
                cols = slice(c * D, (c + 1) * D)
                d_act = dot_nt(d_low, w_down[cols, :])
                d_u = (d_act * upper[flat, cols]).astype(BF)
                du[flat, cols] = d_u
                d_in = d_in + dot_nt(d_u, w_up[:, cols])
            hat, r = norm(h1[flat, :])
            d_gains[1:2, :] += jnp.sum(d_in * hat, axis=0, keepdims=True)
            d_mid = d_end + norm_back(d_in, gains[1:2, :], hat, r)
            dh1[s, rows, :] = d_mid
            total_out[...] += dot_tn(attended[s, rows, :], d_mid.astype(BF))

    def copies(name, source, action):
        window_copies(
            here, layout.rows, layout.plans[0][0][name], source, keep, send, sems, action
        )

    narrow_to_flat(d_dec, small)
    small[4 * C_OUT :, :] = jnp.zeros((small.shape[0] - 4 * C_OUT, 128), F32)
    for k in (1, 2):
        for lane in range(D // 128):
            row = 4 * (C_OUT + k) + lane
            small[row : row + 1, :] = d_gains[k : k + 1, lane * 128 : lane * 128 + 128]
    copies("small", small, "start")
    put_flat(d_out, total_out[...], 0, 4)
    copies("out", d_out, "start")
    for c in range(FF // D):
        cols = slice(c * D, (c + 1) * D)
        put_flat(d_up, dot_tn(n2[...], du[:, cols]), 4 * c, 16)
    copies("up", d_up, "start")
    for c in range(FF // D):
        cols = slice(c * D, (c + 1) * D)
        put_flat(d_down, dot_tn(act[:, cols], dm[...]), 4 * c * D, 4)
        copies(f"down{c}", d_down.at[pl.ds(4 * c * D, 4 * D), :], "start")
    copies("small", small, "wait")
    copies("out", d_out, "wait")
    copies("up", d_up, "wait")
    for c in range(FF // D):
        copies(f"down{c}", d_down.at[pl.ds(4 * c * D, 4 * D), :], "wait")


def mlp(me, h0, attended, w_out, w_up, w_down, w_dec, gains, dec_mt, targets_t, weight, valid, levels, counted,
        layout):
    samples, nodes, _ = h0.shape
    rows = samples * nodes
    count = layout.plans[0][1]
    sent = layout.sizes[0] if layout.fast else 8
    vmem = pl.BlockSpec(memory_space=pltpu.VMEM)
    hbm = pl.BlockSpec(memory_space=pl.ANY)
    return pl.pallas_call(
        functools.partial(mlp_body, layout),
        out_shape=[
            shape((samples, nodes, D)),
            shape((2, 128)),
            shape((layout.sizes[0], 128)),
            shape((sent, 128)),
        ],
        in_specs=[pl.BlockSpec(memory_space=pltpu.SMEM)] + [vmem] * 9 + [hbm] * 4,
        out_specs=[vmem] * 2 + [hbm] * 2,
        scratch_shapes=[
            pltpu.VMEM((1, 1024), F32),
            pltpu.VMEM((D, 128), F32),
            pltpu.VMEM((8, D), F32),
            pltpu.VMEM((layout.small, 128), F32),
            pltpu.VMEM((rows, D), F32),
            pltpu.VMEM((rows, D), BF),
            pltpu.VMEM((rows, FF), F32),
            pltpu.VMEM((rows, FF), BF),
            pltpu.VMEM((rows, D), F32),
            pltpu.VMEM((rows, D), BF),
            pltpu.VMEM((2 * samples * CP, nodes), BF),
            pltpu.VMEM((2 * samples * CP, nodes), F32),
            pltpu.VMEM((rows, D), BF),
            pltpu.VMEM((rows, FF), BF),
            pltpu.VMEM((nodes, 128), BF),
            pltpu.VMEM((D, D), F32),
            pltpu.VMEM((4 * D, 128), F32),
            pltpu.VMEM((16 * D, 128), F32),
            pltpu.VMEM((4 * FF, 128), F32),
            pltpu.VMEM(w_up.shape, BF),
            pltpu.VMEM(w_down.shape, BF),
            pltpu.VMEM(dec_mt.shape, BF),
            pltpu.VMEM(targets_t.shape, F32),
            pltpu.SemaphoreType.DMA((count,)),
            pltpu.SemaphoreType.DMA((4,)),
        ],
        compiler_params=pltpu.CompilerParams(vmem_limit_bytes=60 << 20),
        cost_estimate=pl.CostEstimate(flops=16 << 30, bytes_accessed=24 << 20, transcendentals=0),
    )(me, h0, attended, w_out, w_dec, gains, weight, valid, levels, counted, w_up, w_down, dec_mt, targets_t)


def attend_back_body(
    qkv, before, after, log_c, dh1, w_out,
    d_qkv, d_rims, d_before, d_after,
    pairs, do_both,
):
    samples, nodes, _ = dh1.shape
    halo = before.shape[1]
    for s in range(samples):
        gather_pairs(qkv, before, after, pairs, s)
        for i in range(nodes // 256):
            rows = slice(i * 256, (i + 1) * 256)
            da = dh1[s, rows, :].astype(BF)
            high, low = split(dot_nt(da, w_out[...]))
            for h in range(HEADS):
                lanes = slice(h * HEAD_DIM, (h + 1) * HEAD_DIM)
                do_both[rows, 2 * h * HEAD_DIM : (2 * h + 1) * HEAD_DIM] = high[:, lanes]
                do_both[rows, (2 * h + 1) * HEAD_DIM : (2 * h + 2) * HEAD_DIM] = low[:, lanes]
        for h in range(HEADS):
            lanes = slice(h * HEAD_DIM, (h + 1) * HEAD_DIM)
            vlanes = slice(D + h * HEAD_DIM, D + (h + 1) * HEAD_DIM)
            query = qkv[s, :, lanes]
            keys = pairs[:, lanes]
            values = pairs[:, vlanes]
            do = do_both[:, 2 * h * HEAD_DIM : (2 * h + 2) * HEAD_DIM]
            probs = attention_weights(keys, query, log_c)
            d_probs = dot_nt(jnp.concatenate([values, values], axis=1), do)
            centre = jnp.sum(probs * d_probs, 0, keepdims=True)
            high, low = split(probs * (d_probs - centre))
            dv2 = dot(probs.astype(BF), do)
            dv = dv2[:, :HEAD_DIM] + dv2[:, HEAD_DIM:]
            dk = (dot(high, query) + dot(low, query)) * SCALE
            dq_t = (dot_tn(keys, high) + dot_tn(keys, low)) * SCALE
            d_qkv[s, :, lanes] = dq_t.T.astype(BF)
            klanes = slice(D + h * HEAD_DIM, D + (h + 1) * HEAD_DIM)
            wide_lanes = slice(2 * D + h * HEAD_DIM, 2 * D + (h + 1) * HEAD_DIM)
            d_qkv[s, :, klanes] = dk[halo : halo + nodes].astype(BF)
            d_qkv[s, :, wide_lanes] = dv[halo : halo + nodes].astype(BF)
            for rim, first in ((0, halo), (1, nodes)):
                d_rims[s, rim, :, lanes] = dk[first : first + halo]
                d_rims[s, rim, :, vlanes] = dv[first : first + halo]
            d_before[s, :, lanes] = dk[:halo].astype(BF)
            d_before[s, :, vlanes] = dv[:halo].astype(BF)
            d_after[s, :, lanes] = dk[halo + nodes :].astype(BF)
            d_after[s, :, vlanes] = dv[halo + nodes :].astype(BF)


def attend_back(qkv, before, after, log_c, dh1, w_out):
    samples, nodes, _ = dh1.shape
    halo = before.shape[1]
    rim = by_sample(halo, 2 * D)
    return pl.pallas_call(
        attend_back_body,
        grid=(samples,),
        out_shape=[
            shape((samples, nodes, 3 * D), BF),
            shape((samples, 2, halo, 2 * D)),
            shape((samples, halo, 2 * D), BF),
            shape((samples, halo, 2 * D), BF),
        ],
        in_specs=[by_sample(nodes, 3 * D), rim, rim, same(*log_c.shape), by_sample(nodes, D), same(D, D)],
        out_specs=[by_sample(nodes, 3 * D), by_sample(2, halo, 2 * D), rim, rim],
        scratch_shapes=[pltpu.VMEM((log_c.shape[0], 2 * D), BF), pltpu.VMEM((nodes, 2 * D), BF)],
        compiler_params=pltpu.CompilerParams(vmem_limit_bytes=58 << 20),
        cost_estimate=pl.CostEstimate(flops=8 << 30, bytes_accessed=20 << 20, transcendentals=0),
    )(qkv, before, after, log_c, dh1, w_out)


def encode_back_body(
    layout, samples,
    me, grid, w_enc, enc_mt, w_qkv, gains, h0, dh1, d_in, d_rims, from_lower, from_upper,
    keep, send,
    both, dqkv, n1, d_gain, total, total_enc, d_qkv, d_enc, gain_rows, sems,
):
    nodes, halo, pixels = h0.shape[1], from_lower.shape[1], grid.shape[2]
    step = pl.program_id(0)
    first, final = step == 0, step == samples - 1

    def copies(name, source, action):
        window_copies(
            me[0], layout.rows, layout.plans[1][0][name], source, keep, send, sems, action
        )

    @pl.when(first)
    def _():
        d_gain[...] = jnp.zeros(d_gain.shape, F32)
        total[...] = jnp.zeros(total.shape, F32)
        total_enc[...] = jnp.zeros(total_enc.shape, F32)

    dqkv[...] = d_in[0]
    low_rim = d_rims[0, 0] + from_lower[0].astype(F32)
    dqkv[0:halo, D:] = low_rim.astype(BF)
    high_rim = d_rims[0, 1] + from_upper[0].astype(F32)
    dqkv[nodes - halo :, D:] = high_rim.astype(BF)
    hat, r = norm(h0[0])
    n1[...] = (hat * gains[0:1, :]).astype(BF)
    grad = dot_nt(dqkv[...], w_qkv[...])
    d_gain[0:1, :] += jnp.sum(grad * hat, axis=0, keepdims=True)
    d_start = dh1[0] + norm_back(grad, gains[0:1, :], hat, r)
    high, low = split(d_start * 0.25)
    both[:, 0:D] = high
    both[:, D:] = low
    for c in range(3):
        total[c] += dot_tn(n1[...], dqkv[:, c * D : (c + 1) * D])

    @pl.when(final)
    def _():
        gain_rows[...] = jnp.zeros((8, 128), F32)
        for lane in range(D // 128):
            gain_rows[lane : lane + 1, :] = d_gain[0:1, lane * 128 : lane * 128 + 128]
        copies("gain", gain_rows, "start")
        for c in range(3):
            put_flat(d_qkv, total[c], 4 * c, 12)
        copies("qkv", d_qkv, "start")

    for i in range(pixels // 512):
        rows = slice(i * 512, (i + 1) * 512)
        x_t = grid[0, :, rows]
        pre = dot_tn(x_t, w_enc[...])
        spread2 = dot(enc_mt[rows, :], both[...])
        spread = spread2[:, 0:D] + spread2[:, D:]
        d_pre = (spread * slope(pre, sigmoid(pre))).astype(BF)
        total_enc[...] += dot(x_t, d_pre)

    @pl.when(final)
    def _():
        put_flat(d_enc, total_enc[...], 0, 4)
        copies("enc", d_enc, "start")
        copies("gain", gain_rows, "wait")
        copies("qkv", d_qkv, "wait")
        copies("enc", d_enc, "wait")


def encode_back(me, grid, w_enc, enc_mt, w_qkv, gains, h0, dh1, d_in, d_rims, from_lower, from_upper,
                layout):
    samples, nodes, _ = h0.shape
    halo, pixels = from_lower.shape[1], grid.shape[2]
    rim = by_sample(halo, 2 * D)
    return pl.pallas_call(
        functools.partial(encode_back_body, layout, samples),
        grid=(samples,),
        out_shape=[
            shape((layout.sizes[1], 128)),
            shape((layout.sizes[1] if layout.fast else 8, 128)),
        ],
        in_specs=[
            SCALAR,
            by_sample(C_IN, pixels),
            same(C_IN, D),
            same(*enc_mt.shape),
            same(*w_qkv.shape),
            same(8, D),
            by_sample(nodes, D),
            by_sample(nodes, D),
            by_sample(nodes, 3 * D),
            by_sample(2, halo, 2 * D),
            rim,
            rim,
        ],
        out_specs=[HBM, HBM],
        scratch_shapes=[
            pltpu.VMEM((nodes, 2 * D), BF),
            pltpu.VMEM((nodes, 3 * D), BF),
            pltpu.VMEM((nodes, D), BF),
            pltpu.VMEM((8, D), F32),
            pltpu.VMEM((3, D, D), F32),
            pltpu.VMEM((C_IN, D), F32),
            pltpu.VMEM((12 * D, 128), F32),
            pltpu.VMEM((4 * C_IN, 128), F32),
            pltpu.VMEM((8, 128), F32),
            pltpu.SemaphoreType.DMA((layout.plans[1][1],)),
        ],
        compiler_params=pltpu.CompilerParams(vmem_limit_bytes=58 << 20),
        cost_estimate=pl.CostEstimate(flops=16 << 30, bytes_accessed=24 << 20, transcendentals=0),
    )(me, grid, w_enc, enc_mt, w_qkv, gains, h0, dh1, d_in, d_rims, from_lower, from_upper)


def ring(axis, distance):
    count = lax.axis_size(axis)
    return [(i, (i + distance) % count) for i in range(count)]


def window_plan(shard, count):
    starts = [(LEAD * D + d * shard) // (16 * D) * 16 for d in range(count)]
    ends = [-(-(LEAD * D + (d + 1) * shard) // D) for d in range(count)]
    rows = max(-(-(e - s + 1) // 16) * 16 for s, e in zip(starts, ends))
    return starts, rows


def per_device(
    grid, targets, area, sigma_weight, level_weight, valid, enc_index, dec_index, neighbours,
    params, first_moment, second_moment, average,
):
    shard = params.shape[0]
    devices = lax.axis_size(AXES)
    me = lax.axis_index(AXES)
    fast = (lax.axis_size("patch"), lax.axis_size("dp")) == (8, 4)
    layout = Layout(shard, devices, fast)
    starts, win = layout.starts, layout.win
    begin = LEAD * D + me * shard
    shift = begin - begin // (16 * D) * (16 * D)
    place = me.astype(jnp.int32).reshape(1)

    lane_counts = jnp.sum(valid.reshape(-1, D), axis=0).astype(BF)
    room = 16 * D
    padded = jnp.pad(params.astype(BF), (room, win * D - shard))
    payload = lax.dynamic_slice(padded, (room - shift,), (win * D,))
    payload = lax.dynamic_update_slice(payload, lane_counts, ((win - 1) * D,)).reshape(win, D)
    weight = valid.astype(F32) * area[None, :] * sigma_weight[:, None]
    levels = jnp.pad(level_weight, (0, CP - C_OUT)).reshape(CP, 1)
    pixels = dec_index.shape[0]
    first_work = lambda: count_encoder(enc_index, pixels)

    def second_work(dec_index, neighbours, targets):
        return count_rest(dec_index, neighbours, targets), weight, levels

    def third_work(params):
        positions = me * shard + lax.iota(jnp.int32, shard)
        bounds = segment_bounds() + [(-1, -1)]
        lower = jnp.array([x for x, _ in bounds], jnp.int32)[:, None]
        upper = jnp.array([x for _, x in bounds], jnp.int32)[:, None]
        member = ((positions >= lower) & (positions < upper)).astype(F32)
        return member, jnp.sum(member * (params * params)[None, :], axis=1)

    targets = jnp.transpose(targets, (2, 0, 1))
    second_inputs, third_inputs = (dec_index, neighbours, targets), (params,)
    if fast:
        pieces, plan, first_done, second_done, third_done = gather_windows(
            payload, first_work, second_work, second_inputs, third_work, third_inputs
        )
        place_of = place_by_xor
    else:
        everything = lax.all_gather(payload, AXES, axis=0, tiled=False)
        pieces = [everything.reshape(devices * win, D)]
        plan = [(0, d * win, d, 0, win) for d in range(devices)]
        place_of = lambda here, d: d
        first_done, second_done = first_work(), second_work(*second_inputs)
        third_done = third_work(*third_inputs)
    member, old_sums = third_done
    enc_m, enc_mt = first_done
    (dec_mt, log_c, targets_t), weight, levels = second_done
    grid = jnp.swapaxes(grid, 1, 2)

    w_enc, w_qkv, gains = unpack(
        place, pieces, plan, ("enc", "qkv", "gains"), place_of, devices, win, starts
    )
    h0, qkv, leading, last = encode(grid, w_enc, enc_m, w_qkv, gains)
    before = lax.ppermute(last, "patch", ring("patch", 1))
    after = lax.ppermute(leading, "patch", ring("patch", -1))
    w_out, w_up, w_down, w_dec, counted = unpack(
        place, pieces, plan, ("out", "up", "down", "dec", "count"), place_of, devices, win, starts
    )
    attended = attend(qkv, before, after, log_c)
    dh1, own, keep, send = mlp(
        place, h0, attended, w_out, w_up, w_down, w_dec, gains, dec_mt, targets_t, weight, valid, levels,
        counted, layout,
    )
    back = attend_back(qkv, before, after, log_c, dh1, w_out)
    if fast:
        other = permute(send, 1)
        other, back = lax.optimization_barrier((other, back))
    d_qkv, d_rims, d_before, d_after = back
    from_upper = lax.ppermute(d_before, "patch", ring("patch", -1))
    from_lower = lax.ppermute(d_after, "patch", ring("patch", 1))
    if fast:
        send_a, send_b = first_send(keep, other, layout)
        got = permute(send_a, 2), permute(send_b, 4)
        send_a, send_b, from_upper, from_lower = lax.optimization_barrier(
            (send_a, send_b, from_upper, from_lower)
        )
    second = encode_back(
        place, grid, w_enc, enc_mt, w_qkv, gains, h0, dh1, d_qkv, d_rims, from_lower, from_upper,
        layout,
    )
    if fast:
        second, got = lax.optimization_barrier((second, got))
        keep_a, send_a, keep_b, send_b = second_send(keep, other, *got, layout)
        got = permute(send_a, 4), permute(send_b, 2)
        grad_window = sum_rest((keep_a, keep_b), got, second, layout, me)
    else:
        grad_window = sum_flat(keep, second[0], layout)
    grad = lax.dynamic_slice(grad_window.reshape(-1), (begin - begin // 1024 * 1024,), (shard,))

    new_first = BETA_ONE * first_moment + (1.0 - BETA_ONE) * grad
    new_second = BETA_TWO * second_moment + (1.0 - BETA_TWO) * grad * grad
    update = (
        new_first
        / (1.0 - BETA_ONE**STEP)
        / (jnp.sqrt(new_second / (1.0 - BETA_TWO**STEP)) + LAMB_EPS)
        + DECAY * params
    )
    sums = jnp.stack([old_sums, jnp.sum(member * (update * update)[None, :], axis=1)])
    own = own[:, 0:1]
    sums = jnp.where(jnp.arange(8)[None, :] == 7, own, sums)
    totals = sum_everywhere(sums, fast)
    norms = jnp.sqrt(totals[:, :7])
    step_ratio = jnp.sum(member[:7] * (norms[0] / norms[1])[:, None], axis=0)
    new_params = params - RATE * step_ratio * update
    new_average = EMA_KEEP * average + (1.0 - EMA_KEEP) * new_params
    return (
        totals[:, 7],
        norms,
        new_params,
        new_first,
        new_second,
        new_average,
    )


def solution(mesh):
    flat = P(AXES)
    in_specs = (
        P("dp", "patch", None),
        P("dp", "patch", None),
        P("patch"),
        P("dp"),
        P(),
        P("dp", "patch"),
        P("patch", None),
        P("patch", None),
        P("patch", None),
        flat,
        flat,
        flat,
        flat,
    )
    out_specs = (P(), P(), flat, flat, flat, flat)
    return jax.shard_map(
        per_device, mesh=mesh, in_specs=in_specs, out_specs=out_specs, check_vma=False
    )
```
